32 devices in a mesh: grp: 2 (over x), wave: 16 (over z, y, core).
Axes of the slice: x: 2, y: 2, z: 4, core: 2. Of those that a mesh axis runs over, the one named last changes fastest.
Arguments:
- north_rows: bfloat16 [2560, 128, 274], P(('grp', 'wave')), parts along dimension 0, may hold values from -6 to 6
- south_rows: bfloat16 [2560, 128, 274], P(('grp', 'wave')), parts along dimension 0, may hold values from -6 to 6
- lon_counts: int32 [1280], replicated, may hold values from 20 to 5148, as said below
- slot_wave: int32 [128], replicated, may hold values from 0 to 2559, as said below
- legendre: bfloat16 [128, 1280, 1280], P('wave'), may hold values from -0.15625 to 0.15625
- mode_rates: float32 [137], replicated, may hold values from 0.05 to 20
- to_modes: bfloat16 [137, 137], replicated, may hold values from -0.5 to 0.5
- from_modes: bfloat16 [137, 137], replicated, may hold values from -0.5 to 0.5
Outputs:
- spec_state: bfloat16 [256, 1280, 274], P(('grp', 'wave')), parts along dimension 0
- new_rows: bfloat16 [2560, 128, 274], P(('grp', 'wave')), parts along dimension 0
The draws below stay inside these ranges and needn't reach their ends.
There are 2 independent parts, one for each index of `grp`. The reference program is written for one: setup_inputs(seed, part) draws one part's arguments, and reference() takes and returns one part's arrays. A program takes and returns all parts, laid end to end along the dimension named above; an argument that names none is the same for every part. Nothing has to cross between parts.
Inputs may be any that keep to these rules, and one draw needn't show every extreme that they name: Wavenumber m is present in latitude row j only if 2 m is below lon_counts[j]. `slot_wave`: distinct zonal wavenumbers.
All inputs are finite; a program needn't handle non-finite values.
Results may differ from the reference program's by a relative error of at most 0.0065.
Values may be sent and summed in bfloat16 or wider, within the bound.
No kernel may reach another device: no remote copies, remote signals or barrier semaphores. Data moves between devices by JAX's collectives and lax.ppermute only.
A program may use at most 192 MiB of HBM per device.

```python
import math
import jax
import jax.numpy as jnp
from jax import lax

NLAT = 1280
NMAX = 2559
LEV = 137
MW = 128
NS = 1280


def draw_lon_counts(key, part):
    jitter = jax.random.randint(jax.random.fold_in(key, 11), (NLAT,), 0, 4)
    jitter = jitter.at[0].set(0).at[NLAT - 1].set(3)
    row_number = jnp.arange(NLAT, dtype=jnp.int32) + 1
    return (16 + 2 * row_number * (NMAX + 1) // NLAT + 4 * jitter).astype(jnp.int32)


def draw_slot_wave(key, part):
    inner = jax.random.permutation(jax.random.fold_in(key, 21), NMAX - 1)[:MW - 2] + 1
    values = jnp.concatenate([jnp.array([0, NMAX], dtype=jnp.int32), inner.astype(jnp.int32)])
    placing = jax.random.permutation(jax.random.fold_in(key, 22), MW)
    return values[placing].astype(jnp.int32)


def shard_levels(key, dims, split, least, top_value):
    level = 1.0
    for position, shards_of in split:
        draws = jax.random.uniform(jax.random.fold_in(jax.random.fold_in(key, 6), position), (shards_of,), jnp.float32, least / len(split), top_value / len(split))
        level = level * jnp.repeat(jnp.exp(draws), dims[position] // shards_of).reshape((-1,) + (1,) * (len(dims) - 1 - position))
    return level


def normal_values(own_key, shape, spread, most, pieces=(), kind=jnp.bfloat16):
    entries = spread * jax.random.normal(own_key, shape, jnp.float32)
    if pieces:
        entries = entries * shard_levels(own_key, shape, pieces, -0.22, 0.18)
    return jnp.clip(entries, -most, most).astype(kind)


def setup_inputs(seed: int = 0, part: int = 0) -> dict:
    arg_keys = jax.random.split(jax.random.key(seed), 9)
    part_keys = jax.random.split(jax.random.fold_in(arg_keys[8], part), 9)
    return {
        "north_rows": normal_values(part_keys[0], (NLAT, MW, 2 * LEV), 1.0, 6.0, ((0, 16),)),
        "south_rows": normal_values(part_keys[1], (NLAT, MW, 2 * LEV), 1.0, 6.0, ((0, 16),)),
        "lon_counts": draw_lon_counts(jax.random.fold_in(arg_keys[8], 71), part),
        "slot_wave": draw_slot_wave(jax.random.fold_in(arg_keys[8], 71), part),
        "legendre": normal_values(arg_keys[4], (MW, NS, NLAT), NLAT ** -0.5, 0.15625, ((0, 16),)),
        "mode_rates": jnp.clip(jnp.exp(jax.random.uniform(arg_keys[5], (LEV,), jnp.float32, math.log(0.05), math.log(20.0))), 0.05, 20.0),
        "to_modes": normal_values(arg_keys[6], (LEV, LEV), LEV ** -0.5, 0.5),
        "from_modes": normal_values(arg_keys[7], (LEV, LEV), LEV ** -0.5, 0.5),
    }


def vertical_step(direct, own_waves, mode_rates, to_modes, from_modes):
    slot_count, row_total, channels = direct.shape
    levels = to_modes.shape[0]
    modal_part = jnp.dot(direct.reshape(-1, levels), to_modes, preferred_element_type=jnp.float32)
    modal_part = modal_part.reshape(slot_count, row_total, 2, levels)
    degree = own_waves[:, None] + 2 * jnp.arange(row_total, dtype=jnp.int32)[None, :]
    degree_f = degree.astype(jnp.float32)
    scaled_degree = degree_f * (degree_f + 1.0) / float(NMAX * (NMAX + 1))
    divisor = 1.0 + mode_rates[None, None, None, :] * scaled_degree[:, :, None, None]
    scaled = (modal_part / divisor).astype(jnp.bfloat16).reshape(-1, levels)
    result = jnp.dot(scaled, from_modes, preferred_element_type=jnp.float32)
    result = result.reshape(slot_count, row_total, channels)
    return jnp.where((degree <= NMAX)[:, :, None], result, 0.0).astype(jnp.bfloat16)


def reference(north_rows, south_rows, lon_counts, slot_wave, legendre, mode_rates, to_modes, from_modes):
    live_mask = 2 * slot_wave[None, :] < lon_counts[:, None]
    summed = north_rows.astype(jnp.float32) + south_rows.astype(jnp.float32)
    symmetric = jnp.where(live_mask[:, :, None], summed, 0.0).astype(jnp.bfloat16)

    def one_slot(inputs):
        wavenumber, matrix, slot_rows, live_column = inputs
        direct = jnp.dot(matrix, slot_rows, preferred_element_type=jnp.float32).astype(jnp.bfloat16)
        state = vertical_step(direct[None], wavenumber[None], mode_rates, to_modes, from_modes)[0]
        returned = lax.dot_general(matrix, state, (((0,), (0,)), ((), ())), preferred_element_type=jnp.float32)
        returned = jnp.where(live_column[:, None], returned, 0.0).astype(jnp.bfloat16)
        return state, returned

    spec_state, returned = lax.map(one_slot, (slot_wave, legendre, jnp.moveaxis(symmetric, 1, 0), live_mask.T))
    return spec_state, jnp.moveaxis(returned, 0, 1)
```

```python
import functools

import jax
import jax.numpy as jnp
from jax import lax
from jax.experimental import pallas as pl
from jax.experimental.pallas import tpu as pltpu
from jax.sharding import PartitionSpec as P

NMAX = 2559
VMEM_BYTES = 56 * 1024 * 1024
GROUP = 16


def pack_body(north_ref, south_ref, counts_ref, twice_ref, out_ref):
    _, group, lat_dev, slots = north_ref.shape
    live = twice_ref[...] < counts_ref[...]
    summed = north_ref[0].astype(jnp.float32) + south_ref[0].astype(jnp.float32)
    summed = jnp.where(live[None], summed, 0.0).reshape(group * lat_dev, slots)
    out_ref[...] = summed.astype(jnp.bfloat16).T


def pack(part, north, south, counts, twice):
    _, levels, lat_dev, slots = north.shape
    rows = pl.BlockSpec((1, GROUP, lat_dev, slots), lambda i: (part, i, 0, 0))
    return pl.pallas_call(
        pack_body,
        grid=(pl.cdiv(levels, GROUP),),
        in_specs=[
            rows,
            rows,
            pl.BlockSpec((lat_dev, 1), lambda i: (0, 0)),
            pl.BlockSpec((1, slots), lambda i: (0, 0)),
        ],
        out_specs=pl.BlockSpec((slots, GROUP * lat_dev), lambda i: (0, i)),
        out_shape=jax.ShapeDtypeStruct((slots, levels * lat_dev), jnp.bfloat16),
        compiler_params=pltpu.CompilerParams(vmem_limit_bytes=VMEM_BYTES),
        cost_estimate=pl.CostEstimate(
            flops=2 * levels * lat_dev * slots,
            bytes_accessed=6 * levels * lat_dev * slots,
            transcendentals=0,
        ),
    )(north, south, counts, twice)


def unpack_body(in_ref, *refs):
    out_ref = refs[-1]
    _, group, lat_dev, slots = out_ref.shape
    rows = in_ref[...].T.astype(jnp.float32).reshape(group, lat_dev, slots)
    out_ref[0] = rows.astype(jnp.bfloat16)


def unpack(part, parts, levels, lat_dev, received, earlier):
    slots = received.shape[0]
    in_specs = [pl.BlockSpec((slots, GROUP * lat_dev), lambda i: (0, i))]
    operands = [received]
    aliases = {}
    if earlier is not None:
        in_specs.append(pl.BlockSpec(memory_space=pl.ANY))
        operands.append(earlier)
        aliases = {1: 0}
    return pl.pallas_call(
        unpack_body,
        grid=(pl.cdiv(levels, GROUP),),
        in_specs=in_specs,
        out_specs=pl.BlockSpec((1, GROUP, lat_dev, slots), lambda i: (part, i, 0, 0)),
        out_shape=jax.ShapeDtypeStruct((parts, levels, lat_dev, slots), jnp.bfloat16),
        input_output_aliases=aliases,
        compiler_params=pltpu.CompilerParams(vmem_limit_bytes=VMEM_BYTES),
        cost_estimate=pl.CostEstimate(
            flops=levels * lat_dev * slots,
            bytes_accessed=4 * levels * lat_dev * slots,
            transcendentals=0,
        ),
    )(*operands)


def step_body(waves_ref, sym_ref, legendre_ref, counts_ref, rates_ref, to_ref, from_ref, spec_ref, new_ref):
    wave = waves_ref[pl.program_id(0)]
    row_total = legendre_ref.shape[1]
    matrix = legendre_ref[0]
    direct = lax.dot_general(
        sym_ref[0], matrix, (((1,), (1,)), ((), ())), preferred_element_type=jnp.float32
    ).astype(jnp.bfloat16)
    modal = jnp.dot(to_ref[...], direct, preferred_element_type=jnp.float32)
    degree = wave + 2 * lax.broadcasted_iota(jnp.int32, (1, row_total), 1)
    degree_f = degree.astype(jnp.float32)
    scaled_degree = degree_f * (degree_f + 1.0) / float(NMAX * (NMAX + 1))
    scaled = (modal / (1.0 + rates_ref[...] * scaled_degree)).astype(jnp.bfloat16)
    state = jnp.dot(from_ref[...], scaled, preferred_element_type=jnp.float32)
    state = jnp.where(degree <= NMAX, state, 0.0).astype(jnp.bfloat16)
    spec_ref[0] = state
    rows = jnp.dot(state, matrix, preferred_element_type=jnp.float32)
    new_ref[0] = jnp.where(2 * wave < counts_ref[...], rows, 0.0).astype(jnp.bfloat16)


def spectral_step(symmetric, legendre, own_waves, counts, rates, to_modes_t, from_modes_t):
    slot_dev, levels, lat_total = symmetric.shape
    row_total = legendre.shape[1]
    whole = lambda shape: pl.BlockSpec(shape, lambda s, waves: (0,) * len(shape))
    spec_shape = jax.ShapeDtypeStruct((slot_dev, levels, row_total), jnp.bfloat16)
    new_shape = jax.ShapeDtypeStruct((slot_dev, levels, lat_total), jnp.bfloat16)
    per_slot = lambda a, b: pl.BlockSpec((1, a, b), lambda s, waves: (s, 0, 0))
    return pl.pallas_call(
        step_body,
        grid_spec=pltpu.PrefetchScalarGridSpec(
            num_scalar_prefetch=1,
            grid=(slot_dev,),
            in_specs=[
                per_slot(levels, lat_total),
                per_slot(row_total, lat_total),
                whole((1, lat_total)),
                whole((levels, 1)),
                whole((levels, levels)),
                whole((levels, levels)),
            ],
            out_specs=[per_slot(levels, row_total), per_slot(levels, lat_total)],
        ),
        out_shape=[spec_shape, new_shape],
        compiler_params=pltpu.CompilerParams(vmem_limit_bytes=VMEM_BYTES),
        cost_estimate=pl.CostEstimate(
            flops=4 * slot_dev * row_total * lat_total * levels,
            bytes_accessed=2 * slot_dev * lat_total * (row_total + 3 * levels),
            transcendentals=0,
        ),
    )(own_waves, symmetric, legendre, counts, rates, to_modes_t, from_modes_t)


def per_device(
    north_rows, south_rows, lon_counts, slot_wave, legendre, mode_rates, to_modes, from_modes
):
    lat_dev, slots, channels = north_rows.shape
    slot_dev, row_total, lat_total = legendre.shape
    levels = to_modes.shape[0]
    parts = channels // levels
    devices = slots // slot_dev
    my_index = lax.axis_index("wave")
    own_waves = lax.dynamic_slice_in_dim(slot_wave, my_index * slot_dev, slot_dev)
    local_counts = lax.dynamic_slice_in_dim(lon_counts, my_index * lat_dev, lat_dev)[:, None]
    twice = 2 * slot_wave[None, :]
    north = jnp.transpose(north_rows, (2, 0, 1)).reshape(parts, levels, lat_dev, slots)
    south = jnp.transpose(south_rows, (2, 0, 1)).reshape(parts, levels, lat_dev, slots)
    exchange = functools.partial(
        lax.all_to_all, axis_name="wave", split_axis=0, concat_axis=0, tiled=True
    )
    columns = [exchange(pack(part, north, south, local_counts, twice)) for part in range(parts)]
    states = []
    returned = []
    for part in range(parts):
        symmetric = columns[part].reshape(devices, slot_dev, levels, lat_dev)
        symmetric = jnp.transpose(symmetric, (1, 2, 0, 3)).reshape(slot_dev, levels, lat_total)
        state, rows = spectral_step(
            symmetric, legendre, own_waves, lon_counts[None, :], mode_rates[:, None],
            to_modes.T, from_modes.T,
        )
        states.append(state)
        rows = rows.reshape(slot_dev, levels, devices, lat_dev)
        rows = jnp.transpose(rows, (2, 0, 1, 3)).reshape(slots, levels * lat_dev)
        returned.append(exchange(rows))
    new_rows = None
    for part in range(parts):
        new_rows = unpack(part, parts, levels, lat_dev, returned[part], new_rows)
    new_rows = jnp.transpose(new_rows.reshape(channels, lat_dev, slots), (1, 2, 0))
    spec_state = jnp.transpose(jnp.concatenate(states, axis=1), (0, 2, 1))
    return (spec_state, new_rows)


def solution(mesh):
    in_specs = (
        P(("grp", "wave"), None, None),
        P(("grp", "wave"), None, None),
        P(),
        P(),
        P("wave", None, None),
        P(),
        P(),
        P(),
    )
    out_specs = (P(("grp", "wave"), None, None), P(("grp", "wave"), None, None))
    return jax.shard_map(
        per_device, mesh=mesh, in_specs=in_specs, out_specs=out_specs, check_vma=False
    )
```

```python
import functools
import math

import jax
import jax.numpy as jnp
from jax import lax
from jax.experimental import pallas as pl
from jax.experimental.pallas import tpu as pltpu
from jax.sharding import PartitionSpec as P

NMAX = 2559
VMEM_BYTES = 56 * 1024 * 1024
GROUP = 16
LANES = 128


def pack_body(north_ref, south_ref, counts_ref, twice_ref, out_ref):
    _, group, lat_dev, slots = north_ref.shape
    live = twice_ref[...] < counts_ref[...]
    summed = north_ref[0].astype(jnp.float32) + south_ref[0].astype(jnp.float32)
    summed = jnp.where(live[None], summed, 0.0).reshape(group * lat_dev, slots)
    out_ref[...] = summed.astype(jnp.bfloat16).T


def pack(part, north, south, counts, twice):
    _, levels, lat_dev, slots = north.shape
    rows = pl.BlockSpec((1, GROUP, lat_dev, slots), lambda i: (part, i, 0, 0))
    return pl.pallas_call(
        pack_body,
        grid=(pl.cdiv(levels, GROUP),),
        in_specs=[
            rows,
            rows,
            pl.BlockSpec((lat_dev, 1), lambda i: (0, 0)),
            pl.BlockSpec((1, slots), lambda i: (0, 0)),
        ],
        out_specs=pl.BlockSpec((slots, GROUP * lat_dev), lambda i: (0, i)),
        out_shape=jax.ShapeDtypeStruct((slots, pl.cdiv(levels * lat_dev, LANES) * LANES), jnp.bfloat16),
        compiler_params=pltpu.CompilerParams(vmem_limit_bytes=VMEM_BYTES),
        cost_estimate=pl.CostEstimate(
            flops=2 * levels * lat_dev * slots,
            bytes_accessed=6 * levels * lat_dev * slots,
            transcendentals=0,
        ),
    )(north, south, counts, twice)


def unpack_body(in_ref, *refs):
    out_ref = refs[-1]
    _, group, lat_dev, slots = out_ref.shape
    rows = in_ref[...].T.astype(jnp.float32).reshape(group, lat_dev, slots)
    out_ref[0] = rows.astype(jnp.bfloat16)


def unpack(part, parts, levels, lat_dev, received, earlier):
    slots = received.shape[0]
    in_specs = [pl.BlockSpec((slots, GROUP * lat_dev), lambda i: (0, i))]
    operands = [received]
    aliases = {}
    if earlier is not None:
        in_specs.append(pl.BlockSpec(memory_space=pl.ANY))
        operands.append(earlier)
        aliases = {1: 0}
    return pl.pallas_call(
        unpack_body,
        grid=(pl.cdiv(levels, GROUP),),
        in_specs=in_specs,
        out_specs=pl.BlockSpec((1, GROUP, lat_dev, slots), lambda i: (part, i, 0, 0)),
        out_shape=jax.ShapeDtypeStruct((parts, levels, lat_dev, slots), jnp.bfloat16),
        input_output_aliases=aliases,
        compiler_params=pltpu.CompilerParams(vmem_limit_bytes=VMEM_BYTES),
        cost_estimate=pl.CostEstimate(
            flops=levels * lat_dev * slots,
            bytes_accessed=4 * levels * lat_dev * slots,
            transcendentals=0,
        ),
    )(*operands)


def lane_runs(lanes, source):
    runs = []
    for lane in range(LANES):
        where = source(lanes + lane)
        if where is None:
            continue
        tile = (where[0], where[1] // LANES)
        shift = (lane - where[1]) % LANES
        if runs and runs[-1][1:] == (tile, shift):
            runs[-1] = (lane + 1, tile, shift)
        else:
            runs.append((lane + 1, tile, shift))
    return runs


def merge_runs(runs, load, cache, lane_index):
    out = None
    for end, tile, shift in reversed(runs):
        if (tile, shift) not in cache:
            value = load(*tile)
            cache[tile, shift] = pltpu.roll(value, shift, 1) if shift else value
        value = cache[tile, shift]
        out = value if out is None else jnp.where(lane_index < end, value, out)
    return out


def group_size(lat_dev):
    return LANES // math.gcd(lat_dev, LANES)


def spread(recv_ref, rows_ref, first, group, lat_dev, slot_dev):
    lat_total = rows_ref.shape[0] * LANES
    base = pl.multiple_of(first * lat_dev, LANES)
    lane_index = lax.broadcasted_iota(jnp.int32, (slot_dev, LANES), 1)
    pairs = {}

    def load(device, tile):
        pair = device // 2
        if (pair, tile) not in pairs:
            pairs[pair, tile] = recv_ref[
                2 * pair * slot_dev : 2 * (pair + 1) * slot_dev, pl.ds(base + tile * LANES, LANES)
            ].astype(jnp.float32)
        at = (device % 2) * slot_dev
        return pairs[pair, tile][at : at + slot_dev]

    cache = {}
    for lanes in range(0, lat_total, LANES):
        for i in range(group):
            runs = lane_runs(lanes, lambda j: (j // lat_dev, i * lat_dev + j % lat_dev))
            row = pl.multiple_of((first + i) * slot_dev, slot_dev)
            rows_ref[lanes // LANES, pl.ds(row, slot_dev), :] = merge_runs(
                runs, load, cache, lane_index
            )


def gather(rows_ref, send_ref, first, group, lat_dev, slot_dev):
    devices = rows_ref.shape[0] * LANES // lat_dev
    base = pl.multiple_of(first * lat_dev, LANES)
    lane_index = lax.broadcasted_iota(jnp.int32, (slot_dev, LANES), 1)
    cache = {}

    def load(i, tile):
        row = pl.multiple_of((first + i) * slot_dev, slot_dev)
        return rows_ref[tile, pl.ds(row, slot_dev), :]

    for pair in range(devices // 2):
        for lanes in range(0, group * lat_dev, LANES):
            tiles = []
            for device in (2 * pair, 2 * pair + 1):
                runs = lane_runs(
                    lanes,
                    lambda l: (l // lat_dev, device * lat_dev + l % lat_dev)
                    if l < group * lat_dev
                    else None,
                )
                tiles.append(merge_runs(runs, load, cache, lane_index))
            send_ref[
                2 * pair * slot_dev : 2 * (pair + 1) * slot_dev, pl.ds(base + lanes, LANES)
            ] = jnp.concatenate(tiles, axis=0).astype(jnp.bfloat16)


def join_tiles(ref, rows):
    return jnp.concatenate([ref[tile, rows, :] for tile in range(ref.shape[0])], axis=1)


def split_tiles(ref, rows, value):
    for tile in range(ref.shape[0]):
        ref[tile, rows, :] = value[:, tile * LANES : (tile + 1) * LANES]


def all_groups(levels, lat_dev, body):
    group = group_size(lat_dev)
    full = levels // group

    @pl.loop(0, full)
    def _(g):
        body(g * group, group)

    if levels % group:
        body(full * group, levels % group)


def step_body(waves_ref, recv_ref, legendre_ref, counts_ref, rates_ref, to_ref, from_ref, *refs):
    state_ref, send_ref, rows_ref, spec_ref = refs[-4:]
    slot = pl.program_id(0)
    wave = waves_ref[slot]
    row_total, lat_total = legendre_ref.shape[1:]
    _, levels, slot_dev, _ = state_ref.shape
    lat_dev = lat_total // (recv_ref.shape[0] // slot_dev)

    @pl.when(slot == 0)
    def _():
        all_groups(
            levels, lat_dev, lambda c, n: spread(recv_ref, rows_ref, c, n, lat_dev, slot_dev)
        )

    own = pl.ds(slot, levels, stride=slot_dev)
    matrix = legendre_ref[0]
    direct = lax.dot_general(
        join_tiles(rows_ref, own).astype(jnp.bfloat16),
        matrix,
        (((1,), (1,)), ((), ())),
        preferred_element_type=jnp.float32,
    ).astype(jnp.bfloat16)
    modal = jnp.dot(to_ref[...], direct, preferred_element_type=jnp.float32)
    degree = wave + 2 * lax.broadcasted_iota(jnp.int32, (1, row_total), 1)
    degree_f = degree.astype(jnp.float32)
    scaled_degree = degree_f * (degree_f + 1.0) / float(NMAX * (NMAX + 1))
    scaled = (modal / (1.0 + rates_ref[...] * scaled_degree)).astype(jnp.bfloat16)
    state = jnp.dot(from_ref[...], scaled, preferred_element_type=jnp.float32)
    state = jnp.where(degree <= NMAX, state, 0.0)
    split_tiles(spec_ref, own, state)
    rows = jnp.dot(state.astype(jnp.bfloat16), matrix, preferred_element_type=jnp.float32)
    split_tiles(rows_ref, own, jnp.where(2 * wave < counts_ref[...], rows, 0.0))

    @pl.when(slot == slot_dev - 1)
    def _():
        all_groups(
            levels, lat_dev, lambda c, n: gather(rows_ref, send_ref, c, n, lat_dev, slot_dev)
        )

        @pl.loop(0, levels)
        def _(c):
            at = pl.multiple_of(c * slot_dev, slot_dev)
            state_ref[0, c] = join_tiles(spec_ref, pl.ds(at, slot_dev)).astype(jnp.bfloat16)


def spectral_step(part, parts, received, legendre, own_waves, counts, rates, to_t, from_t, earlier):
    slots, width = received.shape
    slot_dev, row_total, lat_total = legendre.shape
    levels = to_t.shape[0]
    whole = lambda shape: pl.BlockSpec(shape, lambda s, waves: (0,) * len(shape))
    in_specs = [
        whole((slots, width)),
        pl.BlockSpec((1, row_total, lat_total), lambda s, waves: (s, 0, 0)),
        whole((1, lat_total)),
        whole((levels, 1)),
        whole((levels, levels)),
        whole((levels, levels)),
    ]
    operands = [own_waves, received, legendre, counts, rates, to_t, from_t]
    aliases = {}
    if earlier is not None:
        in_specs.append(pl.BlockSpec(memory_space=pl.ANY))
        aliases = {len(operands): 0}
        operands.append(earlier)
    return pl.pallas_call(
        step_body,
        grid_spec=pltpu.PrefetchScalarGridSpec(
            num_scalar_prefetch=1,
            grid=(slot_dev,),
            in_specs=in_specs,
            out_specs=[
                pl.BlockSpec((1, levels, slot_dev, row_total), lambda s, waves: (part, 0, 0, 0)),
                whole((slots, width)),
            ],
            scratch_shapes=[
                pltpu.VMEM((lat_total // LANES, levels * slot_dev, LANES), jnp.float32),
                pltpu.VMEM((row_total // LANES, levels * slot_dev, LANES), jnp.float32),
            ],
        ),
        out_shape=[
            jax.ShapeDtypeStruct((parts, levels, slot_dev, row_total), jnp.bfloat16),
            jax.ShapeDtypeStruct((slots, width), jnp.bfloat16),
        ],
        input_output_aliases=aliases,
        compiler_params=pltpu.CompilerParams(vmem_limit_bytes=VMEM_BYTES),
        cost_estimate=pl.CostEstimate(
            flops=4 * slot_dev * row_total * lat_total * levels,
            bytes_accessed=2 * slot_dev * lat_total * (row_total + 3 * levels),
            transcendentals=0,
        ),
    )(*operands)


def per_device(
    north_rows, south_rows, lon_counts, slot_wave, legendre, mode_rates, to_modes, from_modes
):
    lat_dev, slots, channels = north_rows.shape
    slot_dev, row_total, lat_total = legendre.shape
    levels = to_modes.shape[0]
    parts = channels // levels
    my_index = lax.axis_index("wave")
    own_waves = lax.dynamic_slice_in_dim(slot_wave, my_index * slot_dev, slot_dev)
    local_counts = lax.dynamic_slice_in_dim(lon_counts, my_index * lat_dev, lat_dev)[:, None]
    twice = 2 * slot_wave[None, :]
    north = jnp.transpose(north_rows, (2, 0, 1)).reshape(parts, levels, lat_dev, slots)
    south = jnp.transpose(south_rows, (2, 0, 1)).reshape(parts, levels, lat_dev, slots)
    exchange = functools.partial(
        lax.all_to_all, axis_name="wave", split_axis=0, concat_axis=0, tiled=True
    )
    columns = [exchange(pack(part, north, south, local_counts, twice)) for part in range(parts)]
    spec_state = None
    returned = []
    for part in range(parts):
        spec_state, rows = spectral_step(
            part, parts, columns[part], legendre, own_waves, lon_counts[None, :],
            mode_rates[:, None], to_modes.T, from_modes.T, spec_state,
        )
        returned.append(exchange(rows))
    new_rows = None
    for part in range(parts):
        new_rows = unpack(part, parts, levels, lat_dev, returned[part], new_rows)
    new_rows = jnp.transpose(new_rows.reshape(channels, lat_dev, slots), (1, 2, 0))
    spec_state = jnp.transpose(spec_state.reshape(channels, slot_dev, row_total), (1, 2, 0))
    return (spec_state, new_rows)


def solution(mesh):
    in_specs = (
        P(("grp", "wave"), None, None),
        P(("grp", "wave"), None, None),
        P(),
        P(),
        P("wave", None, None),
        P(),
        P(),
        P(),
    )
    out_specs = (P(("grp", "wave"), None, None), P(("grp", "wave"), None, None))
    return jax.shard_map(
        per_device, mesh=mesh, in_specs=in_specs, out_specs=out_specs, check_vma=False
    )
```

```python
import functools
import math

import jax
import jax.numpy as jnp
from jax import lax
from jax.experimental import pallas as pl
from jax.experimental.pallas import tpu as pltpu
from jax.sharding import PartitionSpec as P

NMAX = 2559
VMEM_BYTES = 56 * 1024 * 1024
GROUP = 16
LANES = 128


def pack_body(counts_ref, waves_ref, north_ref, south_ref, *refs, partners):
    out_refs, live_ref = refs[-1 - partners : -1], refs[-1]
    _, group, lat_dev, slots = north_ref.shape
    my_index = lax.axis_index("wave")

    @pl.when(pl.program_id(0) == 0)
    def _():
        lane_index = lax.broadcasted_iota(jnp.int32, (1, slots), 1)
        twice = lax.fori_loop(
            0,
            slots,
            lambda i, row: jnp.where(lane_index == i, 2 * waves_ref[i], row),
            jnp.zeros((1, slots), jnp.int32),
        )

        @pl.loop(0, lat_dev)
        def _(i):
            count = counts_ref[my_index * lat_dev + i]
            live_ref[pl.ds(i, 1), :] = jnp.where(twice < count, 1.0, 0.0)

    live = live_ref[...] > 0.0
    summed = north_ref[0].astype(jnp.float32) + south_ref[0].astype(jnp.float32)
    summed = jnp.where(live[None], summed, 0.0).reshape(group * lat_dev, slots)
    slot_dev = slots // partners
    summed = pltpu.roll(summed, lax.rem(slots - my_index * slot_dev, slots), 1)
    columns = summed.astype(jnp.bfloat16).T
    for k in range(partners):
        out_refs[k][...] = columns[k * slot_dev : (k + 1) * slot_dev]


def pack(part, partners, north, south, counts, waves, after):
    _, levels, lat_dev, slots = north.shape
    width = pl.cdiv(levels * lat_dev, LANES) * LANES
    slot_dev = slots // partners
    rows = pl.BlockSpec((1, GROUP, lat_dev, slots), lambda i, *_: (part, i, 0, 0))
    return pl.pallas_call(
        functools.partial(pack_body, partners=partners),
        grid_spec=pltpu.PrefetchScalarGridSpec(
            num_scalar_prefetch=2,
            grid=(pl.cdiv(levels, GROUP),),
            in_specs=[rows, rows] + [pl.BlockSpec(memory_space=pl.ANY)] * len(after),
            out_specs=[pl.BlockSpec((slot_dev, GROUP * lat_dev), lambda i, *_: (0, i))] * partners,
            scratch_shapes=[pltpu.VMEM((lat_dev, slots), jnp.float32)],
        ),
        out_shape=[jax.ShapeDtypeStruct((slot_dev, width), jnp.bfloat16)] * partners,
        compiler_params=pltpu.CompilerParams(vmem_limit_bytes=VMEM_BYTES),
        cost_estimate=pl.CostEstimate(
            flops=2 * levels * lat_dev * slots,
            bytes_accessed=6 * levels * lat_dev * slots,
            transcendentals=0,
        ),
    )(counts, waves, north, south, *after)


def unpack_body(*refs, partners):
    in_refs, out_ref = refs[:partners], refs[-1]
    _, group, lat_dev, slots = out_ref.shape
    blocks = [ref[...].astype(jnp.float32) for ref in in_refs]
    rows = jnp.concatenate(blocks, axis=0).astype(jnp.bfloat16).T.astype(jnp.float32)
    rows = pltpu.roll(rows, lax.axis_index("wave") * (slots // partners), 1)
    out_ref[0] = rows.reshape(group, lat_dev, slots).astype(jnp.bfloat16)


def unpack(part, parts, levels, lat_dev, received, earlier):
    partners = len(received)
    slot_dev = received[0].shape[0]
    slots = partners * slot_dev
    in_specs = [pl.BlockSpec((slot_dev, GROUP * lat_dev), lambda i: (0, i))] * partners
    operands = [received[(partners - p) % partners] for p in range(partners)]
    aliases = {}
    if earlier is not None:
        in_specs.append(pl.BlockSpec(memory_space=pl.ANY))
        aliases = {len(operands): 0}
        operands.append(earlier)
    return pl.pallas_call(
        functools.partial(unpack_body, partners=partners),
        grid=(pl.cdiv(levels, GROUP),),
        in_specs=in_specs,
        out_specs=pl.BlockSpec((1, GROUP, lat_dev, slots), lambda i: (part, i, 0, 0)),
        out_shape=jax.ShapeDtypeStruct((parts, levels, lat_dev, slots), jnp.bfloat16),
        input_output_aliases=aliases,
        compiler_params=pltpu.CompilerParams(vmem_limit_bytes=VMEM_BYTES),
        cost_estimate=pl.CostEstimate(
            flops=levels * lat_dev * slots,
            bytes_accessed=4 * levels * lat_dev * slots,
            transcendentals=0,
        ),
    )(*operands)


def lane_runs(lanes, source):
    runs = []
    for lane in range(LANES):
        where = source(lanes + lane)
        if where is None:
            continue
        tile = (where[0], where[1] // LANES)
        shift = (lane - where[1]) % LANES
        if runs and runs[-1][1:] == (tile, shift):
            runs[-1] = (lane + 1, tile, shift)
        else:
            runs.append((lane + 1, tile, shift))
    return runs


def merge_runs(runs, load, cache, lane_index):
    out = None
    for end, tile, shift in reversed(runs):
        if (tile, shift) not in cache:
            value = load(*tile)
            cache[tile, shift] = pltpu.roll(value, shift, 1) if shift else value
        value = cache[tile, shift]
        out = value if out is None else jnp.where(lane_index < end, value, out)
    return out


def group_size(lat_dev):
    return LANES // math.gcd(lat_dev, LANES)


def spread(recv_ref, rows_ref, first, group, lat_dev, slot_dev):
    lat_total = rows_ref.shape[0] * LANES
    base = pl.multiple_of(first * lat_dev, LANES)
    lane_index = lax.broadcasted_iota(jnp.int32, (slot_dev, LANES), 1)

    def load(device, tile):
        return recv_ref[device, :, pl.ds(base + tile * LANES, LANES)].astype(jnp.float32)

    cache = {}
    for lanes in range(0, lat_total, LANES):
        for i in range(group):
            runs = lane_runs(lanes, lambda j: (j // lat_dev, i * lat_dev + j % lat_dev))
            row = pl.multiple_of((first + i) * slot_dev, slot_dev)
            rows_ref[lanes // LANES, pl.ds(row, slot_dev), :] = merge_runs(
                runs, load, cache, lane_index
            )


def gather(rows_ref, send_ref, first, group, lat_dev, slot_dev):
    devices = rows_ref.shape[0] * LANES // lat_dev
    base = pl.multiple_of(first * lat_dev, LANES)
    lane_index = lax.broadcasted_iota(jnp.int32, (slot_dev, LANES), 1)
    cache = {}

    def load(i, tile):
        row = pl.multiple_of((first + i) * slot_dev, slot_dev)
        return rows_ref[tile, pl.ds(row, slot_dev), :]

    for device in range(devices):
        for lanes in range(0, group * lat_dev, LANES):
            runs = lane_runs(
                lanes,
                lambda l: (l // lat_dev, device * lat_dev + l % lat_dev)
                if l < group * lat_dev
                else None,
            )
            tile = merge_runs(runs, load, cache, lane_index).astype(jnp.bfloat16)
            send_ref[device, :, pl.ds(base + lanes, LANES)] = tile


def join_tiles(ref, rows):
    return jnp.concatenate([ref[tile, rows, :] for tile in range(ref.shape[0])], axis=1)


def split_tiles(ref, rows, value):
    for tile in range(ref.shape[0]):
        ref[tile, rows, :] = value[:, tile * LANES : (tile + 1) * LANES]


def all_groups(levels, lat_dev, body):
    group = group_size(lat_dev)
    full = levels // group

    @pl.loop(0, full)
    def _(g):
        body(g * group, group)

    if levels % group:
        body(full * group, levels % group)


def step_body(waves_ref, *refs, partners):
    recv_refs, refs = refs[:partners], refs[partners:]
    legendre_ref, counts_ref, rates_ref, to_ref, from_ref = refs[:5]
    state_ref, send_refs = refs[-4 - partners], refs[-3 - partners : -3]
    rows_ref, spec_ref, blocks_ref = refs[-3:]
    slot = pl.program_id(0)
    my_index = lax.axis_index("wave")
    wave = waves_ref[slot]
    row_total, lat_total = legendre_ref.shape[1:]
    _, levels, slot_dev, _ = state_ref.shape
    lat_dev = lat_total // partners

    @pl.when(slot == 0)
    def _():
        for k in range(partners):
            blocks_ref[lax.rem(my_index + (partners - k), partners)] = recv_refs[k][...]
        all_groups(
            levels, lat_dev, lambda c, n: spread(blocks_ref, rows_ref, c, n, lat_dev, slot_dev)
        )

    own = pl.ds(slot, levels, stride=slot_dev)
    matrix = legendre_ref[0]
    direct = lax.dot_general(
        join_tiles(rows_ref, own).astype(jnp.bfloat16),
        matrix,
        (((1,), (1,)), ((), ())),
        preferred_element_type=jnp.float32,
    ).astype(jnp.bfloat16)
    modal = jnp.dot(to_ref[...], direct, preferred_element_type=jnp.float32)
    degree = wave + 2 * lax.broadcasted_iota(jnp.int32, (1, row_total), 1)
    degree_f = degree.astype(jnp.float32)
    scaled_degree = degree_f * (degree_f + 1.0) / float(NMAX * (NMAX + 1))
    scaled = (modal / (1.0 + rates_ref[...] * scaled_degree)).astype(jnp.bfloat16)
    state = jnp.dot(from_ref[...], scaled, preferred_element_type=jnp.float32)
    state = jnp.where(degree <= NMAX, state, 0.0)
    split_tiles(spec_ref, own, state)
    rows = jnp.dot(state.astype(jnp.bfloat16), matrix, preferred_element_type=jnp.float32)
    split_tiles(rows_ref, own, jnp.where(2 * wave < counts_ref[...], rows, 0.0))

    @pl.when(slot == slot_dev - 1)
    def _():
        all_groups(
            levels, lat_dev, lambda c, n: gather(rows_ref, blocks_ref, c, n, lat_dev, slot_dev)
        )
        for k in range(partners):
            send_refs[k][...] = blocks_ref[lax.rem(my_index + k, partners)]

        @pl.loop(0, levels)
        def _(c):
            at = pl.multiple_of(c * slot_dev, slot_dev)
            state_ref[0, c] = join_tiles(spec_ref, pl.ds(at, slot_dev)).astype(jnp.bfloat16)


def spectral_step(part, parts, received, legendre, own_waves, counts, rates, to_t, from_t, earlier):
    partners = len(received)
    width = received[0].shape[1]
    slot_dev, row_total, lat_total = legendre.shape
    levels = to_t.shape[0]
    whole = lambda shape: pl.BlockSpec(shape, lambda s, waves: (0,) * len(shape))
    in_specs = [whole((slot_dev, width))] * partners + [
        pl.BlockSpec((1, row_total, lat_total), lambda s, waves: (s, 0, 0)),
        whole((1, lat_total)),
        whole((levels, 1)),
        whole((levels, levels)),
        whole((levels, levels)),
    ]
    operands = [own_waves, *received, legendre, counts, rates, to_t, from_t]
    aliases = {}
    if earlier is not None:
        in_specs.append(pl.BlockSpec(memory_space=pl.ANY))
        aliases = {len(operands): 0}
        operands.append(earlier)
    return pl.pallas_call(
        functools.partial(step_body, partners=partners),
        grid_spec=pltpu.PrefetchScalarGridSpec(
            num_scalar_prefetch=1,
            grid=(slot_dev,),
            in_specs=in_specs,
            out_specs=[
                pl.BlockSpec((1, levels, slot_dev, row_total), lambda s, waves: (part, 0, 0, 0)),
            ]
            + [whole((slot_dev, width))] * partners,
            scratch_shapes=[
                pltpu.VMEM((lat_total // LANES, levels * slot_dev, LANES), jnp.float32),
                pltpu.VMEM((row_total // LANES, levels * slot_dev, LANES), jnp.float32),
                pltpu.VMEM((partners, slot_dev, width), jnp.bfloat16),
            ],
        ),
        out_shape=[
            jax.ShapeDtypeStruct((parts, levels, slot_dev, row_total), jnp.bfloat16),
        ]
        + [jax.ShapeDtypeStruct((slot_dev, width), jnp.bfloat16)] * partners,
        input_output_aliases=aliases,
        compiler_params=pltpu.CompilerParams(vmem_limit_bytes=VMEM_BYTES),
        cost_estimate=pl.CostEstimate(
            flops=4 * slot_dev * row_total * lat_total * levels,
            bytes_accessed=2 * slot_dev * lat_total * (row_total + 3 * levels),
            transcendentals=0,
        ),
    )(*operands)


def exchange(blocks):
    partners = len(blocks)
    received = list(blocks)
    for k in sorted(range(1, partners), key=lambda k: -min(k, partners - k)):
        pairs = [(i, (i + k) % partners) for i in range(partners)]
        received[k] = lax.ppermute(blocks[k], "wave", pairs)
    return received


def per_device(
    north_rows, south_rows, lon_counts, slot_wave, legendre, mode_rates, to_modes, from_modes
):
    lat_dev, slots, channels = north_rows.shape
    slot_dev, row_total, lat_total = legendre.shape
    levels = to_modes.shape[0]
    parts = channels // levels
    partners = slots // slot_dev
    my_index = lax.axis_index("wave")
    own_waves = lax.dynamic_slice_in_dim(slot_wave, my_index * slot_dev, slot_dev)
    north = jnp.transpose(north_rows, (2, 0, 1)).reshape(parts, levels, lat_dev, slots)
    south = jnp.transpose(south_rows, (2, 0, 1)).reshape(parts, levels, lat_dev, slots)
    columns = []
    for part in range(parts):
        after = columns[-1][partners // 4 + 1 : partners - partners // 4] if columns else []
        blocks = pack(part, partners, north, south, lon_counts, slot_wave, after)
        columns.append(exchange(blocks))
    spec_state = None
    returned = []
    for part in range(parts):
        spec_state, *blocks = spectral_step(
            part, parts, columns[part], legendre, own_waves, lon_counts[None, :],
            mode_rates[:, None], to_modes.T, from_modes.T, spec_state,
        )
        returned.append(exchange(blocks))
    new_rows = None
    for part in range(parts):
        new_rows = unpack(part, parts, levels, lat_dev, returned[part], new_rows)
    new_rows = jnp.transpose(new_rows.reshape(channels, lat_dev, slots), (1, 2, 0))
    spec_state = jnp.transpose(spec_state.reshape(channels, slot_dev, row_total), (1, 2, 0))
    return (spec_state, new_rows)


def solution(mesh):
    in_specs = (
        P(("grp", "wave"), None, None),
        P(("grp", "wave"), None, None),
        P(),
        P(),
        P("wave", None, None),
        P(),
        P(),
        P(),
    )
    out_specs = (P(("grp", "wave"), None, None), P(("grp", "wave"), None, None))
    return jax.shard_map(
        per_device, mesh=mesh, in_specs=in_specs, out_specs=out_specs, check_vma=False
    )
```

```python
import functools
import math

import jax
import jax.numpy as jnp
from jax import lax
from jax.experimental import pallas as pl
from jax.experimental.pallas import tpu as pltpu
from jax.sharding import PartitionSpec as P

NMAX = 2559
VMEM_BYTES = 62 * 1024 * 1024
GROUP = 48
LANES = 128


def flat_rows(value):
    group, lat_dev, slots = value.shape
    if lat_dev % 16:
        value = value.astype(jnp.float32)
    return value.reshape(group * lat_dev, slots).astype(jnp.bfloat16)


def pack_body(north_ref, south_ref, out_ref):
    summed = north_ref[0].astype(jnp.float32) + south_ref[0].astype(jnp.float32)
    out_ref[...] = flat_rows(summed.astype(jnp.bfloat16)).T


def pack(part, north, south):
    _, levels, lat_dev, slots = north.shape
    rows = pl.BlockSpec((1, GROUP, lat_dev, slots), lambda i: (part, i, 0, 0))
    return pl.pallas_call(
        pack_body,
        grid=(pl.cdiv(levels, GROUP),),
        in_specs=[rows, rows],
        out_specs=pl.BlockSpec((slots, GROUP * lat_dev), lambda i: (0, i)),
        out_shape=jax.ShapeDtypeStruct((slots, pl.cdiv(levels * lat_dev, LANES) * LANES), jnp.bfloat16),
        compiler_params=pltpu.CompilerParams(vmem_limit_bytes=VMEM_BYTES),
        cost_estimate=pl.CostEstimate(
            flops=2 * levels * lat_dev * slots,
            bytes_accessed=6 * levels * lat_dev * slots,
            transcendentals=0,
        ),
    )(north, south)


def unpack_body(in_ref, *refs):
    out_ref = refs[-1]
    _, group, lat_dev, slots = out_ref.shape
    rows = in_ref[...].T
    if lat_dev % 16:
        rows = rows.astype(jnp.float32)
    out_ref[0] = rows.reshape(group, lat_dev, slots).astype(jnp.bfloat16)


def unpack(part, parts, levels, lat_dev, received, earlier):
    slots = received.shape[0]
    in_specs = [pl.BlockSpec((slots, GROUP * lat_dev), lambda i: (0, i))]
    operands = [received]
    aliases = {}
    if earlier is not None:
        in_specs.append(pl.BlockSpec(memory_space=pl.ANY))
        operands.append(earlier)
        aliases = {1: 0}
    return pl.pallas_call(
        unpack_body,
        grid=(pl.cdiv(levels, GROUP),),
        in_specs=in_specs,
        out_specs=pl.BlockSpec((1, GROUP, lat_dev, slots), lambda i: (part, i, 0, 0)),
        out_shape=jax.ShapeDtypeStruct((parts, levels, lat_dev, slots), jnp.bfloat16),
        input_output_aliases=aliases,
        compiler_params=pltpu.CompilerParams(vmem_limit_bytes=VMEM_BYTES),
        cost_estimate=pl.CostEstimate(
            flops=levels * lat_dev * slots,
            bytes_accessed=4 * levels * lat_dev * slots,
            transcendentals=0,
        ),
    )(*operands)


def lane_runs(lanes, source):
    runs = []
    for lane in range(LANES):
        where = source(lanes + lane)
        if where is None:
            continue
        tile = (where[0], where[1] // LANES)
        shift = (lane - where[1]) % LANES
        if runs and runs[-1][1:] == (tile, shift):
            runs[-1] = (lane + 1, tile, shift)
        else:
            runs.append((lane + 1, tile, shift))
    return runs


def merge_runs(runs, load, cache, lane_index):
    out = None
    for end, tile, shift in reversed(runs):
        if (tile, shift) not in cache:
            value = load(*tile)
            cache[tile, shift] = pltpu.roll(value, shift, 1) if shift else value
        value = cache[tile, shift]
        out = value if out is None else jnp.where(lane_index < end, value, out)
    return out


def group_size(lat_dev):
    return LANES // math.gcd(lat_dev, LANES)


def spread(recv_ref, rows_ref, first, group, lat_dev, slot_dev):
    lat_total = rows_ref.shape[0] * LANES
    base = pl.multiple_of(first * lat_dev, LANES)
    lane_index = lax.broadcasted_iota(jnp.int32, (slot_dev, LANES), 1)
    pairs = {}

    def load(device, tile):
        pair = device // 2
        if (pair, tile) not in pairs:
            pairs[pair, tile] = recv_ref[
                2 * pair * slot_dev : 2 * (pair + 1) * slot_dev, pl.ds(base + tile * LANES, LANES)
            ].astype(jnp.float32)
        at = (device % 2) * slot_dev
        return pairs[pair, tile][at : at + slot_dev]

    cache = {}
    for lanes in range(0, lat_total, LANES):
        for i in range(group):
            runs = lane_runs(lanes, lambda j: (j // lat_dev, i * lat_dev + j % lat_dev))
            row = pl.multiple_of((first + i) * slot_dev, slot_dev)
            rows_ref[lanes // LANES, pl.ds(row, slot_dev), :] = merge_runs(
                runs, load, cache, lane_index
            )


def gather(rows_ref, send_ref, first, group, lat_dev, slot_dev):
    devices = rows_ref.shape[0] * LANES // lat_dev
    base = pl.multiple_of(first * lat_dev, LANES)
    lane_index = lax.broadcasted_iota(jnp.int32, (slot_dev, LANES), 1)
    cache = {}

    def load(i, tile):
        row = pl.multiple_of((first + i) * slot_dev, slot_dev)
        return rows_ref[tile, pl.ds(row, slot_dev), :]

    for pair in range(devices // 2):
        for lanes in range(0, group * lat_dev, LANES):
            tiles = []
            for device in (2 * pair, 2 * pair + 1):
                runs = lane_runs(
                    lanes,
                    lambda l: (l // lat_dev, device * lat_dev + l % lat_dev)
                    if l < group * lat_dev
                    else None,
                )
                tiles.append(merge_runs(runs, load, cache, lane_index))
            send_ref[
                2 * pair * slot_dev : 2 * (pair + 1) * slot_dev, pl.ds(base + lanes, LANES)
            ] = jnp.concatenate(tiles, axis=0).astype(jnp.bfloat16)


def join_tiles(ref, rows):
    return jnp.concatenate([ref[tile, rows, :] for tile in range(ref.shape[0])], axis=1)


def split_tiles(ref, rows, value):
    for tile in range(ref.shape[0]):
        ref[tile, rows, :] = value[:, tile * LANES : (tile + 1) * LANES]


def all_groups(levels, lat_dev, body):
    group = group_size(lat_dev)
    full = levels // group

    @pl.loop(0, full)
    def _(g):
        body(g * group, group)

    if levels % group:
        body(full * group, levels % group)


def step_body(waves_ref, recv_ref, legendre_ref, counts_ref, rates_ref, to_ref, from_ref, *refs):
    state_ref, send_ref, rows_ref, spec_ref = refs[-4:]
    slot = pl.program_id(0)
    wave = waves_ref[slot]
    row_total, lat_total = legendre_ref.shape[1:]
    _, levels, slot_dev, _ = state_ref.shape
    lat_dev = lat_total // (recv_ref.shape[0] // slot_dev)

    @pl.when(slot == 0)
    def _():
        all_groups(
            levels, lat_dev, lambda c, n: spread(recv_ref, rows_ref, c, n, lat_dev, slot_dev)
        )

    own = pl.ds(slot, levels, stride=slot_dev)
    matrix = legendre_ref[0]
    live = 2 * wave < counts_ref[...]
    direct = lax.dot_general(
        jnp.where(live, join_tiles(rows_ref, own), 0.0).astype(jnp.bfloat16),
        matrix,
        (((1,), (1,)), ((), ())),
        preferred_element_type=jnp.float32,
    ).astype(jnp.bfloat16)
    modal = jnp.dot(to_ref[...], direct, preferred_element_type=jnp.float32)
    degree = wave + 2 * lax.broadcasted_iota(jnp.int32, (1, row_total), 1)
    degree_f = degree.astype(jnp.float32)
    scaled_degree = degree_f * (degree_f + 1.0) / float(NMAX * (NMAX + 1))
    scaled = (modal / (1.0 + rates_ref[...] * scaled_degree)).astype(jnp.bfloat16)
    state = jnp.dot(from_ref[...], scaled, preferred_element_type=jnp.float32)
    state = jnp.where(degree <= NMAX, state, 0.0)
    split_tiles(spec_ref, own, state)
    rows = jnp.dot(state.astype(jnp.bfloat16), matrix, preferred_element_type=jnp.float32)
    split_tiles(rows_ref, own, jnp.where(live, rows, 0.0))

    @pl.when(slot == slot_dev - 1)
    def _():
        all_groups(
            levels, lat_dev, lambda c, n: gather(rows_ref, send_ref, c, n, lat_dev, slot_dev)
        )

        @pl.loop(0, levels)
        def _(c):
            at = pl.multiple_of(c * slot_dev, slot_dev)
            state_ref[0, c] = join_tiles(spec_ref, pl.ds(at, slot_dev)).astype(jnp.bfloat16)


def spectral_step(part, parts, received, legendre, own_waves, counts, rates, to_t, from_t, earlier):
    slots, width = received.shape
    slot_dev, row_total, lat_total = legendre.shape
    levels = to_t.shape[0]
    whole = lambda shape: pl.BlockSpec(shape, lambda s, waves: (0,) * len(shape))
    in_specs = [
        whole((slots, width)),
        pl.BlockSpec((1, row_total, lat_total), lambda s, waves: (s, 0, 0)),
        whole((1, lat_total)),
        whole((levels, 1)),
        whole((levels, levels)),
        whole((levels, levels)),
    ]
    operands = [own_waves, received, legendre, counts, rates, to_t, from_t]
    aliases = {}
    if earlier is not None:
        in_specs.append(pl.BlockSpec(memory_space=pl.ANY))
        aliases = {len(operands): 0}
        operands.append(earlier)
    return pl.pallas_call(
        step_body,
        grid_spec=pltpu.PrefetchScalarGridSpec(
            num_scalar_prefetch=1,
            grid=(slot_dev,),
            in_specs=in_specs,
            out_specs=[
                pl.BlockSpec((1, levels, slot_dev, row_total), lambda s, waves: (part, 0, 0, 0)),
                whole((slots, width)),
            ],
            scratch_shapes=[
                pltpu.VMEM((lat_total // LANES, levels * slot_dev, LANES), jnp.float32),
                pltpu.VMEM((row_total // LANES, levels * slot_dev, LANES), jnp.float32),
            ],
        ),
        out_shape=[
            jax.ShapeDtypeStruct((parts, levels, slot_dev, row_total), jnp.bfloat16),
            jax.ShapeDtypeStruct((slots, width), jnp.bfloat16),
        ],
        input_output_aliases=aliases,
        compiler_params=pltpu.CompilerParams(vmem_limit_bytes=VMEM_BYTES),
        cost_estimate=pl.CostEstimate(
            flops=4 * slot_dev * row_total * lat_total * levels,
            bytes_accessed=2 * slot_dev * lat_total * (row_total + 3 * levels),
            transcendentals=0,
        ),
    )(*operands)


def per_device(
    north_rows, south_rows, lon_counts, slot_wave, legendre, mode_rates, to_modes, from_modes
):
    lat_dev, slots, channels = north_rows.shape
    slot_dev, row_total, lat_total = legendre.shape
    levels = to_modes.shape[0]
    parts = channels // levels
    my_index = lax.axis_index("wave")
    own_waves = lax.dynamic_slice_in_dim(slot_wave, my_index * slot_dev, slot_dev)
    north = jnp.transpose(north_rows, (2, 0, 1)).reshape(parts, levels, lat_dev, slots)
    south = jnp.transpose(south_rows, (2, 0, 1)).reshape(parts, levels, lat_dev, slots)
    exchange = functools.partial(
        lax.all_to_all, axis_name="wave", split_axis=0, concat_axis=0, tiled=True
    )
    columns = [exchange(pack(part, north, south)) for part in range(parts)]
    spec_state = None
    returned = []
    for part in range(parts):
        spec_state, rows = spectral_step(
            part, parts, columns[part], legendre, own_waves, lon_counts[None, :],
            mode_rates[:, None], to_modes.T, from_modes.T, spec_state,
        )
        returned.append(exchange(rows))
    new_rows = None
    for part in range(parts):
        new_rows = unpack(part, parts, levels, lat_dev, returned[part], new_rows)
    new_rows = jnp.transpose(new_rows.reshape(channels, lat_dev, slots), (1, 2, 0))
    spec_state = jnp.transpose(spec_state.reshape(channels, slot_dev, row_total), (1, 2, 0))
    return (spec_state, new_rows)


def solution(mesh):
    in_specs = (
        P(("grp", "wave"), None, None),
        P(("grp", "wave"), None, None),
        P(),
        P(),
        P("wave", None, None),
        P(),
        P(),
        P(),
    )
    out_specs = (P(("grp", "wave"), None, None), P(("grp", "wave"), None, None))
    return jax.shard_map(
        per_device, mesh=mesh, in_specs=in_specs, out_specs=out_specs, check_vma=False
    )
```

```python
import functools
import math

import jax
import jax.numpy as jnp
from jax import lax
from jax.experimental import pallas as pl
from jax.experimental.pallas import tpu as pltpu
from jax.sharding import PartitionSpec as P

NMAX = 2559
VMEM_BYTES = 255 * 256 * 1024
GROUP = 48
LANES = 128
EARLY = 5


def flat_rows(value):
    group, lat_dev, slots = value.shape
    if lat_dev % 16:
        value = value.astype(jnp.float32)
    return value.reshape(group * lat_dev, slots).astype(jnp.bfloat16)


def partner(my_index, half, turn):
    other = jnp.where(my_index < half, half, 0)
    return other + lax.rem(lax.rem(my_index, half) + turn + half, half)


def own_half(my_index, half):
    return jnp.where(my_index < half, 0, half)


def take_blocks(near_ref, far_refs, blocks_ref):
    half = len(far_refs)
    my_index = lax.axis_index("wave")
    base = own_half(my_index, half)
    for i in range(half):
        blocks_ref[base + i] = near_ref[i]
        blocks_ref[partner(my_index, half, -i)] = far_refs[i][...]


def give_blocks(blocks_ref, near_ref, far_refs):
    half = len(far_refs)
    my_index = lax.axis_index("wave")
    base = own_half(my_index, half)
    for i in range(half):
        near_ref[i] = blocks_ref[base + i]
        far_refs[i][...] = blocks_ref[partner(my_index, half, i)]


def pack_body(north_ref, south_ref, near_ref, *refs):
    far_refs, blocks_ref = refs[:-1], refs[-1]
    slot_dev = blocks_ref.shape[1]
    summed = north_ref[0].astype(jnp.float32) + south_ref[0].astype(jnp.float32)
    columns = flat_rows(summed.astype(jnp.bfloat16)).T
    for device in range(blocks_ref.shape[0]):
        blocks_ref[device] = columns[device * slot_dev : (device + 1) * slot_dev]
    give_blocks(blocks_ref, near_ref, far_refs)


def block_shapes(half, slot_dev, width):
    near = jax.ShapeDtypeStruct((half, slot_dev, width), jnp.bfloat16)
    return [near] + [jax.ShapeDtypeStruct((slot_dev, width), jnp.bfloat16)] * half


def block_specs(half, slot_dev, lanes):
    near = pl.BlockSpec((half, slot_dev, lanes), lambda i: (0, 0, i))
    return [near] + [pl.BlockSpec((slot_dev, lanes), lambda i: (0, i))] * half


def pack(part, half, north, south):
    _, levels, lat_dev, slots = north.shape
    slot_dev = slots // (2 * half)
    width = pl.cdiv(levels * lat_dev, LANES) * LANES
    rows = pl.BlockSpec((1, GROUP, lat_dev, slots), lambda i: (part, i, 0, 0))
    return pl.pallas_call(
        pack_body,
        grid=(pl.cdiv(levels, GROUP),),
        in_specs=[rows, rows],
        out_specs=block_specs(half, slot_dev, GROUP * lat_dev),
        out_shape=block_shapes(half, slot_dev, width),
        scratch_shapes=[pltpu.VMEM((2 * half, slot_dev, GROUP * lat_dev), jnp.bfloat16)],
        compiler_params=pltpu.CompilerParams(vmem_limit_bytes=VMEM_BYTES),
        cost_estimate=pl.CostEstimate(
            flops=2 * levels * lat_dev * slots,
            bytes_accessed=6 * levels * lat_dev * slots,
            transcendentals=0,
        ),
    )(north, south)


def unpack_body(near_ref, *refs, half, passed):
    far_refs, out_ref, blocks_ref = refs[:half], refs[-2 - passed], refs[-1]
    _, group, lat_dev, slots = out_ref.shape
    take_blocks(near_ref, far_refs, blocks_ref)
    blocks = [blocks_ref[device].astype(jnp.float32) for device in range(2 * half)]
    rows = jnp.concatenate(blocks, axis=0).astype(jnp.bfloat16).T
    if lat_dev % 16:
        rows = rows.astype(jnp.float32)
    out_ref[0] = rows.reshape(group, lat_dev, slots).astype(jnp.bfloat16)


def unpack(part, parts, levels, lat_dev, received, earlier, waiting):
    half, slot_dev, _ = received[0].shape
    slots = 2 * half * slot_dev
    in_specs = block_specs(half, slot_dev, GROUP * lat_dev)
    operands = list(received)
    aliases = {}
    if earlier is not None:
        in_specs.append(pl.BlockSpec(memory_space=pl.ANY))
        aliases = {len(operands): 0}
        operands.append(earlier)
    anywhere = pl.BlockSpec(memory_space=pl.ANY)
    for i, block in enumerate(waiting):
        aliases[len(operands)] = 1 + i
        operands.append(block)
        in_specs.append(anywhere)
    outs = pl.pallas_call(
        functools.partial(unpack_body, half=half, passed=len(waiting)),
        grid=(pl.cdiv(levels, GROUP),),
        in_specs=in_specs,
        out_specs=[pl.BlockSpec((1, GROUP, lat_dev, slots), lambda i: (part, i, 0, 0))]
        + [anywhere] * len(waiting),
        out_shape=[jax.ShapeDtypeStruct((parts, levels, lat_dev, slots), jnp.bfloat16)]
        + [jax.ShapeDtypeStruct(block.shape, block.dtype) for block in waiting],
        scratch_shapes=[pltpu.VMEM((2 * half, slot_dev, GROUP * lat_dev), jnp.bfloat16)],
        input_output_aliases=aliases,
        compiler_params=pltpu.CompilerParams(vmem_limit_bytes=VMEM_BYTES),
        cost_estimate=pl.CostEstimate(
            flops=levels * lat_dev * slots,
            bytes_accessed=4 * levels * lat_dev * slots,
            transcendentals=0,
        ),
    )(*operands)
    return outs[0], outs[1:]


def lane_runs(lanes, source):
    runs = []
    for lane in range(LANES):
        where = source(lanes + lane)
        if where is None:
            continue
        tile = (where[0], where[1] // LANES)
        shift = (lane - where[1]) % LANES
        if runs and runs[-1][1:] == (tile, shift):
            runs[-1] = (lane + 1, tile, shift)
        else:
            runs.append((lane + 1, tile, shift))
    return runs


def merge_runs(runs, load, cache, lane_index):
    out = None
    for end, tile, shift in reversed(runs):
        if (tile, shift) not in cache:
            value = load(*tile)
            cache[tile, shift] = pltpu.roll(value, shift, 1) if shift else value
        value = cache[tile, shift]
        out = value if out is None else jnp.where(lane_index < end, value, out)
    return out


def group_size(lat_dev):
    return LANES // math.gcd(lat_dev, LANES)


def spread(recv_ref, rows_ref, first, group, lat_dev, slot_dev):
    lat_total = rows_ref.shape[0] * LANES
    base = pl.multiple_of(first * lat_dev, LANES)
    lane_index = lax.broadcasted_iota(jnp.int32, (slot_dev, LANES), 1)

    def load(device, tile):
        return recv_ref[device, :, pl.ds(base + tile * LANES, LANES)].astype(jnp.float32)

    cache = {}
    for lanes in range(0, lat_total, LANES):
        for i in range(group):
            runs = lane_runs(lanes, lambda j: (j // lat_dev, i * lat_dev + j % lat_dev))
            row = pl.multiple_of((first + i) * slot_dev, slot_dev)
            rows_ref[lanes // LANES, pl.ds(row, slot_dev), :] = merge_runs(
                runs, load, cache, lane_index
            )


def gather(rows_ref, send_ref, first, group, lat_dev, slot_dev):
    devices = rows_ref.shape[0] * LANES // lat_dev
    base = pl.multiple_of(first * lat_dev, LANES)
    lane_index = lax.broadcasted_iota(jnp.int32, (slot_dev, LANES), 1)
    cache = {}

    def load(i, tile):
        row = pl.multiple_of((first + i) * slot_dev, slot_dev)
        return rows_ref[tile, pl.ds(row, slot_dev), :]

    for device in range(devices):
        for lanes in range(0, group * lat_dev, LANES):
            runs = lane_runs(
                lanes,
                lambda l: (l // lat_dev, device * lat_dev + l % lat_dev)
                if l < group * lat_dev
                else None,
            )
            tile = merge_runs(runs, load, cache, lane_index).astype(jnp.bfloat16)
            send_ref[device, :, pl.ds(base + lanes, LANES)] = tile


def join_tiles(ref, rows):
    return jnp.concatenate([ref[tile, rows, :] for tile in range(ref.shape[0])], axis=1)


def split_tiles(ref, rows, value):
    for tile in range(ref.shape[0]):
        ref[tile, rows, :] = value[:, tile * LANES : (tile + 1) * LANES]


def all_groups(levels, lat_dev, body):
    group = group_size(lat_dev)
    full = levels // group

    @pl.loop(0, full)
    def _(g):
        body(g * group, group)

    if levels % group:
        body(full * group, levels % group)


def step_body(waves_ref, recv_ref, *refs, half, passed):
    recv_refs, refs = refs[:half], refs[half:]
    legendre_ref, counts_ref, rates_ref, to_ref, from_ref = refs[:5]
    outs = refs[len(refs) - 5 - half - passed :]
    state_ref, send_ref, send_refs = outs[0], outs[1], outs[2 : 2 + half]
    rows_ref, spec_ref, blocks_ref = refs[-3:]
    slot = pl.program_id(0)
    wave = waves_ref[slot]
    row_total, lat_total = legendre_ref.shape[1:]
    _, levels, slot_dev, _ = state_ref.shape
    lat_dev = lat_total // (2 * half)

    @pl.when(slot == 0)
    def _():
        take_blocks(recv_ref, recv_refs, blocks_ref)
        all_groups(
            levels, lat_dev, lambda c, n: spread(blocks_ref, rows_ref, c, n, lat_dev, slot_dev)
        )

    own = pl.ds(slot, levels, stride=slot_dev)
    matrix = legendre_ref[0]
    live = 2 * wave < counts_ref[...]
    direct = lax.dot_general(
        jnp.where(live, join_tiles(rows_ref, own), 0.0).astype(jnp.bfloat16),
        matrix,
        (((1,), (1,)), ((), ())),
        preferred_element_type=jnp.float32,
    ).astype(jnp.bfloat16)
    modal = jnp.dot(to_ref[...], direct, preferred_element_type=jnp.float32)
    degree = wave + 2 * lax.broadcasted_iota(jnp.int32, (1, row_total), 1)
    degree_f = degree.astype(jnp.float32)
    scaled_degree = degree_f * (degree_f + 1.0) / float(NMAX * (NMAX + 1))
    scaled = (modal / (1.0 + rates_ref[...] * scaled_degree)).astype(jnp.bfloat16)
    state = jnp.dot(from_ref[...], scaled, preferred_element_type=jnp.float32)
    state = jnp.where(degree <= NMAX, state, 0.0)
    split_tiles(spec_ref, own, state)
    rows = jnp.dot(state.astype(jnp.bfloat16), matrix, preferred_element_type=jnp.float32)
    split_tiles(rows_ref, own, jnp.where(live, rows, 0.0))

    @pl.when(slot == slot_dev - 1)
    def _():
        all_groups(
            levels, lat_dev, lambda c, n: gather(rows_ref, blocks_ref, c, n, lat_dev, slot_dev)
        )
        give_blocks(blocks_ref, send_ref, send_refs)

        @pl.loop(0, levels)
        def _(c):
            at = pl.multiple_of(c * slot_dev, slot_dev)
            state_ref[0, c] = join_tiles(spec_ref, pl.ds(at, slot_dev)).astype(jnp.bfloat16)


def spectral_step(part, parts, received, legendre, own_waves, counts, rates, to_t, from_t, earlier, waiting):
    half, _, width = received[0].shape
    slot_dev, row_total, lat_total = legendre.shape
    levels = to_t.shape[0]
    whole = lambda shape: pl.BlockSpec(shape, lambda s, waves: (0,) * len(shape))
    shapes = block_shapes(half, slot_dev, width)
    in_specs = [whole(shape.shape) for shape in shapes] + [
        pl.BlockSpec((1, row_total, lat_total), lambda s, waves: (s, 0, 0)),
        whole((1, lat_total)),
        whole((levels, 1)),
        whole((levels, levels)),
        whole((levels, levels)),
    ]
    operands = [own_waves, *received, legendre, counts, rates, to_t, from_t]
    anywhere = pl.BlockSpec(memory_space=pl.ANY)
    aliases = {}
    if earlier is not None:
        aliases[len(operands)] = 0
        operands.append(earlier)
        in_specs.append(anywhere)
    for i, block in enumerate(waiting):
        aliases[len(operands)] = 1 + len(shapes) + i
        operands.append(block)
        in_specs.append(anywhere)
    outs = pl.pallas_call(
        functools.partial(step_body, half=half, passed=len(waiting)),
        grid_spec=pltpu.PrefetchScalarGridSpec(
            num_scalar_prefetch=1,
            grid=(slot_dev,),
            in_specs=in_specs,
            out_specs=[
                pl.BlockSpec((1, levels, slot_dev, row_total), lambda s, waves: (part, 0, 0, 0)),
            ]
            + [whole(shape.shape) for shape in shapes]
            + [anywhere] * len(waiting),
            scratch_shapes=[
                pltpu.VMEM((lat_total // LANES, levels * slot_dev, LANES), jnp.float32),
                pltpu.VMEM((row_total // LANES, levels * slot_dev, LANES), jnp.float32),
                pltpu.VMEM((2 * half, slot_dev, width), jnp.bfloat16),
            ],
        ),
        out_shape=[
            jax.ShapeDtypeStruct((parts, levels, slot_dev, row_total), jnp.bfloat16),
            *shapes,
            *[jax.ShapeDtypeStruct(block.shape, block.dtype) for block in waiting],
        ],
        input_output_aliases=aliases,
        compiler_params=pltpu.CompilerParams(vmem_limit_bytes=VMEM_BYTES),
        cost_estimate=pl.CostEstimate(
            flops=16 * slot_dev * row_total * lat_total * levels,
            bytes_accessed=2 * slot_dev * lat_total * (row_total + 3 * levels),
            transcendentals=0,
        ),
    )(*operands)
    return outs[0], outs[1 : 1 + len(shapes)], outs[1 + len(shapes) :]


def exchange_near(block, half):
    groups = [list(range(half)), list(range(half, 2 * half))]
    return lax.all_to_all(
        block, "wave", split_axis=0, concat_axis=0, tiled=True, axis_index_groups=groups
    )


def exchange_far(block, half, turn):
    pairs = [
        (i, (half if i < half else 0) + (i % half + turn) % half) for i in range(2 * half)
    ]
    return lax.ppermute(block, "wave", pairs)


def per_device(
    north_rows, south_rows, lon_counts, slot_wave, legendre, mode_rates, to_modes, from_modes
):
    lat_dev, slots, channels = north_rows.shape
    slot_dev, row_total, lat_total = legendre.shape
    levels = to_modes.shape[0]
    parts = channels // levels
    my_index = lax.axis_index("wave")
    own_waves = lax.dynamic_slice_in_dim(slot_wave, my_index * slot_dev, slot_dev)
    north = jnp.transpose(north_rows, (2, 0, 1)).reshape(parts, levels, lat_dev, slots)
    south = jnp.transpose(south_rows, (2, 0, 1)).reshape(parts, levels, lat_dev, slots)
    half = slots // slot_dev // 2
    early = 1 + min(EARLY, half)
    send = lambda blocks: [exchange_near(blocks[0], half)] + [
        exchange_far(block, half, turn) for turn, block in enumerate(blocks[1:])
    ]
    sent = [list(pack(part, half, north, south)) for part in range(parts)]
    returned = []
    spec_state = None
    for part in range(parts):
        beside = sent[part + 1] if part + 1 < parts else (returned or [[]])[-1]
        spec_state, blocks, beside[early:] = spectral_step(
            part, parts, send(sent[part]), legendre, own_waves, lon_counts[None, :],
            mode_rates[:, None], to_modes.T, from_modes.T, spec_state, beside[early:],
        )
        returned.append(list(blocks))
    new_rows = None
    for part in range(parts):
        last = returned[part + 1] if part + 1 < parts else []
        new_rows, last[:1] = unpack(
            part, parts, levels, lat_dev, send(returned[part]), new_rows, last[:1]
        )
    new_rows = jnp.transpose(new_rows.reshape(channels, lat_dev, slots), (1, 2, 0))
    spec_state = jnp.transpose(spec_state.reshape(channels, slot_dev, row_total), (1, 2, 0))
    return (spec_state, new_rows)


def solution(mesh):
    in_specs = (
        P(("grp", "wave"), None, None),
        P(("grp", "wave"), None, None),
        P(),
        P(),
        P("wave", None, None),
        P(),
        P(),
        P(),
    )
    out_specs = (P(("grp", "wave"), None, None), P(("grp", "wave"), None, None))
    return jax.shard_map(
        per_device, mesh=mesh, in_specs=in_specs, out_specs=out_specs, check_vma=False
    )
```

```python
import functools
import math

import jax
import jax.numpy as jnp
from jax import lax
from jax.experimental import pallas as pl
from jax.experimental.pallas import tpu as pltpu
from jax.sharding import PartitionSpec as P

NMAX = 2559
VMEM_BYTES = 255 * 256 * 1024
GROUP = 48
LANES = 128
EARLY = 5


def flat_rows(value):
    group, lat_dev, slots = value.shape
    if lat_dev % 16:
        value = value.astype(jnp.float32)
    return value.reshape(group * lat_dev, slots).astype(jnp.bfloat16)


def partner(my_index, half, turn):
    other = jnp.where(my_index < half, half, 0)
    return other + lax.rem(lax.rem(my_index, half) + turn + half, half)


def own_half(my_index, half):
    return jnp.where(my_index < half, 0, half)


def take_blocks(near_ref, far_refs, blocks_ref):
    half = len(far_refs)
    my_index = lax.axis_index("wave")
    base = own_half(my_index, half)
    for i in range(half):
        blocks_ref[base + i] = near_ref[i]
        blocks_ref[partner(my_index, half, -i)] = far_refs[i][...]


def give_blocks(blocks_ref, near_ref, far_refs):
    half = len(far_refs)
    my_index = lax.axis_index("wave")
    base = own_half(my_index, half)
    for i in range(half):
        near_ref[i] = blocks_ref[base + i]
        far_refs[i][...] = blocks_ref[partner(my_index, half, i)]


def pack_body(north_ref, south_ref, near_ref, *refs):
    far_refs, blocks_ref = refs[:-1], refs[-1]
    slot_dev = blocks_ref.shape[1]
    summed = north_ref[0].astype(jnp.float32) + south_ref[0].astype(jnp.float32)
    columns = flat_rows(summed.astype(jnp.bfloat16)).T
    for device in range(blocks_ref.shape[0]):
        blocks_ref[device] = columns[device * slot_dev : (device + 1) * slot_dev]
    give_blocks(blocks_ref, near_ref, far_refs)


def like(blocks):
    return [jax.ShapeDtypeStruct(block.shape, block.dtype) for block in blocks]


def block_shapes(half, slot_dev, width):
    near = jax.ShapeDtypeStruct((half, slot_dev, width), jnp.bfloat16)
    return [near] + [jax.ShapeDtypeStruct((slot_dev, width), jnp.bfloat16)] * half


def block_specs(half, slot_dev, lanes):
    near = pl.BlockSpec((half, slot_dev, lanes), lambda i: (0, 0, i))
    return [near] + [pl.BlockSpec((slot_dev, lanes), lambda i: (0, i))] * half


def pack(part, half, north, south):
    _, levels, lat_dev, slots = north.shape
    slot_dev = slots // (2 * half)
    width = pl.cdiv(levels * lat_dev, LANES) * LANES
    rows = pl.BlockSpec((1, GROUP, lat_dev, slots), lambda i: (part, i, 0, 0))
    return pl.pallas_call(
        pack_body,
        grid=(pl.cdiv(levels, GROUP),),
        in_specs=[rows, rows],
        out_specs=block_specs(half, slot_dev, GROUP * lat_dev),
        out_shape=block_shapes(half, slot_dev, width),
        scratch_shapes=[pltpu.VMEM((2 * half, slot_dev, GROUP * lat_dev), jnp.bfloat16)],
        compiler_params=pltpu.CompilerParams(vmem_limit_bytes=VMEM_BYTES),
        cost_estimate=pl.CostEstimate(
            flops=2 * levels * lat_dev * slots,
            bytes_accessed=6 * levels * lat_dev * slots,
            transcendentals=0,
        ),
    )(north, south)


def gate(blocks, after):
    anywhere = pl.BlockSpec(memory_space=pl.ANY)
    return pl.pallas_call(
        lambda *refs: None,
        in_specs=[anywhere] * (len(blocks) + len(after)),
        out_specs=[anywhere] * len(blocks),
        out_shape=like(blocks),
        input_output_aliases={i: i for i in range(len(blocks))},
        compiler_params=pltpu.CompilerParams(vmem_limit_bytes=VMEM_BYTES),
    )(*blocks, *after)


def unpack_body(near_ref, *refs, half):
    far_refs, out_ref, blocks_ref = refs[:half], refs[-2], refs[-1]
    _, group, lat_dev, slots = out_ref.shape
    take_blocks(near_ref, far_refs, blocks_ref)
    blocks = [blocks_ref[device].astype(jnp.float32) for device in range(2 * half)]
    rows = jnp.concatenate(blocks, axis=0).astype(jnp.bfloat16).T
    if lat_dev % 16:
        rows = rows.astype(jnp.float32)
    out_ref[0] = rows.reshape(group, lat_dev, slots).astype(jnp.bfloat16)


def unpack(part, parts, levels, lat_dev, received, earlier):
    half, slot_dev, _ = received[0].shape
    slots = 2 * half * slot_dev
    in_specs = block_specs(half, slot_dev, GROUP * lat_dev)
    operands = list(received)
    aliases = {}
    if earlier is not None:
        in_specs.append(pl.BlockSpec(memory_space=pl.ANY))
        aliases = {len(operands): 0}
        operands.append(earlier)
    return pl.pallas_call(
        functools.partial(unpack_body, half=half),
        grid=(pl.cdiv(levels, GROUP),),
        in_specs=in_specs,
        out_specs=pl.BlockSpec((1, GROUP, lat_dev, slots), lambda i: (part, i, 0, 0)),
        out_shape=jax.ShapeDtypeStruct((parts, levels, lat_dev, slots), jnp.bfloat16),
        scratch_shapes=[pltpu.VMEM((2 * half, slot_dev, GROUP * lat_dev), jnp.bfloat16)],
        input_output_aliases=aliases,
        compiler_params=pltpu.CompilerParams(vmem_limit_bytes=VMEM_BYTES),
        cost_estimate=pl.CostEstimate(
            flops=levels * lat_dev * slots,
            bytes_accessed=4 * levels * lat_dev * slots,
            transcendentals=0,
        ),
    )(*operands)


def lane_runs(lanes, source):
    runs = []
    for lane in range(LANES):
        where = source(lanes + lane)
        if where is None:
            continue
        tile = (where[0], where[1] // LANES)
        shift = (lane - where[1]) % LANES
        if runs and runs[-1][1:] == (tile, shift):
            runs[-1] = (lane + 1, tile, shift)
        else:
            runs.append((lane + 1, tile, shift))
    return runs


def merge_runs(runs, load, cache, lane_index):
    out = None
    for end, tile, shift in reversed(runs):
        if (tile, shift) not in cache:
            value = load(*tile)
            cache[tile, shift] = pltpu.roll(value, shift, 1) if shift else value
        value = cache[tile, shift]
        out = value if out is None else jnp.where(lane_index < end, value, out)
    return out


def group_size(lat_dev):
    return LANES // math.gcd(lat_dev, LANES)


def spread(recv_ref, rows_ref, first, group, lat_dev, slot_dev):
    lat_total = rows_ref.shape[0] * LANES
    base = pl.multiple_of(first * lat_dev, LANES)
    lane_index = lax.broadcasted_iota(jnp.int32, (slot_dev, LANES), 1)

    def load(device, tile):
        return recv_ref[device, :, pl.ds(base + tile * LANES, LANES)].astype(jnp.float32)

    cache = {}
    for lanes in range(0, lat_total, LANES):
        for i in range(group):
            runs = lane_runs(lanes, lambda j: (j // lat_dev, i * lat_dev + j % lat_dev))
            row = pl.multiple_of((first + i) * slot_dev, slot_dev)
            rows_ref[lanes // LANES, pl.ds(row, slot_dev), :] = merge_runs(
                runs, load, cache, lane_index
            )


def gather(rows_ref, send_ref, first, group, lat_dev, slot_dev):
    devices = rows_ref.shape[0] * LANES // lat_dev
    base = pl.multiple_of(first * lat_dev, LANES)
    lane_index = lax.broadcasted_iota(jnp.int32, (slot_dev, LANES), 1)
    cache = {}

    def load(i, tile):
        row = pl.multiple_of((first + i) * slot_dev, slot_dev)
        return rows_ref[tile, pl.ds(row, slot_dev), :]

    for device in range(devices):
        for lanes in range(0, group * lat_dev, LANES):
            runs = lane_runs(
                lanes,
                lambda l: (l // lat_dev, device * lat_dev + l % lat_dev)
                if l < group * lat_dev
                else None,
            )
            tile = merge_runs(runs, load, cache, lane_index).astype(jnp.bfloat16)
            send_ref[device, :, pl.ds(base + lanes, LANES)] = tile


def join_tiles(ref, rows):
    return jnp.concatenate([ref[tile, rows, :] for tile in range(ref.shape[0])], axis=1)


def split_tiles(ref, rows, value):
    for tile in range(ref.shape[0]):
        ref[tile, rows, :] = value[:, tile * LANES : (tile + 1) * LANES]


def all_groups(levels, lat_dev, body):
    group = group_size(lat_dev)
    full = levels // group

    @pl.loop(0, full)
    def _(g):
        body(g * group, group)

    if levels % group:
        body(full * group, levels % group)


def step_body(waves_ref, recv_ref, *refs, half, passed):
    recv_refs, refs = refs[:half], refs[half:]
    legendre_ref, counts_ref, rates_ref, to_ref, from_ref = refs[:5]
    outs = refs[len(refs) - 5 - half - passed :]
    state_ref, send_ref, send_refs = outs[0], outs[1], outs[2 : 2 + half]
    rows_ref, spec_ref, blocks_ref = refs[-3:]
    slot = pl.program_id(0)
    wave = waves_ref[slot]
    row_total, lat_total = legendre_ref.shape[1:]
    _, levels, slot_dev, _ = state_ref.shape
    lat_dev = lat_total // (2 * half)

    @pl.when(slot == 0)
    def _():
        take_blocks(recv_ref, recv_refs, blocks_ref)
        all_groups(
            levels, lat_dev, lambda c, n: spread(blocks_ref, rows_ref, c, n, lat_dev, slot_dev)
        )

    own = pl.ds(slot, levels, stride=slot_dev)
    matrix = legendre_ref[0]
    live = 2 * wave < counts_ref[...]
    direct = lax.dot_general(
        jnp.where(live, join_tiles(rows_ref, own), 0.0).astype(jnp.bfloat16),
        matrix,
        (((1,), (1,)), ((), ())),
        preferred_element_type=jnp.float32,
    ).astype(jnp.bfloat16)
    modal = jnp.dot(to_ref[...], direct, preferred_element_type=jnp.float32)
    degree = wave + 2 * lax.broadcasted_iota(jnp.int32, (1, row_total), 1)
    degree_f = degree.astype(jnp.float32)
    scaled_degree = degree_f * (degree_f + 1.0) / float(NMAX * (NMAX + 1))
    scaled = (modal / (1.0 + rates_ref[...] * scaled_degree)).astype(jnp.bfloat16)
    state = jnp.dot(from_ref[...], scaled, preferred_element_type=jnp.float32)
    state = jnp.where(degree <= NMAX, state, 0.0)
    split_tiles(spec_ref, own, state)
    rows = jnp.dot(state.astype(jnp.bfloat16), matrix, preferred_element_type=jnp.float32)
    split_tiles(rows_ref, own, jnp.where(live, rows, 0.0))

    @pl.when(slot == slot_dev - 1)
    def _():
        all_groups(
            levels, lat_dev, lambda c, n: gather(rows_ref, blocks_ref, c, n, lat_dev, slot_dev)
        )
        give_blocks(blocks_ref, send_ref, send_refs)

        @pl.loop(0, levels)
        def _(c):
            at = pl.multiple_of(c * slot_dev, slot_dev)
            state_ref[0, c] = join_tiles(spec_ref, pl.ds(at, slot_dev)).astype(jnp.bfloat16)


def spectral_step(part, parts, received, legendre, own_waves, counts, rates, to_t, from_t, earlier, waiting):
    half, _, width = received[0].shape
    slot_dev, row_total, lat_total = legendre.shape
    levels = to_t.shape[0]
    whole = lambda shape: pl.BlockSpec(shape, lambda s, waves: (0,) * len(shape))
    shapes = block_shapes(half, slot_dev, width)
    in_specs = [whole(shape.shape) for shape in shapes] + [
        pl.BlockSpec((1, row_total, lat_total), lambda s, waves: (s, 0, 0)),
        whole((1, lat_total)),
        whole((levels, 1)),
        whole((levels, levels)),
        whole((levels, levels)),
    ]
    operands = [own_waves, *received, legendre, counts, rates, to_t, from_t]
    anywhere = pl.BlockSpec(memory_space=pl.ANY)
    aliases = {}
    if earlier is not None:
        aliases[len(operands)] = 0
        operands.append(earlier)
        in_specs.append(anywhere)
    for i, block in enumerate(waiting):
        aliases[len(operands)] = 1 + len(shapes) + i
        operands.append(block)
        in_specs.append(anywhere)
    outs = pl.pallas_call(
        functools.partial(step_body, half=half, passed=len(waiting)),
        grid_spec=pltpu.PrefetchScalarGridSpec(
            num_scalar_prefetch=1,
            grid=(slot_dev,),
            in_specs=in_specs,
            out_specs=[
                pl.BlockSpec((1, levels, slot_dev, row_total), lambda s, waves: (part, 0, 0, 0)),
            ]
            + [whole(shape.shape) for shape in shapes]
            + [anywhere] * len(waiting),
            scratch_shapes=[
                pltpu.VMEM((lat_total // LANES, levels * slot_dev, LANES), jnp.float32),
                pltpu.VMEM((row_total // LANES, levels * slot_dev, LANES), jnp.float32),
                pltpu.VMEM((2 * half, slot_dev, width), jnp.bfloat16),
            ],
        ),
        out_shape=[
            jax.ShapeDtypeStruct((parts, levels, slot_dev, row_total), jnp.bfloat16),
            *shapes,
            *like(waiting),
        ],
        input_output_aliases=aliases,
        compiler_params=pltpu.CompilerParams(vmem_limit_bytes=VMEM_BYTES),
        cost_estimate=pl.CostEstimate(
            flops=16 * slot_dev * row_total * lat_total * levels,
            bytes_accessed=2 * slot_dev * lat_total * (row_total + 3 * levels),
            transcendentals=0,
        ),
    )(*operands)
    return outs[0], outs[1 : 1 + len(shapes)], outs[1 + len(shapes) :]


def exchange_near(block, half):
    groups = [list(range(half)), list(range(half, 2 * half))]
    return lax.all_to_all(
        block, "wave", split_axis=0, concat_axis=0, tiled=True, axis_index_groups=groups
    )


def exchange_far(block, half, turn):
    pairs = [
        (i, (half if i < half else 0) + (i % half + turn) % half) for i in range(2 * half)
    ]
    return lax.ppermute(block, "wave", pairs)


def per_device(
    north_rows, south_rows, lon_counts, slot_wave, legendre, mode_rates, to_modes, from_modes
):
    lat_dev, slots, channels = north_rows.shape
    slot_dev, row_total, lat_total = legendre.shape
    levels = to_modes.shape[0]
    parts = channels // levels
    my_index = lax.axis_index("wave")
    own_waves = lax.dynamic_slice_in_dim(slot_wave, my_index * slot_dev, slot_dev)
    north = jnp.transpose(north_rows, (2, 0, 1)).reshape(parts, levels, lat_dev, slots)
    south = jnp.transpose(south_rows, (2, 0, 1)).reshape(parts, levels, lat_dev, slots)
    half = slots // slot_dev // 2
    early = 1 + min(EARLY, half)
    send_far = lambda blocks: [
        exchange_far(block, half, turn) for turn, block in enumerate(blocks[1:])
    ]
    packed = [list(pack(part, half, north, south)) for part in range(parts)]
    far = send_far(packed[0])
    returned = []
    spec_state = None
    for part in range(parts):
        beside = packed[part + 1] if part + 1 < parts else (returned or [[]])[-1]
        if beside:
            beside[:early] = gate(beside[:early], far)
        arrived = [exchange_near(packed[part][0], half), *far]
        spec_state, blocks, beside[early:] = spectral_step(
            part, parts, arrived, legendre, own_waves, lon_counts[None, :],
            mode_rates[:, None], to_modes.T, from_modes.T, spec_state, beside[early:],
        )
        returned.append(list(blocks))
        if beside:
            far = send_far(beside)
    new_rows = None
    for part in range(parts):
        blocks = returned[part]
        if part or parts == 1:
            blocks = gate(blocks, far) if part else blocks
            far = send_far(blocks)
        new_rows = unpack(
            part, parts, levels, lat_dev, [exchange_near(blocks[0], half), *far], new_rows
        )
    new_rows = jnp.transpose(new_rows.reshape(channels, lat_dev, slots), (1, 2, 0))
    spec_state = jnp.transpose(spec_state.reshape(channels, slot_dev, row_total), (1, 2, 0))
    return (spec_state, new_rows)


def solution(mesh):
    in_specs = (
        P(("grp", "wave"), None, None),
        P(("grp", "wave"), None, None),
        P(),
        P(),
        P("wave", None, None),
        P(),
        P(),
        P(),
    )
    out_specs = (P(("grp", "wave"), None, None), P(("grp", "wave"), None, None))
    return jax.shard_map(
        per_device, mesh=mesh, in_specs=in_specs, out_specs=out_specs, check_vma=False
    )
```

```python
import functools
import math

import jax
import jax.numpy as jnp
from jax import lax
from jax.experimental import pallas as pl
from jax.experimental.pallas import tpu as pltpu
from jax.sharding import PartitionSpec as P

NMAX = 2559
VMEM_BYTES = 255 * 256 * 1024
GROUP = 48
LANES = 128
NEAR = 2


def flat_rows(value):
    group, lat_dev, slots = value.shape
    if lat_dev % 16:
        value = value.astype(jnp.float32)
    return value.reshape(group * lat_dev, slots).astype(jnp.bfloat16)


def take_blocks(in_refs, blocks_ref):
    partners = len(in_refs)
    if partners == 1:
        return in_refs[0]
    my_index = lax.axis_index("wave")
    for k in range(partners):
        blocks_ref[lax.rem(my_index + (partners - k), partners)] = in_refs[k][...]
    return blocks_ref


def give_blocks(blocks_ref, out_refs):
    partners = len(out_refs)
    if partners == 1:
        out_refs[0][...] = blocks_ref[...]
        return
    my_index = lax.axis_index("wave")
    for k in range(partners):
        out_refs[k][...] = blocks_ref[lax.rem(my_index + k, partners)]


def gate(blocks, after):
    if not after:
        return blocks
    anywhere = pl.BlockSpec(memory_space=pl.ANY)
    return pl.pallas_call(
        lambda *refs: None,
        in_specs=[anywhere] * (len(blocks) + len(after)),
        out_specs=[anywhere] * len(blocks),
        out_shape=[jax.ShapeDtypeStruct(block.shape, block.dtype) for block in blocks],
        input_output_aliases={i: i for i in range(len(blocks))},
        compiler_params=pltpu.CompilerParams(vmem_limit_bytes=VMEM_BYTES),
    )(*blocks, *after)


def block_shapes(ring, partners, slot_dev, width):
    if ring:
        return [jax.ShapeDtypeStruct((slot_dev, width), jnp.bfloat16)] * partners
    return [jax.ShapeDtypeStruct((partners, slot_dev, width), jnp.bfloat16)]


def block_specs(ring, partners, slot_dev, lanes):
    if ring:
        return [pl.BlockSpec((slot_dev, lanes), lambda i: (0, i))] * partners
    return [pl.BlockSpec((partners, slot_dev, lanes), lambda i: (0, 0, i))]


def pack_body(north_ref, south_ref, *refs, after):
    out_refs, blocks_ref = refs[after:-1], refs[-1]
    partners, slot_dev, _ = blocks_ref.shape
    summed = north_ref[0].astype(jnp.float32) + south_ref[0].astype(jnp.float32)
    columns = flat_rows(summed.astype(jnp.bfloat16)).T
    for device in range(partners):
        blocks_ref[device] = columns[device * slot_dev : (device + 1) * slot_dev]
    give_blocks(blocks_ref, out_refs)


def pack(part, ring, partners, north, south, after):
    _, levels, lat_dev, slots = north.shape
    slot_dev = slots // partners
    width = pl.cdiv(levels * lat_dev, LANES) * LANES
    rows = pl.BlockSpec((1, GROUP, lat_dev, slots), lambda i: (part, i, 0, 0))
    return pl.pallas_call(
        functools.partial(pack_body, after=len(after)),
        grid=(pl.cdiv(levels, GROUP),),
        in_specs=[rows, rows] + [pl.BlockSpec(memory_space=pl.ANY)] * len(after),
        out_specs=block_specs(ring, partners, slot_dev, GROUP * lat_dev),
        out_shape=block_shapes(ring, partners, slot_dev, width),
        scratch_shapes=[pltpu.VMEM((partners, slot_dev, GROUP * lat_dev), jnp.bfloat16)],
        compiler_params=pltpu.CompilerParams(vmem_limit_bytes=VMEM_BYTES),
        cost_estimate=pl.CostEstimate(
            flops=2 * levels * lat_dev * slots,
            bytes_accessed=6 * levels * lat_dev * slots,
            transcendentals=0,
        ),
    )(north, south, *after)


def unpack_body(*refs, arrays):
    out_ref, blocks_ref = refs[-2:]
    _, group, lat_dev, slots = out_ref.shape
    taken_ref = take_blocks(refs[:arrays], blocks_ref)
    blocks = [taken_ref[device].astype(jnp.float32) for device in range(blocks_ref.shape[0])]
    rows = jnp.concatenate(blocks, axis=0).astype(jnp.bfloat16).T
    if lat_dev % 16:
        rows = rows.astype(jnp.float32)
    out_ref[0] = rows.reshape(group, lat_dev, slots).astype(jnp.bfloat16)


def unpack(part, parts, levels, lat_dev, slots, received, earlier):
    slot_dev = received[0].shape[-2]
    partners = slots // slot_dev
    in_specs = block_specs(len(received) > 1, partners, slot_dev, GROUP * lat_dev)
    operands = list(received)
    aliases = {}
    if earlier is not None:
        in_specs.append(pl.BlockSpec(memory_space=pl.ANY))
        aliases = {len(operands): 0}
        operands.append(earlier)
    return pl.pallas_call(
        functools.partial(unpack_body, arrays=len(received)),
        grid=(pl.cdiv(levels, GROUP),),
        in_specs=in_specs,
        out_specs=pl.BlockSpec((1, GROUP, lat_dev, slots), lambda i: (part, i, 0, 0)),
        out_shape=jax.ShapeDtypeStruct((parts, levels, lat_dev, slots), jnp.bfloat16),
        scratch_shapes=[pltpu.VMEM((partners, slot_dev, GROUP * lat_dev), jnp.bfloat16)],
        input_output_aliases=aliases,
        compiler_params=pltpu.CompilerParams(vmem_limit_bytes=VMEM_BYTES),
        cost_estimate=pl.CostEstimate(
            flops=levels * lat_dev * slots,
            bytes_accessed=4 * levels * lat_dev * slots,
            transcendentals=0,
        ),
    )(*operands)


def lane_runs(lanes, source):
    runs = []
    for lane in range(LANES):
        where = source(lanes + lane)
        if where is None:
            continue
        tile = (where[0], where[1] // LANES)
        shift = (lane - where[1]) % LANES
        if runs and runs[-1][1:] == (tile, shift):
            runs[-1] = (lane + 1, tile, shift)
        else:
            runs.append((lane + 1, tile, shift))
    return runs


def merge_runs(runs, load, cache, lane_index):
    out = None
    for end, tile, shift in reversed(runs):
        if (tile, shift) not in cache:
            value = load(*tile)
            cache[tile, shift] = pltpu.roll(value, shift, 1) if shift else value
        value = cache[tile, shift]
        out = value if out is None else jnp.where(lane_index < end, value, out)
    return out


def group_size(lat_dev):
    return LANES // math.gcd(lat_dev, LANES)


def spread(recv_ref, rows_ref, first, group, lat_dev, slot_dev):
    lat_total = rows_ref.shape[0] * LANES
    base = pl.multiple_of(first * lat_dev, LANES)
    lane_index = lax.broadcasted_iota(jnp.int32, (slot_dev, LANES), 1)

    def load(device, tile):
        return recv_ref[device, :, pl.ds(base + tile * LANES, LANES)].astype(jnp.float32)

    cache = {}
    for lanes in range(0, lat_total, LANES):
        for i in range(group):
            runs = lane_runs(lanes, lambda j: (j // lat_dev, i * lat_dev + j % lat_dev))
            row = pl.multiple_of((first + i) * slot_dev, slot_dev)
            rows_ref[lanes // LANES, pl.ds(row, slot_dev), :] = merge_runs(
                runs, load, cache, lane_index
            )


def gather(rows_ref, send_ref, first, group, lat_dev, slot_dev):
    devices = rows_ref.shape[0] * LANES // lat_dev
    base = pl.multiple_of(first * lat_dev, LANES)
    lane_index = lax.broadcasted_iota(jnp.int32, (slot_dev, LANES), 1)
    cache = {}

    def load(i, tile):
        row = pl.multiple_of((first + i) * slot_dev, slot_dev)
        return rows_ref[tile, pl.ds(row, slot_dev), :]

    for device in range(devices):
        for lanes in range(0, group * lat_dev, LANES):
            runs = lane_runs(
                lanes,
                lambda l: (l // lat_dev, device * lat_dev + l % lat_dev)
                if l < group * lat_dev
                else None,
            )
            tile = merge_runs(runs, load, cache, lane_index).astype(jnp.bfloat16)
            send_ref[device, :, pl.ds(base + lanes, LANES)] = tile


def join_tiles(ref, rows):
    return jnp.concatenate([ref[tile, rows, :] for tile in range(ref.shape[0])], axis=1)


def split_tiles(ref, rows, value):
    for tile in range(ref.shape[0]):
        ref[tile, rows, :] = value[:, tile * LANES : (tile + 1) * LANES]


def all_groups(levels, lat_dev, body):
    group = group_size(lat_dev)
    full = levels // group

    @pl.loop(0, full)
    def _(g):
        body(g * group, group)

    if levels % group:
        body(full * group, levels % group)


def step_body(waves_ref, *refs, taken, given):
    recv_refs, refs = refs[:taken], refs[taken:]
    legendre_ref, counts_ref, rates_ref, to_ref, from_ref = refs[:5]
    rows_ref, spec_ref, blocks_ref = refs[-3:]
    state_ref, *send_refs = refs[-4 - given : -3]
    slot = pl.program_id(0)
    wave = waves_ref[slot]
    row_total, lat_total = legendre_ref.shape[1:]
    _, levels, slot_dev, _ = state_ref.shape
    lat_dev = lat_total // blocks_ref.shape[0]

    @pl.when(slot == 0)
    def _():
        recv_ref = take_blocks(recv_refs, blocks_ref)
        all_groups(
            levels, lat_dev, lambda c, n: spread(recv_ref, rows_ref, c, n, lat_dev, slot_dev)
        )

    own = pl.ds(slot, levels, stride=slot_dev)
    matrix = legendre_ref[0]
    live = 2 * wave < counts_ref[...]
    direct = lax.dot_general(
        jnp.where(live, join_tiles(rows_ref, own), 0.0).astype(jnp.bfloat16),
        matrix,
        (((1,), (1,)), ((), ())),
        preferred_element_type=jnp.float32,
    ).astype(jnp.bfloat16)
    modal = jnp.dot(to_ref[...], direct, preferred_element_type=jnp.float32)
    degree = wave + 2 * lax.broadcasted_iota(jnp.int32, (1, row_total), 1)
    degree_f = degree.astype(jnp.float32)
    scaled_degree = degree_f * (degree_f + 1.0) / float(NMAX * (NMAX + 1))
    scaled = (modal / (1.0 + rates_ref[...] * scaled_degree)).astype(jnp.bfloat16)
    state = jnp.dot(from_ref[...], scaled, preferred_element_type=jnp.float32)
    state = jnp.where(degree <= NMAX, state, 0.0)
    split_tiles(spec_ref, own, state)
    rows = jnp.dot(state.astype(jnp.bfloat16), matrix, preferred_element_type=jnp.float32)
    split_tiles(rows_ref, own, jnp.where(live, rows, 0.0))

    @pl.when(slot == slot_dev - 1)
    def _():
        send_ref = blocks_ref if given > 1 else send_refs[0]
        all_groups(
            levels, lat_dev, lambda c, n: gather(rows_ref, send_ref, c, n, lat_dev, slot_dev)
        )
        if given > 1:
            give_blocks(blocks_ref, send_refs)

        @pl.loop(0, levels)
        def _(c):
            at = pl.multiple_of(c * slot_dev, slot_dev)
            state_ref[0, c] = join_tiles(spec_ref, pl.ds(at, slot_dev)).astype(jnp.bfloat16)


def spectral_step(part, parts, ring, partners, received, legendre, own_waves, counts, rates, to_t, from_t, earlier):
    width = received[0].shape[-1]
    slot_dev, row_total, lat_total = legendre.shape
    levels = to_t.shape[0]
    whole = lambda shape: pl.BlockSpec(shape, lambda s, waves: (0,) * len(shape))
    shapes = block_shapes(ring, partners, slot_dev, width)
    in_specs = [whole(block.shape) for block in received] + [
        pl.BlockSpec((1, row_total, lat_total), lambda s, waves: (s, 0, 0)),
        whole((1, lat_total)),
        whole((levels, 1)),
        whole((levels, levels)),
        whole((levels, levels)),
    ]
    operands = [own_waves, *received, legendre, counts, rates, to_t, from_t]
    aliases = {}
    if earlier is not None:
        aliases[len(operands)] = 0
        operands.append(earlier)
        in_specs.append(pl.BlockSpec(memory_space=pl.ANY))
    state, *blocks = pl.pallas_call(
        functools.partial(step_body, taken=len(received), given=len(shapes)),
        grid_spec=pltpu.PrefetchScalarGridSpec(
            num_scalar_prefetch=1,
            grid=(slot_dev,),
            in_specs=in_specs,
            out_specs=[
                pl.BlockSpec((1, levels, slot_dev, row_total), lambda s, waves: (part, 0, 0, 0)),
            ]
            + [whole(shape.shape) for shape in shapes],
            scratch_shapes=[
                pltpu.VMEM((lat_total // LANES, levels * slot_dev, LANES), jnp.float32),
                pltpu.VMEM((row_total // LANES, levels * slot_dev, LANES), jnp.float32),
                pltpu.VMEM((partners, slot_dev, width), jnp.bfloat16),
            ],
        ),
        out_shape=[
            jax.ShapeDtypeStruct((parts, levels, slot_dev, row_total), jnp.bfloat16),
            *shapes,
        ],
        input_output_aliases=aliases,
        compiler_params=pltpu.CompilerParams(vmem_limit_bytes=VMEM_BYTES),
        cost_estimate=pl.CostEstimate(
            flops=16 * slot_dev * row_total * lat_total * levels,
            bytes_accessed=2 * slot_dev * lat_total * (row_total + 3 * levels),
            transcendentals=0,
        ),
    )(*operands)
    return state, blocks


def exchange(blocks):
    partners = len(blocks)
    if partners == 1:
        return [lax.all_to_all(blocks[0], "wave", split_axis=0, concat_axis=0, tiled=True)]
    received = list(blocks)
    for k in sorted(range(1, partners), key=lambda k: -min(k, partners - k)):
        pairs = [(i, (i + k) % partners) for i in range(partners)]
        received[k] = lax.ppermute(blocks[k], "wave", pairs)
    return received


def per_device(
    north_rows, south_rows, lon_counts, slot_wave, legendre, mode_rates, to_modes, from_modes
):
    lat_dev, slots, channels = north_rows.shape
    slot_dev, row_total, lat_total = legendre.shape
    levels = to_modes.shape[0]
    parts = channels // levels
    partners = slots // slot_dev
    my_index = lax.axis_index("wave")
    own_waves = lax.dynamic_slice_in_dim(slot_wave, my_index * slot_dev, slot_dev)
    north = jnp.transpose(north_rows, (2, 0, 1)).reshape(parts, levels, lat_dev, slots)
    south = jnp.transpose(south_rows, (2, 0, 1)).reshape(parts, levels, lat_dev, slots)
    columns = []
    for part in range(parts):
        before = columns[-1] if columns else []
        blocks = pack(part, part == 0, partners, north, south, before[partners // 2 :][:1])
        columns.append(exchange(gate(blocks, before[NEAR + 1 : partners - NEAR])))
    spec_state = None
    returned = []
    for part in range(parts):
        spec_state, blocks = spectral_step(
            part, parts, part == parts - 1, partners, columns[part], legendre, own_waves,
            lon_counts[None, :], mode_rates[:, None], to_modes.T, from_modes.T, spec_state,
        )
        returned.append(exchange(blocks))
    new_rows = None
    for part in range(parts):
        new_rows = unpack(part, parts, levels, lat_dev, slots, returned[part], new_rows)
    new_rows = jnp.transpose(new_rows.reshape(channels, lat_dev, slots), (1, 2, 0))
    spec_state = jnp.transpose(spec_state.reshape(channels, slot_dev, row_total), (1, 2, 0))
    return (spec_state, new_rows)


def solution(mesh):
    in_specs = (
        P(("grp", "wave"), None, None),
        P(("grp", "wave"), None, None),
        P(),
        P(),
        P("wave", None, None),
        P(),
        P(),
        P(),
    )
    out_specs = (P(("grp", "wave"), None, None), P(("grp", "wave"), None, None))
    return jax.shard_map(
        per_device, mesh=mesh, in_specs=in_specs, out_specs=out_specs, check_vma=False
    )
```

```python
import functools
import math

import jax
import jax.numpy as jnp
from jax import lax
from jax.experimental import pallas as pl
from jax.experimental.pallas import tpu as pltpu
from jax.sharding import PartitionSpec as P

NMAX = 2559
VMEM_BYTES = 255 * 256 * 1024
GROUP = 48
LANES = 128
EARLY = 5


def flat_rows(value):
    group, lat_dev, slots = value.shape
    if lat_dev % 16:
        value = value.astype(jnp.float32)
    return value.reshape(group * lat_dev, slots).astype(jnp.bfloat16)


def take_blocks(in_refs, blocks_ref):
    partners = len(in_refs)
    if partners == 1:
        return in_refs[0]
    my_index = lax.axis_index("wave")
    for k in range(partners):
        blocks_ref[lax.rem(my_index + (partners - k), partners)] = in_refs[k][...]
    return blocks_ref


def give_blocks(blocks_ref, out_refs):
    partners = len(out_refs)
    if partners == 1:
        out_refs[0][...] = blocks_ref[...]
        return
    my_index = lax.axis_index("wave")
    for k in range(partners):
        out_refs[k][...] = blocks_ref[lax.rem(my_index + k, partners)]


def like(blocks):
    return [jax.ShapeDtypeStruct(block.shape, block.dtype) for block in blocks]


def gate(blocks, after):
    if not after:
        return blocks
    anywhere = pl.BlockSpec(memory_space=pl.ANY)
    return pl.pallas_call(
        lambda *refs: None,
        in_specs=[anywhere] * (len(blocks) + len(after)),
        out_specs=[anywhere] * len(blocks),
        out_shape=like(blocks),
        input_output_aliases={i: i for i in range(len(blocks))},
        compiler_params=pltpu.CompilerParams(vmem_limit_bytes=VMEM_BYTES),
    )(*blocks, *after)


def block_shapes(ring, partners, slot_dev, width):
    if ring:
        return [jax.ShapeDtypeStruct((slot_dev, width), jnp.bfloat16)] * partners
    return [jax.ShapeDtypeStruct((partners, slot_dev, width), jnp.bfloat16)]


def block_specs(ring, partners, slot_dev, lanes):
    if ring:
        return [pl.BlockSpec((slot_dev, lanes), lambda i: (0, i))] * partners
    return [pl.BlockSpec((partners, slot_dev, lanes), lambda i: (0, 0, i))]


def pack_body(north_ref, south_ref, *refs):
    out_refs, blocks_ref = refs[:-1], refs[-1]
    partners, slot_dev, _ = blocks_ref.shape
    summed = north_ref[0].astype(jnp.float32) + south_ref[0].astype(jnp.float32)
    columns = flat_rows(summed.astype(jnp.bfloat16)).T
    for device in range(partners):
        blocks_ref[device] = columns[device * slot_dev : (device + 1) * slot_dev]
    give_blocks(blocks_ref, out_refs)


def pack(part, ring, partners, north, south):
    _, levels, lat_dev, slots = north.shape
    slot_dev = slots // partners
    width = pl.cdiv(levels * lat_dev, LANES) * LANES
    rows = pl.BlockSpec((1, GROUP, lat_dev, slots), lambda i: (part, i, 0, 0))
    return pl.pallas_call(
        pack_body,
        grid=(pl.cdiv(levels, GROUP),),
        in_specs=[rows, rows],
        out_specs=block_specs(ring, partners, slot_dev, GROUP * lat_dev),
        out_shape=block_shapes(ring, partners, slot_dev, width),
        scratch_shapes=[pltpu.VMEM((partners, slot_dev, GROUP * lat_dev), jnp.bfloat16)],
        compiler_params=pltpu.CompilerParams(vmem_limit_bytes=VMEM_BYTES),
        cost_estimate=pl.CostEstimate(
            flops=2 * levels * lat_dev * slots,
            bytes_accessed=6 * levels * lat_dev * slots,
            transcendentals=0,
        ),
    )(north, south)


def unpack_body(*refs, arrays, passed):
    out_ref, blocks_ref = refs[-2 - passed], refs[-1]
    _, group, lat_dev, slots = out_ref.shape
    taken_ref = take_blocks(refs[:arrays], blocks_ref)
    blocks = [taken_ref[device].astype(jnp.float32) for device in range(blocks_ref.shape[0])]
    rows = jnp.concatenate(blocks, axis=0).astype(jnp.bfloat16).T
    if lat_dev % 16:
        rows = rows.astype(jnp.float32)
    out_ref[0] = rows.reshape(group, lat_dev, slots).astype(jnp.bfloat16)


def unpack(part, parts, levels, lat_dev, slots, received, earlier, waiting):
    slot_dev = received[0].shape[-2]
    partners = slots // slot_dev
    in_specs = block_specs(len(received) > 1, partners, slot_dev, GROUP * lat_dev)
    operands = list(received)
    aliases = {}
    if earlier is not None:
        in_specs.append(pl.BlockSpec(memory_space=pl.ANY))
        aliases = {len(operands): 0}
        operands.append(earlier)
    anywhere = pl.BlockSpec(memory_space=pl.ANY)
    for i, block in enumerate(waiting):
        aliases[len(operands)] = 1 + i
        operands.append(block)
        in_specs.append(anywhere)
    rows, *waiting = pl.pallas_call(
        functools.partial(unpack_body, arrays=len(received), passed=len(waiting)),
        grid=(pl.cdiv(levels, GROUP),),
        in_specs=in_specs,
        out_specs=[pl.BlockSpec((1, GROUP, lat_dev, slots), lambda i: (part, i, 0, 0))]
        + [anywhere] * len(waiting),
        out_shape=[
            jax.ShapeDtypeStruct((parts, levels, lat_dev, slots), jnp.bfloat16),
            *like(waiting),
        ],
        scratch_shapes=[pltpu.VMEM((partners, slot_dev, GROUP * lat_dev), jnp.bfloat16)],
        input_output_aliases=aliases,
        compiler_params=pltpu.CompilerParams(vmem_limit_bytes=VMEM_BYTES),
        cost_estimate=pl.CostEstimate(
            flops=levels * lat_dev * slots,
            bytes_accessed=4 * levels * lat_dev * slots,
            transcendentals=0,
        ),
    )(*operands)
    return rows, waiting


def lane_runs(lanes, source):
    runs = []
    for lane in range(LANES):
        where = source(lanes + lane)
        if where is None:
            continue
        tile = (where[0], where[1] // LANES)
        shift = (lane - where[1]) % LANES
        if runs and runs[-1][1:] == (tile, shift):
            runs[-1] = (lane + 1, tile, shift)
        else:
            runs.append((lane + 1, tile, shift))
    return runs


def merge_runs(runs, load, cache, lane_index):
    out = None
    for end, tile, shift in reversed(runs):
        if (tile, shift) not in cache:
            value = load(*tile)
            cache[tile, shift] = pltpu.roll(value, shift, 1) if shift else value
        value = cache[tile, shift]
        out = value if out is None else jnp.where(lane_index < end, value, out)
    return out


def group_size(lat_dev):
    return LANES // math.gcd(lat_dev, LANES)


def spread(recv_ref, rows_ref, first, group, lat_dev, slot_dev):
    lat_total = rows_ref.shape[0] * LANES
    base = pl.multiple_of(first * lat_dev, LANES)
    lane_index = lax.broadcasted_iota(jnp.int32, (slot_dev, LANES), 1)

    def load(device, tile):
        return recv_ref[device, :, pl.ds(base + tile * LANES, LANES)].astype(jnp.float32)

    cache = {}
    for lanes in range(0, lat_total, LANES):
        for i in range(group):
            runs = lane_runs(lanes, lambda j: (j // lat_dev, i * lat_dev + j % lat_dev))
            row = pl.multiple_of((first + i) * slot_dev, slot_dev)
            rows_ref[lanes // LANES, pl.ds(row, slot_dev), :] = merge_runs(
                runs, load, cache, lane_index
            )


def gather(rows_ref, send_ref, first, group, lat_dev, slot_dev):
    devices = rows_ref.shape[0] * LANES // lat_dev
    base = pl.multiple_of(first * lat_dev, LANES)
    lane_index = lax.broadcasted_iota(jnp.int32, (slot_dev, LANES), 1)
    cache = {}

    def load(i, tile):
        row = pl.multiple_of((first + i) * slot_dev, slot_dev)
        return rows_ref[tile, pl.ds(row, slot_dev), :]

    for device in range(devices):
        for lanes in range(0, group * lat_dev, LANES):
            runs = lane_runs(
                lanes,
                lambda l: (l // lat_dev, device * lat_dev + l % lat_dev)
                if l < group * lat_dev
                else None,
            )
            tile = merge_runs(runs, load, cache, lane_index).astype(jnp.bfloat16)
            send_ref[device, :, pl.ds(base + lanes, LANES)] = tile


def join_tiles(ref, rows):
    return jnp.concatenate([ref[tile, rows, :] for tile in range(ref.shape[0])], axis=1)


def split_tiles(ref, rows, value):
    for tile in range(ref.shape[0]):
        ref[tile, rows, :] = value[:, tile * LANES : (tile + 1) * LANES]


def all_groups(levels, lat_dev, body):
    group = group_size(lat_dev)
    full = levels // group

    @pl.loop(0, full)
    def _(g):
        body(g * group, group)

    if levels % group:
        body(full * group, levels % group)


def step_body(waves_ref, *refs, taken, given, passed):
    recv_refs, refs = refs[:taken], refs[taken:]
    legendre_ref, counts_ref, rates_ref, to_ref, from_ref = refs[:5]
    rows_ref, spec_ref, blocks_ref = refs[-3:]
    state_ref, *send_refs = refs[len(refs) - 4 - given - passed :][: 1 + given]
    slot = pl.program_id(0)
    wave = waves_ref[slot]
    row_total, lat_total = legendre_ref.shape[1:]
    _, levels, slot_dev, _ = state_ref.shape
    lat_dev = lat_total // blocks_ref.shape[0]

    @pl.when(slot == 0)
    def _():
        recv_ref = take_blocks(recv_refs, blocks_ref)
        all_groups(
            levels, lat_dev, lambda c, n: spread(recv_ref, rows_ref, c, n, lat_dev, slot_dev)
        )

    own = pl.ds(slot, levels, stride=slot_dev)
    matrix = legendre_ref[0]
    live = 2 * wave < counts_ref[...]
    direct = lax.dot_general(
        jnp.where(live, join_tiles(rows_ref, own), 0.0).astype(jnp.bfloat16),
        matrix,
        (((1,), (1,)), ((), ())),
        preferred_element_type=jnp.float32,
    ).astype(jnp.bfloat16)
    modal = jnp.dot(to_ref[...], direct, preferred_element_type=jnp.float32)
    degree = wave + 2 * lax.broadcasted_iota(jnp.int32, (1, row_total), 1)
    degree_f = degree.astype(jnp.float32)
    scaled_degree = degree_f * (degree_f + 1.0) / float(NMAX * (NMAX + 1))
    scaled = (modal / (1.0 + rates_ref[...] * scaled_degree)).astype(jnp.bfloat16)
    state = jnp.dot(from_ref[...], scaled, preferred_element_type=jnp.float32)
    state = jnp.where(degree <= NMAX, state, 0.0)
    split_tiles(spec_ref, own, state)
    rows = jnp.dot(state.astype(jnp.bfloat16), matrix, preferred_element_type=jnp.float32)
    split_tiles(rows_ref, own, jnp.where(live, rows, 0.0))

    @pl.when(slot == slot_dev - 1)
    def _():
        send_ref = blocks_ref if given > 1 else send_refs[0]
        all_groups(
            levels, lat_dev, lambda c, n: gather(rows_ref, send_ref, c, n, lat_dev, slot_dev)
        )
        if given > 1:
            give_blocks(blocks_ref, send_refs)

        @pl.loop(0, levels)
        def _(c):
            at = pl.multiple_of(c * slot_dev, slot_dev)
            state_ref[0, c] = join_tiles(spec_ref, pl.ds(at, slot_dev)).astype(jnp.bfloat16)


def spectral_step(
    part, parts, ring, partners, received, legendre, own_waves, counts, rates, to_t, from_t, earlier, waiting
):
    width = received[0].shape[-1]
    slot_dev, row_total, lat_total = legendre.shape
    levels = to_t.shape[0]
    whole = lambda shape: pl.BlockSpec(shape, lambda s, waves: (0,) * len(shape))
    shapes = block_shapes(ring, partners, slot_dev, width)
    in_specs = [whole(block.shape) for block in received] + [
        pl.BlockSpec((1, row_total, lat_total), lambda s, waves: (s, 0, 0)),
        whole((1, lat_total)),
        whole((levels, 1)),
        whole((levels, levels)),
        whole((levels, levels)),
    ]
    operands = [own_waves, *received, legendre, counts, rates, to_t, from_t]
    aliases = {}
    if earlier is not None:
        aliases[len(operands)] = 0
        operands.append(earlier)
        in_specs.append(pl.BlockSpec(memory_space=pl.ANY))
    anywhere = pl.BlockSpec(memory_space=pl.ANY)
    for i, block in enumerate(waiting):
        aliases[len(operands)] = 1 + len(shapes) + i
        operands.append(block)
        in_specs.append(anywhere)
    state, *blocks = pl.pallas_call(
        functools.partial(step_body, taken=len(received), given=len(shapes), passed=len(waiting)),
        grid_spec=pltpu.PrefetchScalarGridSpec(
            num_scalar_prefetch=1,
            grid=(slot_dev,),
            in_specs=in_specs,
            out_specs=[
                pl.BlockSpec((1, levels, slot_dev, row_total), lambda s, waves: (part, 0, 0, 0)),
            ]
            + [whole(shape.shape) for shape in shapes]
            + [anywhere] * len(waiting),
            scratch_shapes=[
                pltpu.VMEM((lat_total // LANES, levels * slot_dev, LANES), jnp.float32),
                pltpu.VMEM((row_total // LANES, levels * slot_dev, LANES), jnp.float32),
                pltpu.VMEM((partners, slot_dev, width), jnp.bfloat16),
            ],
        ),
        out_shape=[
            jax.ShapeDtypeStruct((parts, levels, slot_dev, row_total), jnp.bfloat16),
            *shapes,
            *like(waiting),
        ],
        input_output_aliases=aliases,
        compiler_params=pltpu.CompilerParams(vmem_limit_bytes=VMEM_BYTES),
        cost_estimate=pl.CostEstimate(
            flops=16 * slot_dev * row_total * lat_total * levels,
            bytes_accessed=2 * slot_dev * lat_total * (row_total + 3 * levels),
            transcendentals=0,
        ),
    )(*operands)
    return state, blocks[: len(shapes)], blocks[len(shapes) :]


def far_first(partners):
    return sorted(range(1, partners), key=lambda k: -min(k, partners - k))


def exchange(blocks):
    partners = len(blocks)
    if partners == 1:
        return [lax.all_to_all(blocks[0], "wave", split_axis=0, concat_axis=0, tiled=True)]
    received = list(blocks)
    for k in far_first(partners):
        pairs = [(i, (i + k) % partners) for i in range(partners)]
        received[k] = lax.ppermute(blocks[k], "wave", pairs)
    return received


def per_device(
    north_rows, south_rows, lon_counts, slot_wave, legendre, mode_rates, to_modes, from_modes
):
    lat_dev, slots, channels = north_rows.shape
    slot_dev, row_total, lat_total = legendre.shape
    levels = to_modes.shape[0]
    parts = channels // levels
    partners = slots // slot_dev
    my_index = lax.axis_index("wave")
    own_waves = lax.dynamic_slice_in_dim(slot_wave, my_index * slot_dev, slot_dev)
    north = jnp.transpose(north_rows, (2, 0, 1)).reshape(parts, levels, lat_dev, slots)
    south = jnp.transpose(south_rows, (2, 0, 1)).reshape(parts, levels, lat_dev, slots)
    late = far_first(partners)[EARLY:]
    packed = [list(pack(part, part % 2 == 1, partners, north, south)) for part in range(parts)]
    returned = []
    spec_state = None
    arrived = []
    for part in range(parts):
        if part % 2 == 0:
            packed[part] = gate(packed[part], arrived)
        arrived = exchange(packed[part])
        beside = packed[part + 1] if part % 2 == 0 and part + 1 < parts else []
        waiting = [beside[k] for k in late] if beside else []
        spec_state, blocks, waiting = spectral_step(
            part, parts, part % 2 == 1, partners, arrived, legendre, own_waves,
            lon_counts[None, :], mode_rates[:, None], to_modes.T, from_modes.T, spec_state, waiting,
        )
        for k, block in zip(late, waiting):
            beside[k] = block
        returned.append(list(blocks))
    new_rows = None
    for part in range(parts):
        if part % 2 == 0:
            returned[part] = gate(returned[part], arrived)
        arrived = exchange(returned[part])
        beside = returned[part + 1] if part % 2 == 0 and part + 1 < parts else []
        waiting = [beside[k] for k in late] if beside else []
        new_rows, waiting = unpack(
            part, parts, levels, lat_dev, slots, arrived, new_rows, waiting
        )
        for k, block in zip(late, waiting):
            beside[k] = block
    new_rows = jnp.transpose(new_rows.reshape(channels, lat_dev, slots), (1, 2, 0))
    spec_state = jnp.transpose(spec_state.reshape(channels, slot_dev, row_total), (1, 2, 0))
    return (spec_state, new_rows)


def solution(mesh):
    in_specs = (
        P(("grp", "wave"), None, None),
        P(("grp", "wave"), None, None),
        P(),
        P(),
        P("wave", None, None),
        P(),
        P(),
        P(),
    )
    out_specs = (P(("grp", "wave"), None, None), P(("grp", "wave"), None, None))
    return jax.shard_map(
        per_device, mesh=mesh, in_specs=in_specs, out_specs=out_specs, check_vma=False
    )
```

```python
import functools
import math

import jax
import jax.numpy as jnp
from jax import lax
from jax.experimental import pallas as pl
from jax.experimental.pallas import tpu as pltpu
from jax.sharding import PartitionSpec as P

NMAX = 2559
VMEM_BYTES = 62 * 1024 * 1024
GROUPS = 3
LANES = 128


def flat_rows(value):
    group, lat_dev, slots = value.shape
    if lat_dev % 16:
        value = value.astype(jnp.float32)
    return value.reshape(group * lat_dev, slots).astype(jnp.bfloat16)


def pack_body(north_ref, south_ref, out_ref):
    out_ref[...] = flat_rows(north_ref[0] + south_ref[0]).T


def pack(part, north, south):
    _, levels, lat_dev, slots = north.shape
    group = GROUPS * group_size(lat_dev)
    rows = pl.BlockSpec((1, group, lat_dev, slots), lambda i: (part, i, 0, 0))
    return pl.pallas_call(
        pack_body,
        grid=(pl.cdiv(levels, group),),
        in_specs=[rows, rows],
        out_specs=pl.BlockSpec((slots, group * lat_dev), lambda i: (0, i)),
        out_shape=jax.ShapeDtypeStruct((slots, pl.cdiv(levels * lat_dev, LANES) * LANES), jnp.bfloat16),
        compiler_params=pltpu.CompilerParams(vmem_limit_bytes=VMEM_BYTES),
        cost_estimate=pl.CostEstimate(
            flops=2 * levels * lat_dev * slots,
            bytes_accessed=6 * levels * lat_dev * slots,
            transcendentals=0,
        ),
    )(north, south)


def unpack_body(in_ref, *refs):
    out_ref = refs[-1]
    _, group, lat_dev, slots = out_ref.shape
    rows = in_ref[...].T
    if lat_dev % 16:
        rows = rows.astype(jnp.float32)
    out_ref[0] = rows.reshape(group, lat_dev, slots).astype(jnp.bfloat16)


def unpack(part, parts, levels, lat_dev, received, earlier):
    slots = received.shape[0]
    group = GROUPS * group_size(lat_dev)
    in_specs = [pl.BlockSpec((slots, group * lat_dev), lambda i: (0, i))]
    operands = [received]
    aliases = {}
    if earlier is not None:
        in_specs.append(pl.BlockSpec(memory_space=pl.ANY))
        operands.append(earlier)
        aliases = {1: 0}
    return pl.pallas_call(
        unpack_body,
        grid=(pl.cdiv(levels, group),),
        in_specs=in_specs,
        out_specs=pl.BlockSpec((1, group, lat_dev, slots), lambda i: (part, i, 0, 0)),
        out_shape=jax.ShapeDtypeStruct((parts, levels, lat_dev, slots), jnp.bfloat16),
        input_output_aliases=aliases,
        compiler_params=pltpu.CompilerParams(vmem_limit_bytes=VMEM_BYTES),
        cost_estimate=pl.CostEstimate(
            flops=levels * lat_dev * slots,
            bytes_accessed=4 * levels * lat_dev * slots,
            transcendentals=0,
        ),
    )(*operands)


def lane_runs(lanes, source):
    runs = []
    for lane in range(LANES):
        where = source(lanes + lane)
        if where is None:
            continue
        tile = (where[0], where[1] // LANES)
        shift = (lane - where[1]) % LANES
        if runs and runs[-1][1:] == (tile, shift):
            runs[-1] = (lane + 1, tile, shift)
        else:
            runs.append((lane + 1, tile, shift))
    return runs


def merge_runs(runs, load, cache, lane_index):
    out = None
    for end, tile, shift in reversed(runs):
        if (tile, shift) not in cache:
            value = load(*tile)
            cache[tile, shift] = pltpu.roll(value, shift, 1) if shift else value
        value = cache[tile, shift]
        out = value if out is None else jnp.where(lane_index < end, value, out)
    return out


def group_size(lat_dev):
    return LANES // math.gcd(lat_dev, LANES)


def spread(recv_ref, rows_ref, first, group, lat_dev, slot_dev):
    lat_total = rows_ref.shape[0] * LANES
    base = pl.multiple_of(first * lat_dev, LANES)
    lane_index = lax.broadcasted_iota(jnp.int32, (slot_dev, LANES), 1)
    pairs = {}

    def load(device, tile):
        pair = device // 2
        if (pair, tile) not in pairs:
            pairs[pair, tile] = recv_ref[
                2 * pair * slot_dev : 2 * (pair + 1) * slot_dev, pl.ds(base + tile * LANES, LANES)
            ].astype(jnp.float32)
        at = (device % 2) * slot_dev
        return pairs[pair, tile][at : at + slot_dev]

    cache = {}
    for lanes in range(0, lat_total, LANES):
        for i in range(group):
            runs = lane_runs(lanes, lambda j: (j // lat_dev, i * lat_dev + j % lat_dev))
            row = pl.multiple_of((first + i) * slot_dev, slot_dev)
            rows_ref[lanes // LANES, pl.ds(row, slot_dev), :] = merge_runs(
                runs, load, cache, lane_index
            )


def gather(rows_ref, send_ref, first, group, lat_dev, slot_dev):
    devices = rows_ref.shape[0] * LANES // lat_dev
    base = pl.multiple_of(first * lat_dev, LANES)
    lane_index = lax.broadcasted_iota(jnp.int32, (slot_dev, LANES), 1)
    cache = {}

    def load(i, tile):
        row = pl.multiple_of((first + i) * slot_dev, slot_dev)
        return rows_ref[tile, pl.ds(row, slot_dev), :]

    for pair in range(devices // 2):
        for lanes in range(0, group * lat_dev, LANES):
            tiles = []
            for device in (2 * pair, 2 * pair + 1):
                runs = lane_runs(
                    lanes,
                    lambda l: (l // lat_dev, device * lat_dev + l % lat_dev)
                    if l < group * lat_dev
                    else None,
                )
                tiles.append(merge_runs(runs, load, cache, lane_index))
            send_ref[
                2 * pair * slot_dev : 2 * (pair + 1) * slot_dev, pl.ds(base + lanes, LANES)
            ] = jnp.concatenate(tiles, axis=0).astype(jnp.bfloat16)


def join_tiles(ref, rows):
    return jnp.concatenate([ref[tile, rows, :] for tile in range(ref.shape[0])], axis=1)


def split_tiles(ref, rows, value):
    for tile in range(ref.shape[0]):
        ref[tile, rows, :] = value[:, tile * LANES : (tile + 1) * LANES]


def all_groups(levels, lat_dev, body):
    group = group_size(lat_dev)
    full = levels // group

    @pl.loop(0, full)
    def _(g):
        body(g * group, group)

    if levels % group:
        body(full * group, levels % group)


def step_body(waves_ref, recv_ref, legendre_ref, counts_ref, rates_ref, to_ref, from_ref, *refs):
    state_ref, send_ref, rows_ref, spec_ref = refs[-4:]
    slot = pl.program_id(0)
    wave = waves_ref[slot]
    row_total, lat_total = legendre_ref.shape[1:]
    _, levels, slot_dev, _ = state_ref.shape
    lat_dev = lat_total // (recv_ref.shape[0] // slot_dev)

    @pl.when(slot == 0)
    def _():
        all_groups(
            levels, lat_dev, lambda c, n: spread(recv_ref, rows_ref, c, n, lat_dev, slot_dev)
        )

    own = pl.ds(slot, levels, stride=slot_dev)
    matrix = legendre_ref[0]
    live = 2 * wave < counts_ref[...]
    direct = lax.dot_general(
        jnp.where(live, join_tiles(rows_ref, own), 0.0).astype(jnp.bfloat16),
        matrix,
        (((1,), (1,)), ((), ())),
        preferred_element_type=jnp.float32,
    ).astype(jnp.bfloat16)
    modal = jnp.dot(to_ref[...], direct, preferred_element_type=jnp.float32)
    degree = wave + 2 * lax.broadcasted_iota(jnp.int32, (1, row_total), 1)
    degree_f = degree.astype(jnp.float32)
    scaled_degree = degree_f * (degree_f + 1.0) / float(NMAX * (NMAX + 1))
    scaled = (modal / (1.0 + rates_ref[...] * scaled_degree)).astype(jnp.bfloat16)
    state = jnp.dot(from_ref[...], scaled, preferred_element_type=jnp.float32)
    state = jnp.where(degree <= NMAX, state, 0.0)
    split_tiles(spec_ref, own, state)
    rows = jnp.dot(state.astype(jnp.bfloat16), matrix, preferred_element_type=jnp.float32)
    split_tiles(rows_ref, own, jnp.where(live, rows, 0.0))

    @pl.when(slot == slot_dev - 1)
    def _():
        all_groups(
            levels, lat_dev, lambda c, n: gather(rows_ref, send_ref, c, n, lat_dev, slot_dev)
        )

        @pl.loop(0, levels)
        def _(c):
            at = pl.multiple_of(c * slot_dev, slot_dev)
            state_ref[0, c] = join_tiles(spec_ref, pl.ds(at, slot_dev)).astype(jnp.bfloat16)


def spectral_step(part, parts, received, legendre, own_waves, counts, rates, to_t, from_t, earlier):
    slots, width = received.shape
    slot_dev, row_total, lat_total = legendre.shape
    levels = to_t.shape[0]
    whole = lambda shape: pl.BlockSpec(shape, lambda s, waves: (0,) * len(shape))
    in_specs = [
        whole((slots, width)),
        pl.BlockSpec((1, row_total, lat_total), lambda s, waves: (s, 0, 0)),
        whole((1, lat_total)),
        whole((levels, 1)),
        whole((levels, levels)),
        whole((levels, levels)),
    ]
    operands = [own_waves, received, legendre, counts, rates, to_t, from_t]
    aliases = {}
    if earlier is not None:
        in_specs.append(pl.BlockSpec(memory_space=pl.ANY))
        aliases = {len(operands): 0}
        operands.append(earlier)
    return pl.pallas_call(
        step_body,
        grid_spec=pltpu.PrefetchScalarGridSpec(
            num_scalar_prefetch=1,
            grid=(slot_dev,),
            in_specs=in_specs,
            out_specs=[
                pl.BlockSpec((1, levels, slot_dev, row_total), lambda s, waves: (part, 0, 0, 0)),
                whole((slots, width)),
            ],
            scratch_shapes=[
                pltpu.VMEM((lat_total // LANES, levels * slot_dev, LANES), jnp.float32),
                pltpu.VMEM((row_total // LANES, levels * slot_dev, LANES), jnp.float32),
            ],
        ),
        out_shape=[
            jax.ShapeDtypeStruct((parts, levels, slot_dev, row_total), jnp.bfloat16),
            jax.ShapeDtypeStruct((slots, width), jnp.bfloat16),
        ],
        input_output_aliases=aliases,
        compiler_params=pltpu.CompilerParams(vmem_limit_bytes=VMEM_BYTES),
        cost_estimate=pl.CostEstimate(
            flops=4 * slot_dev * row_total * lat_total * levels,
            bytes_accessed=2 * slot_dev * lat_total * (row_total + 3 * levels),
            transcendentals=0,
        ),
    )(*operands)


def per_device(
    north_rows, south_rows, lon_counts, slot_wave, legendre, mode_rates, to_modes, from_modes
):
    lat_dev, slots, channels = north_rows.shape
    slot_dev, row_total, lat_total = legendre.shape
    levels = to_modes.shape[0]
    parts = channels // levels
    my_index = lax.axis_index("wave")
    own_waves = lax.dynamic_slice_in_dim(slot_wave, my_index * slot_dev, slot_dev)
    north = jnp.transpose(north_rows, (2, 0, 1)).reshape(parts, levels, lat_dev, slots)
    south = jnp.transpose(south_rows, (2, 0, 1)).reshape(parts, levels, lat_dev, slots)
    exchange = functools.partial(
        lax.all_to_all, axis_name="wave", split_axis=0, concat_axis=0, tiled=True
    )
    columns = [exchange(pack(part, north, south)) for part in range(parts)]
    spec_state = None
    returned = []
    for part in range(parts):
        spec_state, rows = spectral_step(
            part, parts, columns[part], legendre, own_waves, lon_counts[None, :],
            mode_rates[:, None], to_modes.T, from_modes.T, spec_state,
        )
        returned.append(exchange(rows))
    new_rows = None
    for part in range(parts):
        new_rows = unpack(part, parts, levels, lat_dev, returned[part], new_rows)
    new_rows = jnp.transpose(new_rows.reshape(channels, lat_dev, slots), (1, 2, 0))
    spec_state = jnp.transpose(spec_state.reshape(channels, slot_dev, row_total), (1, 2, 0))
    return (spec_state, new_rows)


def solution(mesh):
    in_specs = (
        P(("grp", "wave"), None, None),
        P(("grp", "wave"), None, None),
        P(),
        P(),
        P("wave", None, None),
        P(),
        P(),
        P(),
    )
    out_specs = (P(("grp", "wave"), None, None), P(("grp", "wave"), None, None))
    return jax.shard_map(
        per_device, mesh=mesh, in_specs=in_specs, out_specs=out_specs, check_vma=False
    )
```

```python
import functools
import math

import jax
import jax.numpy as jnp
from jax import lax
from jax.experimental import pallas as pl
from jax.experimental.pallas import tpu as pltpu
from jax.sharding import PartitionSpec as P

NMAX = 2559
VMEM_BYTES = 62 * 1024 * 1024
GROUPS = 2
LANES = 128


def flat_rows(value):
    group, lat_dev, slots = value.shape
    if lat_dev % 16:
        value = value.astype(jnp.float32)
    return value.reshape(group * lat_dev, slots).astype(jnp.bfloat16)


def pieces(levels, lat_dev, width):
    group = GROUPS * group_size(lat_dev)
    out = []
    for first in range(0, levels, group):
        lane = first * lat_dev
        count = min(group, levels - first)
        out.append((first, count, lane, min(group * lat_dev, width - lane)))
    return out


def pack_body(north_ref, south_ref, out_ref, north_buf, south_buf, out_buf, in_sems, out_sems, *, part):
    _, levels, lat_dev, slots = north_ref.shape
    cut = pieces(levels, lat_dev, out_ref.shape[1])
    group = cut[0][1]
    loads, stores = [], []
    for i, (first, count, _, _) in enumerate(cut):
        some = pl.ds(first, count)
        loads.append(
            [
                pltpu.make_async_copy(ref.at[part, some], buf.at[some], in_sems.at[j, i])
                for j, (ref, buf) in enumerate([(north_ref, north_buf), (south_ref, south_buf)])
            ]
        )
        for load in loads[-1]:
            load.start()
    for buf in (north_buf, south_buf):
        if buf.shape[0] > levels:
            buf[levels:] = jnp.zeros((buf.shape[0] - levels, lat_dev, slots), buf.dtype)
    for i, (first, _, lane, lanes) in enumerate(cut):
        for load in loads[i]:
            load.wait()
        summed = north_buf[first : first + group] + south_buf[first : first + group]
        out_buf[:, lane : lane + lanes] = flat_rows(summed).T[:, :lanes]
        some = pl.ds(lane, lanes)
        stores.append(pltpu.make_async_copy(out_buf.at[:, some], out_ref.at[:, some], out_sems.at[i]))
        stores[-1].start()
    for store in stores:
        store.wait()


def pack(part, north, south):
    _, levels, lat_dev, slots = north.shape
    width = pl.cdiv(levels * lat_dev, LANES) * LANES
    cut = pieces(levels, lat_dev, width)
    anywhere = pl.BlockSpec(memory_space=pl.ANY)
    rows = pltpu.VMEM((len(cut) * cut[0][1], lat_dev, slots), jnp.bfloat16)
    return pl.pallas_call(
        functools.partial(pack_body, part=part),
        in_specs=[anywhere, anywhere],
        out_specs=anywhere,
        out_shape=jax.ShapeDtypeStruct((slots, width), jnp.bfloat16),
        scratch_shapes=[
            rows,
            rows,
            pltpu.VMEM((slots, width), jnp.bfloat16),
            pltpu.SemaphoreType.DMA((2, len(cut))),
            pltpu.SemaphoreType.DMA((len(cut),)),
        ],
        compiler_params=pltpu.CompilerParams(vmem_limit_bytes=VMEM_BYTES),
        cost_estimate=pl.CostEstimate(
            flops=2 * levels * lat_dev * slots,
            bytes_accessed=6 * levels * lat_dev * slots,
            transcendentals=0,
        ),
    )(north, south)


def unpack_body(in_ref, *refs, part):
    out_ref, in_buf, out_buf, in_sems, out_sems = refs[-5:]
    levels, lat_dev, slots = out_buf.shape
    cut = pieces(levels, lat_dev, in_ref.shape[1])
    loads, stores = [], []
    for i, (_, _, lane, lanes) in enumerate(cut):
        some = pl.ds(lane, lanes)
        loads.append(pltpu.make_async_copy(in_ref.at[:, some], in_buf.at[:, some], in_sems.at[i]))
        loads[-1].start()
    for i, (first, count, lane, lanes) in enumerate(cut):
        loads[i].wait()
        rows = in_buf[:, lane : lane + lanes].T
        if lat_dev % 16:
            rows = rows.astype(jnp.float32)
        rows = rows[: count * lat_dev].reshape(count, lat_dev, slots)
        out_buf[first : first + count] = rows.astype(jnp.bfloat16)
        some = pl.ds(first, count)
        stores.append(pltpu.make_async_copy(out_buf.at[some], out_ref.at[part, some], out_sems.at[i]))
        stores[-1].start()
    for store in stores:
        store.wait()


def unpack(part, parts, levels, lat_dev, received, earlier):
    slots, width = received.shape
    cut = pieces(levels, lat_dev, width)
    anywhere = pl.BlockSpec(memory_space=pl.ANY)
    operands = [received] if earlier is None else [received, earlier]
    return pl.pallas_call(
        functools.partial(unpack_body, part=part),
        in_specs=[anywhere] * len(operands),
        out_specs=anywhere,
        out_shape=jax.ShapeDtypeStruct((parts, levels, lat_dev, slots), jnp.bfloat16),
        input_output_aliases={} if earlier is None else {1: 0},
        scratch_shapes=[
            pltpu.VMEM((slots, width), jnp.bfloat16),
            pltpu.VMEM((levels, lat_dev, slots), jnp.bfloat16),
            pltpu.SemaphoreType.DMA((len(cut),)),
            pltpu.SemaphoreType.DMA((len(cut),)),
        ],
        compiler_params=pltpu.CompilerParams(vmem_limit_bytes=VMEM_BYTES),
        cost_estimate=pl.CostEstimate(
            flops=levels * lat_dev * slots,
            bytes_accessed=4 * levels * lat_dev * slots,
            transcendentals=0,
        ),
    )(*operands)


def lane_runs(lanes, source):
    runs = []
    for lane in range(LANES):
        where = source(lanes + lane)
        if where is None:
            continue
        tile = (where[0], where[1] // LANES)
        shift = (lane - where[1]) % LANES
        if runs and runs[-1][1:] == (tile, shift):
            runs[-1] = (lane + 1, tile, shift)
        else:
            runs.append((lane + 1, tile, shift))
    return runs


def merge_runs(runs, load, cache, lane_index):
    out = None
    for end, tile, shift in reversed(runs):
        if (tile, shift) not in cache:
            value = load(*tile)
            cache[tile, shift] = pltpu.roll(value, shift, 1) if shift else value
        value = cache[tile, shift]
        out = value if out is None else jnp.where(lane_index < end, value, out)
    return out


def group_size(lat_dev):
    return LANES // math.gcd(lat_dev, LANES)


def spread(recv_ref, rows_ref, first, group, lat_dev, slot_dev):
    lat_total = rows_ref.shape[0] * LANES
    base = pl.multiple_of(first * lat_dev, LANES)
    lane_index = lax.broadcasted_iota(jnp.int32, (slot_dev, LANES), 1)
    pairs = {}

    def load(device, tile):
        pair = device // 2
        if (pair, tile) not in pairs:
            pairs[pair, tile] = recv_ref[
                2 * pair * slot_dev : 2 * (pair + 1) * slot_dev, pl.ds(base + tile * LANES, LANES)
            ].astype(jnp.float32)
        at = (device % 2) * slot_dev
        return pairs[pair, tile][at : at + slot_dev]

    cache = {}
    for lanes in range(0, lat_total, LANES):
        for i in range(group):
            runs = lane_runs(lanes, lambda j: (j // lat_dev, i * lat_dev + j % lat_dev))
            row = pl.multiple_of((first + i) * slot_dev, slot_dev)
            rows_ref[lanes // LANES, pl.ds(row, slot_dev), :] = merge_runs(
                runs, load, cache, lane_index
            )


def gather(rows_ref, send_ref, first, group, lat_dev, slot_dev):
    devices = rows_ref.shape[0] * LANES // lat_dev
    base = pl.multiple_of(first * lat_dev, LANES)
    lane_index = lax.broadcasted_iota(jnp.int32, (slot_dev, LANES), 1)
    cache = {}

    def load(i, tile):
        row = pl.multiple_of((first + i) * slot_dev, slot_dev)
        return rows_ref[tile, pl.ds(row, slot_dev), :]

    for pair in range(devices // 2):
        for lanes in range(0, group * lat_dev, LANES):
            tiles = []
            for device in (2 * pair, 2 * pair + 1):
                runs = lane_runs(
                    lanes,
                    lambda l: (l // lat_dev, device * lat_dev + l % lat_dev)
                    if l < group * lat_dev
                    else None,
                )
                tiles.append(merge_runs(runs, load, cache, lane_index))
            send_ref[
                2 * pair * slot_dev : 2 * (pair + 1) * slot_dev, pl.ds(base + lanes, LANES)
            ] = jnp.concatenate(tiles, axis=0).astype(jnp.bfloat16)


def join_tiles(ref, rows):
    return jnp.concatenate([ref[tile, rows, :] for tile in range(ref.shape[0])], axis=1)


def split_tiles(ref, rows, value):
    for tile in range(ref.shape[0]):
        ref[tile, rows, :] = value[:, tile * LANES : (tile + 1) * LANES]


def all_groups(levels, lat_dev, body):
    group = group_size(lat_dev)
    full = levels // group

    @pl.loop(0, full)
    def _(g):
        body(g * group, group)

    if levels % group:
        body(full * group, levels % group)


def step_body(waves_ref, recv_ref, legendre_ref, counts_ref, rates_ref, to_ref, from_ref, *refs):
    state_ref, send_ref, rows_ref, spec_ref = refs[-4:]
    slot = pl.program_id(0)
    wave = waves_ref[slot]
    row_total, lat_total = legendre_ref.shape[1:]
    _, levels, slot_dev, _ = state_ref.shape
    lat_dev = lat_total // (recv_ref.shape[0] // slot_dev)

    @pl.when(slot == 0)
    def _():
        all_groups(
            levels, lat_dev, lambda c, n: spread(recv_ref, rows_ref, c, n, lat_dev, slot_dev)
        )

    own = pl.ds(slot, levels, stride=slot_dev)
    matrix = legendre_ref[0]
    live = 2 * wave < counts_ref[...]
    direct = lax.dot_general(
        jnp.where(live, join_tiles(rows_ref, own), 0.0).astype(jnp.bfloat16),
        matrix,
        (((1,), (1,)), ((), ())),
        preferred_element_type=jnp.float32,
    ).astype(jnp.bfloat16)
    modal = jnp.dot(to_ref[...], direct, preferred_element_type=jnp.float32)
    degree = wave + 2 * lax.broadcasted_iota(jnp.int32, (1, row_total), 1)
    degree_f = degree.astype(jnp.float32)
    scaled_degree = degree_f * (degree_f + 1.0) / float(NMAX * (NMAX + 1))
    scaled = (modal / (1.0 + rates_ref[...] * scaled_degree)).astype(jnp.bfloat16)
    state = jnp.dot(from_ref[...], scaled, preferred_element_type=jnp.float32)
    state = jnp.where(degree <= NMAX, state, 0.0)
    split_tiles(spec_ref, own, state)
    rows = jnp.dot(state.astype(jnp.bfloat16), matrix, preferred_element_type=jnp.float32)
    split_tiles(rows_ref, own, jnp.where(live, rows, 0.0))

    @pl.when(slot == slot_dev - 1)
    def _():
        all_groups(
            levels, lat_dev, lambda c, n: gather(rows_ref, send_ref, c, n, lat_dev, slot_dev)
        )

        @pl.loop(0, levels)
        def _(c):
            at = pl.multiple_of(c * slot_dev, slot_dev)
            state_ref[0, c] = join_tiles(spec_ref, pl.ds(at, slot_dev)).astype(jnp.bfloat16)


def spectral_step(part, parts, received, legendre, own_waves, counts, rates, to_t, from_t, earlier):
    slots, width = received.shape
    slot_dev, row_total, lat_total = legendre.shape
    levels = to_t.shape[0]
    whole = lambda shape: pl.BlockSpec(shape, lambda s, waves: (0,) * len(shape))
    in_specs = [
        whole((slots, width)),
        pl.BlockSpec((1, row_total, lat_total), lambda s, waves: (s, 0, 0)),
        whole((1, lat_total)),
        whole((levels, 1)),
        whole((levels, levels)),
        whole((levels, levels)),
    ]
    operands = [own_waves, received, legendre, counts, rates, to_t, from_t]
    aliases = {}
    if earlier is not None:
        in_specs.append(pl.BlockSpec(memory_space=pl.ANY))
        aliases = {len(operands): 0}
        operands.append(earlier)
    return pl.pallas_call(
        step_body,
        grid_spec=pltpu.PrefetchScalarGridSpec(
            num_scalar_prefetch=1,
            grid=(slot_dev,),
            in_specs=in_specs,
            out_specs=[
                pl.BlockSpec((1, levels, slot_dev, row_total), lambda s, waves: (part, 0, 0, 0)),
                whole((slots, width)),
            ],
            scratch_shapes=[
                pltpu.VMEM((lat_total // LANES, levels * slot_dev, LANES), jnp.float32),
                pltpu.VMEM((row_total // LANES, levels * slot_dev, LANES), jnp.float32),
            ],
        ),
        out_shape=[
            jax.ShapeDtypeStruct((parts, levels, slot_dev, row_total), jnp.bfloat16),
            jax.ShapeDtypeStruct((slots, width), jnp.bfloat16),
        ],
        input_output_aliases=aliases,
        compiler_params=pltpu.CompilerParams(vmem_limit_bytes=VMEM_BYTES),
        cost_estimate=pl.CostEstimate(
            flops=4 * slot_dev * row_total * lat_total * levels,
            bytes_accessed=2 * slot_dev * lat_total * (row_total + 3 * levels),
            transcendentals=0,
        ),
    )(*operands)


def per_device(
    north_rows, south_rows, lon_counts, slot_wave, legendre, mode_rates, to_modes, from_modes
):
    lat_dev, slots, channels = north_rows.shape
    slot_dev, row_total, lat_total = legendre.shape
    levels = to_modes.shape[0]
    parts = channels // levels
    my_index = lax.axis_index("wave")
    own_waves = lax.dynamic_slice_in_dim(slot_wave, my_index * slot_dev, slot_dev)
    north = jnp.transpose(north_rows, (2, 0, 1)).reshape(parts, levels, lat_dev, slots)
    south = jnp.transpose(south_rows, (2, 0, 1)).reshape(parts, levels, lat_dev, slots)
    exchange = functools.partial(
        lax.all_to_all, axis_name="wave", split_axis=0, concat_axis=0, tiled=True
    )
    columns = [exchange(pack(part, north, south)) for part in range(parts)]
    spec_state = None
    returned = []
    for part in range(parts):
        spec_state, rows = spectral_step(
            part, parts, columns[part], legendre, own_waves, lon_counts[None, :],
            mode_rates[:, None], to_modes.T, from_modes.T, spec_state,
        )
        returned.append(exchange(rows))
    new_rows = None
    for part in range(parts):
        new_rows = unpack(part, parts, levels, lat_dev, returned[part], new_rows)
    new_rows = jnp.transpose(new_rows.reshape(channels, lat_dev, slots), (1, 2, 0))
    spec_state = jnp.transpose(spec_state.reshape(channels, slot_dev, row_total), (1, 2, 0))
    return (spec_state, new_rows)


def solution(mesh):
    in_specs = (
        P(("grp", "wave"), None, None),
        P(("grp", "wave"), None, None),
        P(),
        P(),
        P("wave", None, None),
        P(),
        P(),
        P(),
    )
    out_specs = (P(("grp", "wave"), None, None), P(("grp", "wave"), None, None))
    return jax.shard_map(
        per_device, mesh=mesh, in_specs=in_specs, out_specs=out_specs, check_vma=False
    )
```

```python
import functools
import math

import jax
import jax.numpy as jnp
from jax import lax
from jax.experimental import pallas as pl
from jax.experimental.pallas import tpu as pltpu
from jax.sharding import PartitionSpec as P

NMAX = 2559
VMEM_BYTES = 62 * 1024 * 1024
GROUPS = 2
AHEAD = 3
LANES = 128


def flat_rows(value):
    group, lat_dev, slots = value.shape
    if lat_dev % 16:
        value = value.astype(jnp.float32)
    return value.reshape(group * lat_dev, slots).astype(jnp.bfloat16)


def pieces(levels, lat_dev, width):
    group = GROUPS * group_size(lat_dev)
    out = []
    for first in range(0, levels, group):
        lane = first * lat_dev
        count = min(group, levels - first)
        out.append((first, count, lane, min(group * lat_dev, width - lane)))
    return out


def pack_body(north_ref, south_ref, out_ref, north_buf, south_buf, out_buf, in_sems, out_sems, *, part):
    _, levels, lat_dev, slots = north_ref.shape
    cut = pieces(levels, lat_dev, out_ref.shape[1])
    group = cut[0][1]
    loads, stores = [], []
    for i, (first, count, _, _) in enumerate(cut):
        some = pl.ds(first, count)
        loads.append(
            [
                pltpu.make_async_copy(ref.at[part, some], buf.at[some], in_sems.at[j, i])
                for j, (ref, buf) in enumerate([(north_ref, north_buf), (south_ref, south_buf)])
            ]
        )
    for load in sum(loads[:AHEAD], []):
        load.start()
    for buf in (north_buf, south_buf):
        if buf.shape[0] > levels:
            buf[levels:] = jnp.zeros((buf.shape[0] - levels, lat_dev, slots), buf.dtype)
    for i, (first, _, lane, lanes) in enumerate(cut):
        for load in loads[i]:
            load.wait()
        for load in sum(loads[i + AHEAD : i + AHEAD + 1], []):
            load.start()
        summed = north_buf[first : first + group] + south_buf[first : first + group]
        out_buf[:, lane : lane + lanes] = flat_rows(summed).T[:, :lanes]
        some = pl.ds(lane, lanes)
        stores.append(pltpu.make_async_copy(out_buf.at[:, some], out_ref.at[:, some], out_sems.at[i]))
        stores[-1].start()
    for store in stores:
        store.wait()


def pack(part, north, south):
    _, levels, lat_dev, slots = north.shape
    width = pl.cdiv(levels * lat_dev, LANES) * LANES
    cut = pieces(levels, lat_dev, width)
    anywhere = pl.BlockSpec(memory_space=pl.ANY)
    rows = pltpu.VMEM((len(cut) * cut[0][1], lat_dev, slots), jnp.bfloat16)
    return pl.pallas_call(
        functools.partial(pack_body, part=part),
        in_specs=[anywhere, anywhere],
        out_specs=anywhere,
        out_shape=jax.ShapeDtypeStruct((slots, width), jnp.bfloat16),
        scratch_shapes=[
            rows,
            rows,
            pltpu.VMEM((slots, width), jnp.bfloat16),
            pltpu.SemaphoreType.DMA((2, len(cut))),
            pltpu.SemaphoreType.DMA((len(cut),)),
        ],
        compiler_params=pltpu.CompilerParams(vmem_limit_bytes=VMEM_BYTES),
        cost_estimate=pl.CostEstimate(
            flops=2 * levels * lat_dev * slots,
            bytes_accessed=6 * levels * lat_dev * slots,
            transcendentals=0,
        ),
    )(north, south)


def unpack_body(in_ref, *refs, part):
    out_ref, in_buf, out_buf, in_sems, out_sems = refs[-5:]
    levels, lat_dev, slots = out_buf.shape
    cut = pieces(levels, lat_dev, in_ref.shape[1])
    loads, stores = [], []
    for i, (_, _, lane, lanes) in enumerate(cut):
        some = pl.ds(lane, lanes)
        loads.append(pltpu.make_async_copy(in_ref.at[:, some], in_buf.at[:, some], in_sems.at[i]))
    for load in loads[:AHEAD]:
        load.start()
    for i, (first, count, lane, lanes) in enumerate(cut):
        loads[i].wait()
        for load in loads[i + AHEAD : i + AHEAD + 1]:
            load.start()
        rows = in_buf[:, lane : lane + lanes].T
        if lat_dev % 16:
            rows = rows.astype(jnp.float32)
        rows = rows[: count * lat_dev].reshape(count, lat_dev, slots)
        out_buf[first : first + count] = rows.astype(jnp.bfloat16)
        some = pl.ds(first, count)
        stores.append(pltpu.make_async_copy(out_buf.at[some], out_ref.at[part, some], out_sems.at[i]))
        stores[-1].start()
    for store in stores:
        store.wait()


def unpack(part, parts, levels, lat_dev, received, earlier):
    slots, width = received.shape
    cut = pieces(levels, lat_dev, width)
    anywhere = pl.BlockSpec(memory_space=pl.ANY)
    operands = [received] if earlier is None else [received, earlier]
    return pl.pallas_call(
        functools.partial(unpack_body, part=part),
        in_specs=[anywhere] * len(operands),
        out_specs=anywhere,
        out_shape=jax.ShapeDtypeStruct((parts, levels, lat_dev, slots), jnp.bfloat16),
        input_output_aliases={} if earlier is None else {1: 0},
        scratch_shapes=[
            pltpu.VMEM((slots, width), jnp.bfloat16),
            pltpu.VMEM((levels, lat_dev, slots), jnp.bfloat16),
            pltpu.SemaphoreType.DMA((len(cut),)),
            pltpu.SemaphoreType.DMA((len(cut),)),
        ],
        compiler_params=pltpu.CompilerParams(vmem_limit_bytes=VMEM_BYTES),
        cost_estimate=pl.CostEstimate(
            flops=levels * lat_dev * slots,
            bytes_accessed=4 * levels * lat_dev * slots,
            transcendentals=0,
        ),
    )(*operands)


def lane_runs(lanes, source):
    runs = []
    for lane in range(LANES):
        where = source(lanes + lane)
        if where is None:
            continue
        tile = (where[0], where[1] // LANES)
        shift = (lane - where[1]) % LANES
        if runs and runs[-1][1:] == (tile, shift):
            runs[-1] = (lane + 1, tile, shift)
        else:
            runs.append((lane + 1, tile, shift))
    return runs


def merge_runs(runs, load, cache, lane_index):
    out = None
    for end, tile, shift in reversed(runs):
        if (tile, shift) not in cache:
            value = load(*tile)
            cache[tile, shift] = pltpu.roll(value, shift, 1) if shift else value
        value = cache[tile, shift]
        out = value if out is None else jnp.where(lane_index < end, value, out)
    return out


def group_size(lat_dev):
    return LANES // math.gcd(lat_dev, LANES)


def spread(recv_ref, rows_ref, first, group, lat_dev, slot_dev):
    lat_total = rows_ref.shape[0] * LANES
    base = pl.multiple_of(first * lat_dev, LANES)
    lane_index = lax.broadcasted_iota(jnp.int32, (slot_dev, LANES), 1)
    pairs = {}

    def load(device, tile):
        pair = device // 2
        if (pair, tile) not in pairs:
            pairs[pair, tile] = recv_ref[
                2 * pair * slot_dev : 2 * (pair + 1) * slot_dev, pl.ds(base + tile * LANES, LANES)
            ].astype(jnp.float32)
        at = (device % 2) * slot_dev
        return pairs[pair, tile][at : at + slot_dev]

    cache = {}
    for lanes in range(0, lat_total, LANES):
        for i in range(group):
            runs = lane_runs(lanes, lambda j: (j // lat_dev, i * lat_dev + j % lat_dev))
            row = pl.multiple_of((first + i) * slot_dev, slot_dev)
            rows_ref[lanes // LANES, pl.ds(row, slot_dev), :] = merge_runs(
                runs, load, cache, lane_index
            )


def gather(rows_ref, send_ref, first, group, lat_dev, slot_dev):
    devices = rows_ref.shape[0] * LANES // lat_dev
    base = pl.multiple_of(first * lat_dev, LANES)
    lane_index = lax.broadcasted_iota(jnp.int32, (slot_dev, LANES), 1)
    cache = {}

    def load(i, tile):
        row = pl.multiple_of((first + i) * slot_dev, slot_dev)
        return rows_ref[tile, pl.ds(row, slot_dev), :]

    for pair in range(devices // 2):
        for lanes in range(0, group * lat_dev, LANES):
            tiles = []
            for device in (2 * pair, 2 * pair + 1):
                runs = lane_runs(
                    lanes,
                    lambda l: (l // lat_dev, device * lat_dev + l % lat_dev)
                    if l < group * lat_dev
                    else None,
                )
                tiles.append(merge_runs(runs, load, cache, lane_index))
            send_ref[
                2 * pair * slot_dev : 2 * (pair + 1) * slot_dev, pl.ds(base + lanes, LANES)
            ] = jnp.concatenate(tiles, axis=0).astype(jnp.bfloat16)


def join_tiles(ref, rows):
    return jnp.concatenate([ref[tile, rows, :] for tile in range(ref.shape[0])], axis=1)


def split_tiles(ref, rows, value):
    for tile in range(ref.shape[0]):
        ref[tile, rows, :] = value[:, tile * LANES : (tile + 1) * LANES]


def all_groups(levels, lat_dev, body):
    group = group_size(lat_dev)
    full = levels // group

    @pl.loop(0, full)
    def _(g):
        body(g * group, group)

    if levels % group:
        body(full * group, levels % group)


def step_body(waves_ref, recv_ref, legendre_ref, counts_ref, rates_ref, to_ref, from_ref, *refs):
    state_ref, send_ref, rows_ref, spec_ref = refs[-4:]
    slot = pl.program_id(0)
    wave = waves_ref[slot]
    row_total, lat_total = legendre_ref.shape[1:]
    _, levels, slot_dev, _ = state_ref.shape
    lat_dev = lat_total // (recv_ref.shape[0] // slot_dev)

    @pl.when(slot == 0)
    def _():
        all_groups(
            levels, lat_dev, lambda c, n: spread(recv_ref, rows_ref, c, n, lat_dev, slot_dev)
        )

    own = pl.ds(slot, levels, stride=slot_dev)
    matrix = legendre_ref[0]
    live = 2 * wave < counts_ref[...]
    direct = lax.dot_general(
        jnp.where(live, join_tiles(rows_ref, own), 0.0).astype(jnp.bfloat16),
        matrix,
        (((1,), (1,)), ((), ())),
        preferred_element_type=jnp.float32,
    ).astype(jnp.bfloat16)
    modal = jnp.dot(to_ref[...], direct, preferred_element_type=jnp.float32)
    degree = wave + 2 * lax.broadcasted_iota(jnp.int32, (1, row_total), 1)
    degree_f = degree.astype(jnp.float32)
    scaled_degree = degree_f * (degree_f + 1.0) / float(NMAX * (NMAX + 1))
    scaled = (modal / (1.0 + rates_ref[...] * scaled_degree)).astype(jnp.bfloat16)
    state = jnp.dot(from_ref[...], scaled, preferred_element_type=jnp.float32)
    state = jnp.where(degree <= NMAX, state, 0.0)
    split_tiles(spec_ref, own, state)
    rows = jnp.dot(state.astype(jnp.bfloat16), matrix, preferred_element_type=jnp.float32)
    split_tiles(rows_ref, own, jnp.where(live, rows, 0.0))

    @pl.when(slot == slot_dev - 1)
    def _():
        all_groups(
            levels, lat_dev, lambda c, n: gather(rows_ref, send_ref, c, n, lat_dev, slot_dev)
        )

        @pl.loop(0, levels)
        def _(c):
            at = pl.multiple_of(c * slot_dev, slot_dev)
            state_ref[0, c] = join_tiles(spec_ref, pl.ds(at, slot_dev)).astype(jnp.bfloat16)


def spectral_step(part, parts, received, legendre, own_waves, counts, rates, to_t, from_t, earlier):
    slots, width = received.shape
    slot_dev, row_total, lat_total = legendre.shape
    levels = to_t.shape[0]
    whole = lambda shape: pl.BlockSpec(shape, lambda s, waves: (0,) * len(shape))
    in_specs = [
        whole((slots, width)),
        pl.BlockSpec((1, row_total, lat_total), lambda s, waves: (s, 0, 0)),
        whole((1, lat_total)),
        whole((levels, 1)),
        whole((levels, levels)),
        whole((levels, levels)),
    ]
    operands = [own_waves, received, legendre, counts, rates, to_t, from_t]
    aliases = {}
    if earlier is not None:
        in_specs.append(pl.BlockSpec(memory_space=pl.ANY))
        aliases = {len(operands): 0}
        operands.append(earlier)
    return pl.pallas_call(
        step_body,
        grid_spec=pltpu.PrefetchScalarGridSpec(
            num_scalar_prefetch=1,
            grid=(slot_dev,),
            in_specs=in_specs,
            out_specs=[
                pl.BlockSpec((1, levels, slot_dev, row_total), lambda s, waves: (part, 0, 0, 0)),
                whole((slots, width)),
            ],
            scratch_shapes=[
                pltpu.VMEM((lat_total // LANES, levels * slot_dev, LANES), jnp.float32),
                pltpu.VMEM((row_total // LANES, levels * slot_dev, LANES), jnp.float32),
            ],
        ),
        out_shape=[
            jax.ShapeDtypeStruct((parts, levels, slot_dev, row_total), jnp.bfloat16),
            jax.ShapeDtypeStruct((slots, width), jnp.bfloat16),
        ],
        input_output_aliases=aliases,
        compiler_params=pltpu.CompilerParams(vmem_limit_bytes=VMEM_BYTES),
        cost_estimate=pl.CostEstimate(
            flops=4 * slot_dev * row_total * lat_total * levels,
            bytes_accessed=2 * slot_dev * lat_total * (row_total + 3 * levels),
            transcendentals=0,
        ),
    )(*operands)


def per_device(
    north_rows, south_rows, lon_counts, slot_wave, legendre, mode_rates, to_modes, from_modes
):
    lat_dev, slots, channels = north_rows.shape
    slot_dev, row_total, lat_total = legendre.shape
    levels = to_modes.shape[0]
    parts = channels // levels
    my_index = lax.axis_index("wave")
    own_waves = lax.dynamic_slice_in_dim(slot_wave, my_index * slot_dev, slot_dev)
    north = jnp.transpose(north_rows, (2, 0, 1)).reshape(parts, levels, lat_dev, slots)
    south = jnp.transpose(south_rows, (2, 0, 1)).reshape(parts, levels, lat_dev, slots)
    exchange = functools.partial(
        lax.all_to_all, axis_name="wave", split_axis=0, concat_axis=0, tiled=True
    )
    columns = [exchange(pack(part, north, south)) for part in range(parts)]
    spec_state = None
    returned = []
    for part in range(parts):
        spec_state, rows = spectral_step(
            part, parts, columns[part], legendre, own_waves, lon_counts[None, :],
            mode_rates[:, None], to_modes.T, from_modes.T, spec_state,
        )
        returned.append(exchange(rows))
    new_rows = None
    for part in range(parts):
        new_rows = unpack(part, parts, levels, lat_dev, returned[part], new_rows)
    new_rows = jnp.transpose(new_rows.reshape(channels, lat_dev, slots), (1, 2, 0))
    spec_state = jnp.transpose(spec_state.reshape(channels, slot_dev, row_total), (1, 2, 0))
    return (spec_state, new_rows)


def solution(mesh):
    in_specs = (
        P(("grp", "wave"), None, None),
        P(("grp", "wave"), None, None),
        P(),
        P(),
        P("wave", None, None),
        P(),
        P(),
        P(),
    )
    out_specs = (P(("grp", "wave"), None, None), P(("grp", "wave"), None, None))
    return jax.shard_map(
        per_device, mesh=mesh, in_specs=in_specs, out_specs=out_specs, check_vma=False
    )
```

```python
import functools
import math

import jax
import jax.numpy as jnp
from jax import lax
from jax.experimental import pallas as pl
from jax.experimental.pallas import tpu as pltpu
from jax.sharding import PartitionSpec as P

NMAX = 2559
VMEM_BYTES = 62 * 1024 * 1024
GROUPS = 1
LANES = 128


def flat_rows(value):
    group, lat_dev, slots = value.shape
    if lat_dev % 16:
        value = value.astype(jnp.float32)
    return value.reshape(group * lat_dev, slots).astype(jnp.bfloat16)


def pieces(levels, lat_dev, width):
    group = GROUPS * group_size(lat_dev)
    out = []
    for first in range(0, levels, group):
        lane = first * lat_dev
        count = min(group, levels - first)
        out.append((first, count, lane, min(group * lat_dev, width - lane)))
    return out


def pack_body(north_ref, south_ref, out_ref, north_buf, south_buf, out_buf, in_sems, out_sems, *, part):
    _, levels, lat_dev, slots = north_ref.shape
    cut = pieces(levels, lat_dev, out_ref.shape[1])
    group = cut[0][1]
    loads, stores = [], []
    for i, (first, count, _, _) in enumerate(cut):
        some = pl.ds(first, count)
        loads.append(
            [
                pltpu.make_async_copy(ref.at[part, some], buf.at[some], in_sems.at[j, i])
                for j, (ref, buf) in enumerate([(north_ref, north_buf), (south_ref, south_buf)])
            ]
        )
        for load in loads[-1]:
            load.start()
    for buf in (north_buf, south_buf):
        if buf.shape[0] > levels:
            buf[levels:] = jnp.zeros((buf.shape[0] - levels, lat_dev, slots), buf.dtype)
    for i, (first, _, lane, lanes) in enumerate(cut):
        for load in loads[i]:
            load.wait()
        summed = north_buf[first : first + group] + south_buf[first : first + group]
        out_buf[:, lane : lane + lanes] = flat_rows(summed).T[:, :lanes]
        some = pl.ds(lane, lanes)
        stores.append(pltpu.make_async_copy(out_buf.at[:, some], out_ref.at[:, some], out_sems.at[i]))
        stores[-1].start()
    for store in stores:
        store.wait()


def pack(part, north, south):
    _, levels, lat_dev, slots = north.shape
    width = pl.cdiv(levels * lat_dev, LANES) * LANES
    cut = pieces(levels, lat_dev, width)
    anywhere = pl.BlockSpec(memory_space=pl.ANY)
    rows = pltpu.VMEM((len(cut) * cut[0][1], lat_dev, slots), jnp.bfloat16)
    return pl.pallas_call(
        functools.partial(pack_body, part=part),
        in_specs=[anywhere, anywhere],
        out_specs=anywhere,
        out_shape=jax.ShapeDtypeStruct((slots, width), jnp.bfloat16),
        scratch_shapes=[
            rows,
            rows,
            pltpu.VMEM((slots, width), jnp.bfloat16),
            pltpu.SemaphoreType.DMA((2, len(cut))),
            pltpu.SemaphoreType.DMA((len(cut),)),
        ],
        compiler_params=pltpu.CompilerParams(vmem_limit_bytes=VMEM_BYTES),
        cost_estimate=pl.CostEstimate(
            flops=2 * levels * lat_dev * slots,
            bytes_accessed=6 * levels * lat_dev * slots,
            transcendentals=0,
        ),
    )(north, south)


def unpack_body(in_ref, *refs, part):
    out_ref, in_buf, out_buf, in_sems, out_sems = refs[-5:]
    levels, lat_dev, slots = out_buf.shape
    cut = pieces(levels, lat_dev, in_ref.shape[1])
    loads, stores = [], []
    for i, (_, _, lane, lanes) in enumerate(cut):
        some = pl.ds(lane, lanes)
        loads.append(pltpu.make_async_copy(in_ref.at[:, some], in_buf.at[:, some], in_sems.at[i]))
        loads[-1].start()
    for i, (first, count, lane, lanes) in enumerate(cut):
        loads[i].wait()
        rows = in_buf[:, lane : lane + lanes].T
        if lat_dev % 16:
            rows = rows.astype(jnp.float32)
        rows = rows[: count * lat_dev].reshape(count, lat_dev, slots)
        out_buf[first : first + count] = rows.astype(jnp.bfloat16)
        some = pl.ds(first, count)
        stores.append(pltpu.make_async_copy(out_buf.at[some], out_ref.at[part, some], out_sems.at[i]))
        stores[-1].start()
    for store in stores:
        store.wait()


def unpack(part, parts, levels, lat_dev, received, earlier):
    slots, width = received.shape
    cut = pieces(levels, lat_dev, width)
    anywhere = pl.BlockSpec(memory_space=pl.ANY)
    operands = [received] if earlier is None else [received, earlier]
    return pl.pallas_call(
        functools.partial(unpack_body, part=part),
        in_specs=[anywhere] * len(operands),
        out_specs=anywhere,
        out_shape=jax.ShapeDtypeStruct((parts, levels, lat_dev, slots), jnp.bfloat16),
        input_output_aliases={} if earlier is None else {1: 0},
        scratch_shapes=[
            pltpu.VMEM((slots, width), jnp.bfloat16),
            pltpu.VMEM((levels, lat_dev, slots), jnp.bfloat16),
            pltpu.SemaphoreType.DMA((len(cut),)),
            pltpu.SemaphoreType.DMA((len(cut),)),
        ],
        compiler_params=pltpu.CompilerParams(vmem_limit_bytes=VMEM_BYTES),
        cost_estimate=pl.CostEstimate(
            flops=levels * lat_dev * slots,
            bytes_accessed=4 * levels * lat_dev * slots,
            transcendentals=0,
        ),
    )(*operands)


def lane_runs(lanes, source):
    runs = []
    for lane in range(LANES):
        where = source(lanes + lane)
        if where is None:
            continue
        tile = (where[0], where[1] // LANES)
        shift = (lane - where[1]) % LANES
        if runs and runs[-1][1:] == (tile, shift):
            runs[-1] = (lane + 1, tile, shift)
        else:
            runs.append((lane + 1, tile, shift))
    return runs


def merge_runs(runs, load, cache, lane_index):
    out = None
    for end, tile, shift in reversed(runs):
        if (tile, shift) not in cache:
            value = load(*tile)
            cache[tile, shift] = pltpu.roll(value, shift, 1) if shift else value
        value = cache[tile, shift]
        out = value if out is None else jnp.where(lane_index < end, value, out)
    return out


def group_size(lat_dev):
    return LANES // math.gcd(lat_dev, LANES)


def spread(recv_ref, rows_ref, first, group, lat_dev, slot_dev):
    lat_total = rows_ref.shape[0] * LANES
    base = pl.multiple_of(first * lat_dev, LANES)
    lane_index = lax.broadcasted_iota(jnp.int32, (slot_dev, LANES), 1)
    pairs = {}

    def load(device, tile):
        pair = device // 2
        if (pair, tile) not in pairs:
            pairs[pair, tile] = recv_ref[
                2 * pair * slot_dev : 2 * (pair + 1) * slot_dev, pl.ds(base + tile * LANES, LANES)
            ].astype(jnp.float32)
        at = (device % 2) * slot_dev
        return pairs[pair, tile][at : at + slot_dev]

    cache = {}
    for lanes in range(0, lat_total, LANES):
        for i in range(group):
            runs = lane_runs(lanes, lambda j: (j // lat_dev, i * lat_dev + j % lat_dev))
            row = pl.multiple_of((first + i) * slot_dev, slot_dev)
            rows_ref[lanes // LANES, pl.ds(row, slot_dev), :] = merge_runs(
                runs, load, cache, lane_index
            )


def gather(rows_ref, send_ref, first, group, lat_dev, slot_dev):
    devices = rows_ref.shape[0] * LANES // lat_dev
    base = pl.multiple_of(first * lat_dev, LANES)
    lane_index = lax.broadcasted_iota(jnp.int32, (slot_dev, LANES), 1)
    cache = {}

    def load(i, tile):
        row = pl.multiple_of((first + i) * slot_dev, slot_dev)
        return rows_ref[tile, pl.ds(row, slot_dev), :]

    for pair in range(devices // 2):
        for lanes in range(0, group * lat_dev, LANES):
            tiles = []
            for device in (2 * pair, 2 * pair + 1):
                runs = lane_runs(
                    lanes,
                    lambda l: (l // lat_dev, device * lat_dev + l % lat_dev)
                    if l < group * lat_dev
                    else None,
                )
                tiles.append(merge_runs(runs, load, cache, lane_index))
            send_ref[
                2 * pair * slot_dev : 2 * (pair + 1) * slot_dev, pl.ds(base + lanes, LANES)
            ] = jnp.concatenate(tiles, axis=0).astype(jnp.bfloat16)


def join_tiles(ref, rows):
    return jnp.concatenate([ref[tile, rows, :] for tile in range(ref.shape[0])], axis=1)


def split_tiles(ref, rows, value):
    for tile in range(ref.shape[0]):
        ref[tile, rows, :] = value[:, tile * LANES : (tile + 1) * LANES]


def all_groups(levels, lat_dev, body):
    group = group_size(lat_dev)
    full = levels // group

    @pl.loop(0, full)
    def _(g):
        body(g * group, group)

    if levels % group:
        body(full * group, levels % group)


def step_body(waves_ref, recv_ref, legendre_ref, counts_ref, rates_ref, to_ref, from_ref, *refs):
    state_ref, send_ref, rows_ref, spec_ref = refs[-4:]
    slot = pl.program_id(0)
    wave = waves_ref[slot]
    row_total, lat_total = legendre_ref.shape[1:]
    _, levels, slot_dev, _ = state_ref.shape
    lat_dev = lat_total // (recv_ref.shape[0] // slot_dev)

    @pl.when(slot == 0)
    def _():
        all_groups(
            levels, lat_dev, lambda c, n: spread(recv_ref, rows_ref, c, n, lat_dev, slot_dev)
        )

    own = pl.ds(slot, levels, stride=slot_dev)
    matrix = legendre_ref[0]
    live = 2 * wave < counts_ref[...]
    direct = lax.dot_general(
        jnp.where(live, join_tiles(rows_ref, own), 0.0).astype(jnp.bfloat16),
        matrix,
        (((1,), (1,)), ((), ())),
        preferred_element_type=jnp.float32,
    ).astype(jnp.bfloat16)
    modal = jnp.dot(to_ref[...], direct, preferred_element_type=jnp.float32)
    degree = wave + 2 * lax.broadcasted_iota(jnp.int32, (1, row_total), 1)
    degree_f = degree.astype(jnp.float32)
    scaled_degree = degree_f * (degree_f + 1.0) / float(NMAX * (NMAX + 1))
    scaled = (modal / (1.0 + rates_ref[...] * scaled_degree)).astype(jnp.bfloat16)
    state = jnp.dot(from_ref[...], scaled, preferred_element_type=jnp.float32)
    state = jnp.where(degree <= NMAX, state, 0.0)
    split_tiles(spec_ref, own, state)
    rows = jnp.dot(state.astype(jnp.bfloat16), matrix, preferred_element_type=jnp.float32)
    split_tiles(rows_ref, own, jnp.where(live, rows, 0.0))

    @pl.when(slot == slot_dev - 1)
    def _():
        all_groups(
            levels, lat_dev, lambda c, n: gather(rows_ref, send_ref, c, n, lat_dev, slot_dev)
        )

        @pl.loop(0, levels)
        def _(c):
            at = pl.multiple_of(c * slot_dev, slot_dev)
            state_ref[0, c] = join_tiles(spec_ref, pl.ds(at, slot_dev)).astype(jnp.bfloat16)


def spectral_step(part, parts, received, legendre, own_waves, counts, rates, to_t, from_t, earlier):
    slots, width = received.shape
    slot_dev, row_total, lat_total = legendre.shape
    levels = to_t.shape[0]
    whole = lambda shape: pl.BlockSpec(shape, lambda s, waves: (0,) * len(shape))
    in_specs = [
        whole((slots, width)),
        pl.BlockSpec((1, row_total, lat_total), lambda s, waves: (s, 0, 0)),
        whole((1, lat_total)),
        whole((levels, 1)),
        whole((levels, levels)),
        whole((levels, levels)),
    ]
    operands = [own_waves, received, legendre, counts, rates, to_t, from_t]
    aliases = {}
    if earlier is not None:
        in_specs.append(pl.BlockSpec(memory_space=pl.ANY))
        aliases = {len(operands): 0}
        operands.append(earlier)
    return pl.pallas_call(
        step_body,
        grid_spec=pltpu.PrefetchScalarGridSpec(
            num_scalar_prefetch=1,
            grid=(slot_dev,),
            in_specs=in_specs,
            out_specs=[
                pl.BlockSpec((1, levels, slot_dev, row_total), lambda s, waves: (part, 0, 0, 0)),
                whole((slots, width)),
            ],
            scratch_shapes=[
                pltpu.VMEM((lat_total // LANES, levels * slot_dev, LANES), jnp.float32),
                pltpu.VMEM((row_total // LANES, levels * slot_dev, LANES), jnp.float32),
            ],
        ),
        out_shape=[
            jax.ShapeDtypeStruct((parts, levels, slot_dev, row_total), jnp.bfloat16),
            jax.ShapeDtypeStruct((slots, width), jnp.bfloat16),
        ],
        input_output_aliases=aliases,
        compiler_params=pltpu.CompilerParams(vmem_limit_bytes=VMEM_BYTES),
        cost_estimate=pl.CostEstimate(
            flops=4 * slot_dev * row_total * lat_total * levels,
            bytes_accessed=2 * slot_dev * lat_total * (row_total + 3 * levels),
            transcendentals=0,
        ),
    )(*operands)


def per_device(
    north_rows, south_rows, lon_counts, slot_wave, legendre, mode_rates, to_modes, from_modes
):
    lat_dev, slots, channels = north_rows.shape
    slot_dev, row_total, lat_total = legendre.shape
    levels = to_modes.shape[0]
    parts = channels // levels
    my_index = lax.axis_index("wave")
    own_waves = lax.dynamic_slice_in_dim(slot_wave, my_index * slot_dev, slot_dev)
    north = jnp.transpose(north_rows, (2, 0, 1)).reshape(parts, levels, lat_dev, slots)
    south = jnp.transpose(south_rows, (2, 0, 1)).reshape(parts, levels, lat_dev, slots)
    exchange = functools.partial(
        lax.all_to_all, axis_name="wave", split_axis=0, concat_axis=0, tiled=True
    )
    columns = [exchange(pack(part, north, south)) for part in range(parts)]
    spec_state = None
    returned = []
    for part in range(parts):
        spec_state, rows = spectral_step(
            part, parts, columns[part], legendre, own_waves, lon_counts[None, :],
            mode_rates[:, None], to_modes.T, from_modes.T, spec_state,
        )
        returned.append(exchange(rows))
    new_rows = None
    for part in range(parts):
        new_rows = unpack(part, parts, levels, lat_dev, returned[part], new_rows)
    new_rows = jnp.transpose(new_rows.reshape(channels, lat_dev, slots), (1, 2, 0))
    spec_state = jnp.transpose(spec_state.reshape(channels, slot_dev, row_total), (1, 2, 0))
    return (spec_state, new_rows)


def solution(mesh):
    in_specs = (
        P(("grp", "wave"), None, None),
        P(("grp", "wave"), None, None),
        P(),
        P(),
        P("wave", None, None),
        P(),
        P(),
        P(),
    )
    out_specs = (P(("grp", "wave"), None, None), P(("grp", "wave"), None, None))
    return jax.shard_map(
        per_device, mesh=mesh, in_specs=in_specs, out_specs=out_specs, check_vma=False
    )
```

```python
import functools
import math

import jax
import jax.numpy as jnp
from jax import lax
from jax.experimental import pallas as pl
from jax.experimental.pallas import tpu as pltpu
from jax.sharding import PartitionSpec as P

NMAX = 2559
VMEM_BYTES = 62 * 1024 * 1024
GROUPS = 3
LANES = 128


def flat_rows(value):
    group, lat_dev, slots = value.shape
    if lat_dev % 16:
        value = value.astype(jnp.float32)
    return value.reshape(group * lat_dev, slots).astype(jnp.bfloat16)


def pieces(levels, lat_dev, width):
    group = GROUPS * group_size(lat_dev)
    out = []
    for first in range(0, levels, group):
        lane = first * lat_dev
        count = min(group, levels - first)
        out.append((first, count, lane, min(group * lat_dev, width - lane)))
    return out


def pack_body(north_ref, south_ref, out_ref, north_buf, south_buf, out_buf, in_sems, out_sems, *, part):
    _, levels, lat_dev, slots = north_ref.shape
    cut = pieces(levels, lat_dev, out_ref.shape[1])
    group = cut[0][1]
    loads, stores = [], []
    for i, (first, count, _, _) in enumerate(cut):
        some = pl.ds(first, count)
        loads.append(
            [
                pltpu.make_async_copy(ref.at[part, some], buf.at[some], in_sems.at[j, i])
                for j, (ref, buf) in enumerate([(north_ref, north_buf), (south_ref, south_buf)])
            ]
        )
        for load in loads[-1]:
            load.start()
    for buf in (north_buf, south_buf):
        if buf.shape[0] > levels:
            buf[levels:] = jnp.zeros((buf.shape[0] - levels, lat_dev, slots), buf.dtype)
    for i, (first, _, lane, lanes) in enumerate(cut):
        for load in loads[i]:
            load.wait()
        summed = north_buf[first : first + group] + south_buf[first : first + group]
        out_buf[:, lane : lane + lanes] = flat_rows(summed).T[:, :lanes]
        some = pl.ds(lane, lanes)
        stores.append(pltpu.make_async_copy(out_buf.at[:, some], out_ref.at[:, some], out_sems.at[i]))
        stores[-1].start()
    for store in stores:
        store.wait()


def pack(part, north, south):
    _, levels, lat_dev, slots = north.shape
    width = pl.cdiv(levels * lat_dev, LANES) * LANES
    cut = pieces(levels, lat_dev, width)
    anywhere = pl.BlockSpec(memory_space=pl.ANY)
    rows = pltpu.VMEM((len(cut) * cut[0][1], lat_dev, slots), jnp.bfloat16)
    return pl.pallas_call(
        functools.partial(pack_body, part=part),
        in_specs=[anywhere, anywhere],
        out_specs=anywhere,
        out_shape=jax.ShapeDtypeStruct((slots, width), jnp.bfloat16),
        scratch_shapes=[
            rows,
            rows,
            pltpu.VMEM((slots, width), jnp.bfloat16),
            pltpu.SemaphoreType.DMA((2, len(cut))),
            pltpu.SemaphoreType.DMA((len(cut),)),
        ],
        compiler_params=pltpu.CompilerParams(vmem_limit_bytes=VMEM_BYTES),
        cost_estimate=pl.CostEstimate(
            flops=2 * levels * lat_dev * slots,
            bytes_accessed=6 * levels * lat_dev * slots,
            transcendentals=0,
        ),
    )(north, south)


def unpack_body(in_ref, *refs, part):
    out_ref, in_buf, out_buf, in_sems, out_sems = refs[-5:]
    levels, lat_dev, slots = out_buf.shape
    cut = pieces(levels, lat_dev, in_ref.shape[1])
    loads, stores = [], []
    for i, (_, _, lane, lanes) in enumerate(cut):
        some = pl.ds(lane, lanes)
        loads.append(pltpu.make_async_copy(in_ref.at[:, some], in_buf.at[:, some], in_sems.at[i]))
        loads[-1].start()
    for i, (first, count, lane, lanes) in enumerate(cut):
        loads[i].wait()
        rows = in_buf[:, lane : lane + lanes].T
        if lat_dev % 16:
            rows = rows.astype(jnp.float32)
        rows = rows[: count * lat_dev].reshape(count, lat_dev, slots)
        out_buf[first : first + count] = rows.astype(jnp.bfloat16)
        some = pl.ds(first, count)
        stores.append(pltpu.make_async_copy(out_buf.at[some], out_ref.at[part, some], out_sems.at[i]))
        stores[-1].start()
    for store in stores:
        store.wait()


def unpack(part, parts, levels, lat_dev, received, earlier):
    slots, width = received.shape
    cut = pieces(levels, lat_dev, width)
    anywhere = pl.BlockSpec(memory_space=pl.ANY)
    operands = [received] if earlier is None else [received, earlier]
    return pl.pallas_call(
        functools.partial(unpack_body, part=part),
        in_specs=[anywhere] * len(operands),
        out_specs=anywhere,
        out_shape=jax.ShapeDtypeStruct((parts, levels, lat_dev, slots), jnp.bfloat16),
        input_output_aliases={} if earlier is None else {1: 0},
        scratch_shapes=[
            pltpu.VMEM((slots, width), jnp.bfloat16),
            pltpu.VMEM((levels, lat_dev, slots), jnp.bfloat16),
            pltpu.SemaphoreType.DMA((len(cut),)),
            pltpu.SemaphoreType.DMA((len(cut),)),
        ],
        compiler_params=pltpu.CompilerParams(vmem_limit_bytes=VMEM_BYTES),
        cost_estimate=pl.CostEstimate(
            flops=levels * lat_dev * slots,
            bytes_accessed=4 * levels * lat_dev * slots,
            transcendentals=0,
        ),
    )(*operands)


def lane_runs(lanes, source):
    runs = []
    for lane in range(LANES):
        where = source(lanes + lane)
        if where is None:
            continue
        tile = (where[0], where[1] // LANES)
        shift = (lane - where[1]) % LANES
        if runs and runs[-1][1:] == (tile, shift):
            runs[-1] = (lane + 1, tile, shift)
        else:
            runs.append((lane + 1, tile, shift))
    return runs


def merge_runs(runs, load, cache, lane_index):
    out = None
    for end, tile, shift in reversed(runs):
        if (tile, shift) not in cache:
            value = load(*tile)
            cache[tile, shift] = pltpu.roll(value, shift, 1) if shift else value
        value = cache[tile, shift]
        out = value if out is None else jnp.where(lane_index < end, value, out)
    return out


def group_size(lat_dev):
    return LANES // math.gcd(lat_dev, LANES)


def spread(recv_ref, rows_ref, first, group, lat_dev, slot_dev):
    lat_total = rows_ref.shape[0] * LANES
    base = pl.multiple_of(first * lat_dev, LANES)
    lane_index = lax.broadcasted_iota(jnp.int32, (slot_dev, LANES), 1)
    pairs = {}

    def load(device, tile):
        pair = device // 2
        if (pair, tile) not in pairs:
            pairs[pair, tile] = recv_ref[
                2 * pair * slot_dev : 2 * (pair + 1) * slot_dev, pl.ds(base + tile * LANES, LANES)
            ].astype(jnp.float32)
        at = (device % 2) * slot_dev
        return pairs[pair, tile][at : at + slot_dev]

    cache = {}
    for lanes in range(0, lat_total, LANES):
        for i in range(group):
            runs = lane_runs(lanes, lambda j: (j // lat_dev, i * lat_dev + j % lat_dev))
            row = pl.multiple_of((first + i) * slot_dev, slot_dev)
            rows_ref[lanes // LANES, pl.ds(row, slot_dev), :] = merge_runs(
                runs, load, cache, lane_index
            )


def gather(rows_ref, send_ref, first, group, lat_dev, slot_dev):
    devices = rows_ref.shape[0] * LANES // lat_dev
    base = pl.multiple_of(first * lat_dev, LANES)
    lane_index = lax.broadcasted_iota(jnp.int32, (slot_dev, LANES), 1)
    cache = {}

    def load(i, tile):
        row = pl.multiple_of((first + i) * slot_dev, slot_dev)
        return rows_ref[tile, pl.ds(row, slot_dev), :]

    for pair in range(devices // 2):
        for lanes in range(0, group * lat_dev, LANES):
            tiles = []
            for device in (2 * pair, 2 * pair + 1):
                runs = lane_runs(
                    lanes,
                    lambda l: (l // lat_dev, device * lat_dev + l % lat_dev)
                    if l < group * lat_dev
                    else None,
                )
                tiles.append(merge_runs(runs, load, cache, lane_index))
            send_ref[
                2 * pair * slot_dev : 2 * (pair + 1) * slot_dev, pl.ds(base + lanes, LANES)
            ] = jnp.concatenate(tiles, axis=0).astype(jnp.bfloat16)


def join_tiles(ref, rows):
    return jnp.concatenate([ref[tile, rows, :] for tile in range(ref.shape[0])], axis=1)


def split_tiles(ref, rows, value):
    for tile in range(ref.shape[0]):
        ref[tile, rows, :] = value[:, tile * LANES : (tile + 1) * LANES]


def all_groups(levels, lat_dev, body):
    group = group_size(lat_dev)
    full = levels // group

    @pl.loop(0, full)
    def _(g):
        body(g * group, group)

    if levels % group:
        body(full * group, levels % group)


def step_body(waves_ref, recv_ref, legendre_ref, counts_ref, rates_ref, to_ref, from_ref, *refs):
    state_ref, send_ref, rows_ref, spec_ref = refs[-4:]
    slot = pl.program_id(0)
    wave = waves_ref[slot]
    row_total, lat_total = legendre_ref.shape[1:]
    _, levels, slot_dev, _ = state_ref.shape
    lat_dev = lat_total // (recv_ref.shape[0] // slot_dev)

    @pl.when(slot == 0)
    def _():
        all_groups(
            levels, lat_dev, lambda c, n: spread(recv_ref, rows_ref, c, n, lat_dev, slot_dev)
        )

    own = pl.ds(slot, levels, stride=slot_dev)
    matrix = legendre_ref[0]
    live = 2 * wave < counts_ref[...]
    direct = lax.dot_general(
        jnp.where(live, join_tiles(rows_ref, own), 0.0).astype(jnp.bfloat16),
        matrix,
        (((1,), (1,)), ((), ())),
        preferred_element_type=jnp.float32,
    ).astype(jnp.bfloat16)
    modal = jnp.dot(to_ref[...], direct, preferred_element_type=jnp.float32)
    degree = wave + 2 * lax.broadcasted_iota(jnp.int32, (1, row_total), 1)
    degree_f = degree.astype(jnp.float32)
    scaled_degree = degree_f * (degree_f + 1.0) / float(NMAX * (NMAX + 1))
    scaled = (modal / (1.0 + rates_ref[...] * scaled_degree)).astype(jnp.bfloat16)
    state = jnp.dot(from_ref[...], scaled, preferred_element_type=jnp.float32)
    state = jnp.where(degree <= NMAX, state, 0.0)
    split_tiles(spec_ref, own, state)
    rows = jnp.dot(state.astype(jnp.bfloat16), matrix, preferred_element_type=jnp.float32)
    split_tiles(rows_ref, own, jnp.where(live, rows, 0.0))

    @pl.when(slot == slot_dev - 1)
    def _():
        all_groups(
            levels, lat_dev, lambda c, n: gather(rows_ref, send_ref, c, n, lat_dev, slot_dev)
        )

        @pl.loop(0, levels)
        def _(c):
            at = pl.multiple_of(c * slot_dev, slot_dev)
            state_ref[0, c] = join_tiles(spec_ref, pl.ds(at, slot_dev)).astype(jnp.bfloat16)


def spectral_step(part, parts, received, legendre, own_waves, counts, rates, to_t, from_t, earlier):
    slots, width = received.shape
    slot_dev, row_total, lat_total = legendre.shape
    levels = to_t.shape[0]
    whole = lambda shape: pl.BlockSpec(shape, lambda s, waves: (0,) * len(shape))
    in_specs = [
        whole((slots, width)),
        pl.BlockSpec((1, row_total, lat_total), lambda s, waves: (s, 0, 0)),
        whole((1, lat_total)),
        whole((levels, 1)),
        whole((levels, levels)),
        whole((levels, levels)),
    ]
    operands = [own_waves, received, legendre, counts, rates, to_t, from_t]
    aliases = {}
    if earlier is not None:
        in_specs.append(pl.BlockSpec(memory_space=pl.ANY))
        aliases = {len(operands): 0}
        operands.append(earlier)
    return pl.pallas_call(
        step_body,
        grid_spec=pltpu.PrefetchScalarGridSpec(
            num_scalar_prefetch=1,
            grid=(slot_dev,),
            in_specs=in_specs,
            out_specs=[
                pl.BlockSpec((1, levels, slot_dev, row_total), lambda s, waves: (part, 0, 0, 0)),
                whole((slots, width)),
            ],
            scratch_shapes=[
                pltpu.VMEM((lat_total // LANES, levels * slot_dev, LANES), jnp.float32),
                pltpu.VMEM((row_total // LANES, levels * slot_dev, LANES), jnp.float32),
            ],
        ),
        out_shape=[
            jax.ShapeDtypeStruct((parts, levels, slot_dev, row_total), jnp.bfloat16),
            jax.ShapeDtypeStruct((slots, width), jnp.bfloat16),
        ],
        input_output_aliases=aliases,
        compiler_params=pltpu.CompilerParams(vmem_limit_bytes=VMEM_BYTES),
        cost_estimate=pl.CostEstimate(
            flops=4 * slot_dev * row_total * lat_total * levels,
            bytes_accessed=2 * slot_dev * lat_total * (row_total + 3 * levels),
            transcendentals=0,
        ),
    )(*operands)


def per_device(
    north_rows, south_rows, lon_counts, slot_wave, legendre, mode_rates, to_modes, from_modes
):
    lat_dev, slots, channels = north_rows.shape
    slot_dev, row_total, lat_total = legendre.shape
    levels = to_modes.shape[0]
    parts = channels // levels
    my_index = lax.axis_index("wave")
    own_waves = lax.dynamic_slice_in_dim(slot_wave, my_index * slot_dev, slot_dev)
    north = jnp.transpose(north_rows, (2, 0, 1)).reshape(parts, levels, lat_dev, slots)
    south = jnp.transpose(south_rows, (2, 0, 1)).reshape(parts, levels, lat_dev, slots)
    exchange = functools.partial(
        lax.all_to_all, axis_name="wave", split_axis=0, concat_axis=0, tiled=True
    )
    columns = [exchange(pack(part, north, south)) for part in range(parts)]
    spec_state = None
    returned = []
    for part in range(parts):
        spec_state, rows = spectral_step(
            part, parts, columns[part], legendre, own_waves, lon_counts[None, :],
            mode_rates[:, None], to_modes.T, from_modes.T, spec_state,
        )
        returned.append(exchange(rows))
    new_rows = None
    for part in range(parts):
        new_rows = unpack(part, parts, levels, lat_dev, returned[part], new_rows)
    new_rows = jnp.transpose(new_rows.reshape(channels, lat_dev, slots), (1, 2, 0))
    spec_state = jnp.transpose(spec_state.reshape(channels, slot_dev, row_total), (1, 2, 0))
    return (spec_state, new_rows)


def solution(mesh):
    in_specs = (
        P(("grp", "wave"), None, None),
        P(("grp", "wave"), None, None),
        P(),
        P(),
        P("wave", None, None),
        P(),
        P(),
        P(),
    )
    out_specs = (P(("grp", "wave"), None, None), P(("grp", "wave"), None, None))
    return jax.shard_map(
        per_device, mesh=mesh, in_specs=in_specs, out_specs=out_specs, check_vma=False
    )
```

```python
import functools
import math

import jax
import jax.numpy as jnp
from jax import lax
from jax.experimental import pallas as pl
from jax.experimental.pallas import tpu as pltpu
from jax.sharding import PartitionSpec as P

NMAX = 2559
VMEM_BYTES = 62 * 1024 * 1024
GROUPS = 6
LANES = 128


def flat_rows(value):
    group, lat_dev, slots = value.shape
    if lat_dev % 16:
        value = value.astype(jnp.float32)
    return value.reshape(group * lat_dev, slots).astype(jnp.bfloat16)


def pieces(levels, lat_dev, width):
    group = GROUPS * group_size(lat_dev)
    out = []
    for first in range(0, levels, group):
        lane = first * lat_dev
        count = min(group, levels - first)
        out.append((first, count, lane, min(group * lat_dev, width - lane)))
    return out


def pack_body(north_ref, south_ref, out_ref, north_buf, south_buf, out_buf, in_sems, out_sems, *, part):
    _, levels, lat_dev, slots = north_ref.shape
    cut = pieces(levels, lat_dev, out_ref.shape[1])
    group = cut[0][1]
    loads, stores = [], []
    for i, (first, count, _, _) in enumerate(cut):
        some = pl.ds(first, count)
        loads.append(
            [
                pltpu.make_async_copy(ref.at[part, some], buf.at[some], in_sems.at[j, i])
                for j, (ref, buf) in enumerate([(north_ref, north_buf), (south_ref, south_buf)])
            ]
        )
        for load in loads[-1]:
            load.start()
    for buf in (north_buf, south_buf):
        if buf.shape[0] > levels:
            buf[levels:] = jnp.zeros((buf.shape[0] - levels, lat_dev, slots), buf.dtype)
    for i, (first, _, lane, lanes) in enumerate(cut):
        for load in loads[i]:
            load.wait()
        summed = north_buf[first : first + group] + south_buf[first : first + group]
        out_buf[:, lane : lane + lanes] = flat_rows(summed).T[:, :lanes]
        some = pl.ds(lane, lanes)
        stores.append(pltpu.make_async_copy(out_buf.at[:, some], out_ref.at[:, some], out_sems.at[i]))
        stores[-1].start()
    for store in stores:
        store.wait()


def pack(part, north, south):
    _, levels, lat_dev, slots = north.shape
    width = pl.cdiv(levels * lat_dev, LANES) * LANES
    cut = pieces(levels, lat_dev, width)
    anywhere = pl.BlockSpec(memory_space=pl.ANY)
    rows = pltpu.VMEM((len(cut) * cut[0][1], lat_dev, slots), jnp.bfloat16)
    return pl.pallas_call(
        functools.partial(pack_body, part=part),
        in_specs=[anywhere, anywhere],
        out_specs=anywhere,
        out_shape=jax.ShapeDtypeStruct((slots, width), jnp.bfloat16),
        scratch_shapes=[
            rows,
            rows,
            pltpu.VMEM((slots, width), jnp.bfloat16),
            pltpu.SemaphoreType.DMA((2, len(cut))),
            pltpu.SemaphoreType.DMA((len(cut),)),
        ],
        compiler_params=pltpu.CompilerParams(vmem_limit_bytes=VMEM_BYTES),
        cost_estimate=pl.CostEstimate(
            flops=2 * levels * lat_dev * slots,
            bytes_accessed=6 * levels * lat_dev * slots,
            transcendentals=0,
        ),
    )(north, south)


def unpack_body(in_ref, *refs, part):
    out_ref, in_buf, out_buf, in_sems, out_sems = refs[-5:]
    levels, lat_dev, slots = out_buf.shape
    cut = pieces(levels, lat_dev, in_ref.shape[1])
    loads, stores = [], []
    for i, (_, _, lane, lanes) in enumerate(cut):
        some = pl.ds(lane, lanes)
        loads.append(pltpu.make_async_copy(in_ref.at[:, some], in_buf.at[:, some], in_sems.at[i]))
        loads[-1].start()
    for i, (first, count, lane, lanes) in enumerate(cut):
        loads[i].wait()
        rows = in_buf[:, lane : lane + lanes].T
        if lat_dev % 16:
            rows = rows.astype(jnp.float32)
        rows = rows[: count * lat_dev].reshape(count, lat_dev, slots)
        out_buf[first : first + count] = rows.astype(jnp.bfloat16)
        some = pl.ds(first, count)
        stores.append(pltpu.make_async_copy(out_buf.at[some], out_ref.at[part, some], out_sems.at[i]))
        stores[-1].start()
    for store in stores:
        store.wait()


def unpack(part, parts, levels, lat_dev, received, earlier):
    slots, width = received.shape
    cut = pieces(levels, lat_dev, width)
    anywhere = pl.BlockSpec(memory_space=pl.ANY)
    operands = [received] if earlier is None else [received, earlier]
    return pl.pallas_call(
        functools.partial(unpack_body, part=part),
        in_specs=[anywhere] * len(operands),
        out_specs=anywhere,
        out_shape=jax.ShapeDtypeStruct((parts, levels, lat_dev, slots), jnp.bfloat16),
        input_output_aliases={} if earlier is None else {1: 0},
        scratch_shapes=[
            pltpu.VMEM((slots, width), jnp.bfloat16),
            pltpu.VMEM((levels, lat_dev, slots), jnp.bfloat16),
            pltpu.SemaphoreType.DMA((len(cut),)),
            pltpu.SemaphoreType.DMA((len(cut),)),
        ],
        compiler_params=pltpu.CompilerParams(vmem_limit_bytes=VMEM_BYTES),
        cost_estimate=pl.CostEstimate(
            flops=levels * lat_dev * slots,
            bytes_accessed=4 * levels * lat_dev * slots,
            transcendentals=0,
        ),
    )(*operands)


def lane_runs(lanes, source):
    runs = []
    for lane in range(LANES):
        where = source(lanes + lane)
        if where is None:
            continue
        tile = (where[0], where[1] // LANES)
        shift = (lane - where[1]) % LANES
        if runs and runs[-1][1:] == (tile, shift):
            runs[-1] = (lane + 1, tile, shift)
        else:
            runs.append((lane + 1, tile, shift))
    return runs


def merge_runs(runs, load, cache, lane_index):
    out = None
    for end, tile, shift in reversed(runs):
        if (tile, shift) not in cache:
            value = load(*tile)
            cache[tile, shift] = pltpu.roll(value, shift, 1) if shift else value
        value = cache[tile, shift]
        out = value if out is None else jnp.where(lane_index < end, value, out)
    return out


def group_size(lat_dev):
    return LANES // math.gcd(lat_dev, LANES)


def spread(recv_ref, rows_ref, first, group, lat_dev, slot_dev):
    lat_total = rows_ref.shape[0] * LANES
    base = pl.multiple_of(first * lat_dev, LANES)
    lane_index = lax.broadcasted_iota(jnp.int32, (slot_dev, LANES), 1)
    pairs = {}

    def load(device, tile):
        pair = device // 2
        if (pair, tile) not in pairs:
            pairs[pair, tile] = recv_ref[
                2 * pair * slot_dev : 2 * (pair + 1) * slot_dev, pl.ds(base + tile * LANES, LANES)
            ].astype(jnp.float32)
        at = (device % 2) * slot_dev
        return pairs[pair, tile][at : at + slot_dev]

    cache = {}
    for lanes in range(0, lat_total, LANES):
        for i in range(group):
            runs = lane_runs(lanes, lambda j: (j // lat_dev, i * lat_dev + j % lat_dev))
            row = pl.multiple_of((first + i) * slot_dev, slot_dev)
            rows_ref[lanes // LANES, pl.ds(row, slot_dev), :] = merge_runs(
                runs, load, cache, lane_index
            )


def gather(rows_ref, send_ref, first, group, lat_dev, slot_dev):
    devices = rows_ref.shape[0] * LANES // lat_dev
    base = pl.multiple_of(first * lat_dev, LANES)
    lane_index = lax.broadcasted_iota(jnp.int32, (slot_dev, LANES), 1)
    cache = {}

    def load(i, tile):
        row = pl.multiple_of((first + i) * slot_dev, slot_dev)
        return rows_ref[tile, pl.ds(row, slot_dev), :]

    for pair in range(devices // 2):
        for lanes in range(0, group * lat_dev, LANES):
            tiles = []
            for device in (2 * pair, 2 * pair + 1):
                runs = lane_runs(
                    lanes,
                    lambda l: (l // lat_dev, device * lat_dev + l % lat_dev)
                    if l < group * lat_dev
                    else None,
                )
                tiles.append(merge_runs(runs, load, cache, lane_index))
            send_ref[
                2 * pair * slot_dev : 2 * (pair + 1) * slot_dev, pl.ds(base + lanes, LANES)
            ] = jnp.concatenate(tiles, axis=0).astype(jnp.bfloat16)


def join_tiles(ref, rows):
    return jnp.concatenate([ref[tile, rows, :] for tile in range(ref.shape[0])], axis=1)


def split_tiles(ref, rows, value):
    for tile in range(ref.shape[0]):
        ref[tile, rows, :] = value[:, tile * LANES : (tile + 1) * LANES]


def all_groups(levels, lat_dev, body):
    group = group_size(lat_dev)
    full = levels // group

    @pl.loop(0, full)
    def _(g):
        body(g * group, group)

    if levels % group:
        body(full * group, levels % group)


def step_body(waves_ref, recv_ref, legendre_ref, counts_ref, rates_ref, to_ref, from_ref, *refs):
    state_ref, send_ref, rows_ref, spec_ref = refs[-4:]
    slot = pl.program_id(0)
    wave = waves_ref[slot]
    row_total, lat_total = legendre_ref.shape[1:]
    _, levels, slot_dev, _ = state_ref.shape
    lat_dev = lat_total // (recv_ref.shape[0] // slot_dev)

    @pl.when(slot == 0)
    def _():
        all_groups(
            levels, lat_dev, lambda c, n: spread(recv_ref, rows_ref, c, n, lat_dev, slot_dev)
        )

    own = pl.ds(slot, levels, stride=slot_dev)
    matrix = legendre_ref[0]
    live = 2 * wave < counts_ref[...]
    direct = lax.dot_general(
        jnp.where(live, join_tiles(rows_ref, own), 0.0).astype(jnp.bfloat16),
        matrix,
        (((1,), (1,)), ((), ())),
        preferred_element_type=jnp.float32,
    ).astype(jnp.bfloat16)
    modal = jnp.dot(to_ref[...], direct, preferred_element_type=jnp.float32)
    degree = wave + 2 * lax.broadcasted_iota(jnp.int32, (1, row_total), 1)
    degree_f = degree.astype(jnp.float32)
    scaled_degree = degree_f * (degree_f + 1.0) / float(NMAX * (NMAX + 1))
    scaled = (modal / (1.0 + rates_ref[...] * scaled_degree)).astype(jnp.bfloat16)
    state = jnp.dot(from_ref[...], scaled, preferred_element_type=jnp.float32)
    state = jnp.where(degree <= NMAX, state, 0.0)
    split_tiles(spec_ref, own, state)
    rows = jnp.dot(state.astype(jnp.bfloat16), matrix, preferred_element_type=jnp.float32)
    split_tiles(rows_ref, own, jnp.where(live, rows, 0.0))

    @pl.when(slot == slot_dev - 1)
    def _():
        all_groups(
            levels, lat_dev, lambda c, n: gather(rows_ref, send_ref, c, n, lat_dev, slot_dev)
        )

        @pl.loop(0, levels)
        def _(c):
            at = pl.multiple_of(c * slot_dev, slot_dev)
            state_ref[0, c] = join_tiles(spec_ref, pl.ds(at, slot_dev)).astype(jnp.bfloat16)


def spectral_step(part, parts, received, legendre, own_waves, counts, rates, to_t, from_t, earlier):
    slots, width = received.shape
    slot_dev, row_total, lat_total = legendre.shape
    levels = to_t.shape[0]
    whole = lambda shape: pl.BlockSpec(shape, lambda s, waves: (0,) * len(shape))
    in_specs = [
        whole((slots, width)),
        pl.BlockSpec((1, row_total, lat_total), lambda s, waves: (s, 0, 0)),
        whole((1, lat_total)),
        whole((levels, 1)),
        whole((levels, levels)),
        whole((levels, levels)),
    ]
    operands = [own_waves, received, legendre, counts, rates, to_t, from_t]
    aliases = {}
    if earlier is not None:
        in_specs.append(pl.BlockSpec(memory_space=pl.ANY))
        aliases = {len(operands): 0}
        operands.append(earlier)
    return pl.pallas_call(
        step_body,
        grid_spec=pltpu.PrefetchScalarGridSpec(
            num_scalar_prefetch=1,
            grid=(slot_dev,),
            in_specs=in_specs,
            out_specs=[
                pl.BlockSpec((1, levels, slot_dev, row_total), lambda s, waves: (part, 0, 0, 0)),
                whole((slots, width)),
            ],
            scratch_shapes=[
                pltpu.VMEM((lat_total // LANES, levels * slot_dev, LANES), jnp.float32),
                pltpu.VMEM((row_total // LANES, levels * slot_dev, LANES), jnp.float32),
            ],
        ),
        out_shape=[
            jax.ShapeDtypeStruct((parts, levels, slot_dev, row_total), jnp.bfloat16),
            jax.ShapeDtypeStruct((slots, width), jnp.bfloat16),
        ],
        input_output_aliases=aliases,
        compiler_params=pltpu.CompilerParams(vmem_limit_bytes=VMEM_BYTES),
        cost_estimate=pl.CostEstimate(
            flops=4 * slot_dev * row_total * lat_total * levels,
            bytes_accessed=2 * slot_dev * lat_total * (row_total + 3 * levels),
            transcendentals=0,
        ),
    )(*operands)


def per_device(
    north_rows, south_rows, lon_counts, slot_wave, legendre, mode_rates, to_modes, from_modes
):
    lat_dev, slots, channels = north_rows.shape
    slot_dev, row_total, lat_total = legendre.shape
    levels = to_modes.shape[0]
    parts = channels // levels
    my_index = lax.axis_index("wave")
    own_waves = lax.dynamic_slice_in_dim(slot_wave, my_index * slot_dev, slot_dev)
    north = jnp.transpose(north_rows, (2, 0, 1)).reshape(parts, levels, lat_dev, slots)
    south = jnp.transpose(south_rows, (2, 0, 1)).reshape(parts, levels, lat_dev, slots)
    exchange = functools.partial(
        lax.all_to_all, axis_name="wave", split_axis=0, concat_axis=0, tiled=True
    )
    columns = [exchange(pack(part, north, south)) for part in range(parts)]
    spec_state = None
    returned = []
    for part in range(parts):
        spec_state, rows = spectral_step(
            part, parts, columns[part], legendre, own_waves, lon_counts[None, :],
            mode_rates[:, None], to_modes.T, from_modes.T, spec_state,
        )
        returned.append(exchange(rows))
    new_rows = None
    for part in range(parts):
        new_rows = unpack(part, parts, levels, lat_dev, returned[part], new_rows)
    new_rows = jnp.transpose(new_rows.reshape(channels, lat_dev, slots), (1, 2, 0))
    spec_state = jnp.transpose(spec_state.reshape(channels, slot_dev, row_total), (1, 2, 0))
    return (spec_state, new_rows)


def solution(mesh):
    in_specs = (
        P(("grp", "wave"), None, None),
        P(("grp", "wave"), None, None),
        P(),
        P(),
        P("wave", None, None),
        P(),
        P(),
        P(),
    )
    out_specs = (P(("grp", "wave"), None, None), P(("grp", "wave"), None, None))
    return jax.shard_map(
        per_device, mesh=mesh, in_specs=in_specs, out_specs=out_specs, check_vma=False
    )
```
